32 devices in a mesh: ctx: 8 (over z, core), ch: 4 (over y, x).
Axes of the slice: x: 2, y: 2, z: 4, core: 2. Of those that a mesh axis runs over, the one named last changes fastest.
Arguments:
- g_out: bfloat16 [8192, 8192], P('ctx', 'ch'), may hold values from -6 to 6
- w_out: bfloat16 [1024, 8192], P(None, 'ch'), may hold values from -0.0625 to 0.0625
- gate_x1: bfloat16 [8192, 1024], P('ctx', 'ch'), may hold values from -6 to 6
- gate_x2: bfloat16 [8192, 1024], P('ctx', 'ch'), may hold values from -6 to 6
- value_v: bfloat16 [8192, 1024], P('ctx', 'ch'), may hold values from -6 to 6
- residue: float32 [1024, 16], P('ch'), may hold values from -4 to 4
- decay: float32 [1024, 16], P('ch'), may hold values from 6.1035156e-05 to 0.05
Outputs:
- grad_x1: bfloat16 [8192, 1024], P('ctx', 'ch')
- grad_x2: bfloat16 [8192, 1024], P('ctx', 'ch')
- grad_v: bfloat16 [8192, 1024], P('ctx', 'ch')
- residue_grad: float32 [1024, 16], P(('ch', 'ctx'))
- decay_grad: float32 [1024, 16], P(('ch', 'ctx'))
The draws below stay inside these ranges and needn't reach their ends.
All inputs are finite; a program needn't handle non-finite values.
Results may differ from the reference program's by a relative error of at most 0.023.
Values may be sent and summed in bfloat16 or wider, within the bound.
No kernel may reach another device: no remote copies, remote signals or barrier semaphores. Data moves between devices by JAX's collectives and lax.ppermute only.
A program may use at most 128 MiB of HBM per device.

```python
import math
import jax
import jax.numpy as jnp
from jax import lax

DM = 8192
SLAB = 1024
MODES = 16
LEN = 8192
N_CH = 4


def block_scale(stream_key, dims, split, smallest, top_value):
    factor_of = 1.0
    for axis_at, parts in split:
        steps = jax.random.uniform(jax.random.fold_in(jax.random.fold_in(stream_key, 6), axis_at), (parts,), jnp.float32, smallest / len(split), top_value / len(split))
        factor_of = factor_of * jnp.repeat(jnp.exp(steps), dims[axis_at] // parts).reshape((-1,) + (1,) * (len(dims) - 1 - axis_at))
    return factor_of


def noise(key, dims, width, most, shards=(), held_as=jnp.bfloat16):
    loudness = block_scale(key, dims, shards, -0.22, 0.18) if shards else 1.0
    values = jax.random.normal(key, dims, jnp.float32) * width * loudness
    return jnp.minimum(jnp.maximum(values, -most), most).astype(held_as)


def setup_inputs(seed: int = 0) -> dict:
    arg_keys = jax.random.split(jax.random.key(seed), 8)
    return {
        "g_out": noise(arg_keys[0], (LEN, DM), 1.0, 6.0, ((0, 8), (1, 4))),
        "w_out": noise(arg_keys[1], (SLAB, DM), DM ** -0.5, 0.0625, ((1, 4),)),
        "gate_x1": noise(arg_keys[2], (LEN, SLAB), 1.0, 6.0, ((0, 8), (1, 4))),
        "gate_x2": noise(arg_keys[3], (LEN, SLAB), 1.0, 6.0, ((0, 8), (1, 4))),
        "value_v": noise(arg_keys[4], (LEN, SLAB), 1.0, 6.0, ((0, 8), (1, 4))),
        "residue": noise(arg_keys[5], (SLAB, MODES), 1.0, 4.0, ((0, 4),), jnp.float32),
        "decay": jnp.clip(jnp.exp(math.log(0.05) - 6.7083283 * jax.random.uniform(arg_keys[6], (SLAB, MODES), jnp.float32) ** block_scale(arg_keys[6], (SLAB, MODES), ((0, 4),), -0.2, 0.2)), 6.103515625e-05, 0.05),
    }


def filter_rows(blocked):
    residues, decays = blocked
    positions = jnp.arange(LEN).astype(jnp.float32)
    modes_table = jnp.exp(-decays[:, :, None] * positions[None, None, :])
    return jnp.sum(modes_table * residues[:, :, None], axis=1) * (LEN ** -0.5)


def filter_grads(blocked):
    slopes, residues, decays = blocked
    positions = jnp.arange(LEN).astype(jnp.float32)
    modes_table = jnp.exp(-decays[:, :, None] * positions[None, None, :])
    weighted = slopes[:, None, :] * modes_table
    residue_part = jnp.sum(weighted, axis=2) / LEN
    moment = jnp.sum(weighted * positions[None, None, :], axis=2) / LEN
    return residue_part, -residues * decays * moment


def reference(g_out, w_out, gate_x1, gate_x2, value_v, residue, decay):
    block_width = DM // N_CH
    grad_in = jnp.zeros((LEN, SLAB), jnp.float32)
    for column_block in range(N_CH):
        lower = column_block * block_width
        partial_value = jnp.dot(g_out[:, lower:lower + block_width], w_out[:, lower:lower + block_width].T, preferred_element_type=jnp.float32)
        rounded = lax.optimization_barrier(partial_value.astype(jnp.bfloat16))
        grad_in = grad_in + rounded.astype(jnp.float32)
    mixed = (gate_x2.astype(jnp.float32) * value_v.astype(jnp.float32)).astype(jnp.bfloat16)
    upstream = (grad_in * gate_x1.astype(jnp.float32)).astype(jnp.bfloat16)
    groups = 8
    impulse = lax.map(filter_rows, (residue.reshape(groups, SLAB // groups, MODES), decay.reshape(groups, SLAB // groups, MODES))).reshape(SLAB, LEN)
    padded_length = 2 * LEN
    spec_mixed = jnp.fft.rfft(mixed.astype(jnp.float32).T, n=padded_length, axis=1)
    spec_upstream = jnp.fft.rfft(upstream.astype(jnp.float32).T, n=padded_length, axis=1)
    spec_impulse = jnp.fft.rfft(impulse, n=padded_length, axis=1)
    response = jnp.fft.irfft(spec_impulse * spec_mixed, n=padded_length, axis=1)[:, :LEN]
    adjoint = jnp.fft.irfft(jnp.conj(spec_impulse) * spec_upstream, n=padded_length, axis=1)[:, :LEN]
    slopes = jnp.fft.irfft(jnp.conj(spec_mixed) * spec_upstream, n=padded_length, axis=1)[:, :LEN]
    grad_x1 = (grad_in * response.T).astype(jnp.bfloat16)
    grad_x2 = (adjoint.T * value_v.astype(jnp.float32)).astype(jnp.bfloat16)
    grad_v = (adjoint.T * gate_x2.astype(jnp.float32)).astype(jnp.bfloat16)
    residue_grad, decay_grad = lax.map(filter_grads, (slopes.reshape(groups, SLAB // groups, LEN), residue.reshape(groups, SLAB // groups, MODES), decay.reshape(groups, SLAB // groups, MODES)))
    return grad_x1, grad_x2, grad_v, residue_grad.reshape(SLAB, MODES), decay_grad.reshape(SLAB, MODES)
```

```python
import functools

import jax
import jax.numpy as jnp
from jax import lax
from jax.experimental import pallas as pl
from jax.experimental.pallas import tpu as pltpu
from jax.sharding import PartitionSpec as P

LANES = 128
BLOCKS = 8
F32 = jnp.float32
BF16 = jnp.bfloat16


def halving_layout(order):
    if not order:
        return [0]
    rest = halving_layout(order[1:])
    return [offset ^ order[0] for offset in rest] + rest


def xor_pairs(count, step):
    return [(index, index ^ step) for index in range(count)]


def params(vmem=48 * 2**20):
    return pltpu.CompilerParams(vmem_limit_bytes=vmem)


def project_body(which_ref, g_ref, w_ref, out_ref):
    out_ref[...] = lax.dot_general(
        g_ref[...], w_ref[...], (((1,), (1,)), ((), ())), preferred_element_type=F32
    ).astype(out_ref.dtype)


def project(which, g_out, w_out, start, rows, width, dtype):
    depth = g_out.shape[1]
    count = which.shape[0]
    tile = min(rows, 256)
    tiles = rows // tile
    first = start // tile
    spec = pltpu.PrefetchScalarGridSpec(
        num_scalar_prefetch=1,
        grid=(count, tiles),
        in_specs=[
            pl.BlockSpec((tile, depth), lambda j, i, s: (first + i, 0)),
            pl.BlockSpec((width, depth), lambda j, i, s: (s[j], 0)),
        ],
        out_specs=pl.BlockSpec((tile, width), lambda j, i, s: (i, j)),
    )
    return pl.pallas_call(
        project_body,
        grid_spec=spec,
        out_shape=jax.ShapeDtypeStruct((rows, count * width), dtype),
        compiler_params=params(),
        cost_estimate=pl.CostEstimate(
            flops=2 * rows * depth * count * width,
            bytes_accessed=2 * depth * (rows + count * width),
            transcendentals=0,
        ),
        name="project",
    )(which, g_out, w_out)


def spread(ref, row, lanes):
    return jnp.broadcast_to(ref[pl.ds(row, 1), lanes], (BLOCKS, LANES))


def forward_body(segments, modes, x2_ref, v_ref, a_ref, r_ref, decay_ref,
                 xperm_ref, yloc_ref, hb_ref, eb_ref, total_ref, nat):
    channels = x2_ref.shape[1]
    unroll = 4
    half = modes // 2
    for lane in range(channels // LANES):
        lanes = pl.ds(lane * LANES, LANES)
        mixed = (x2_ref[:, lanes].astype(F32) * v_ref[:, lanes].astype(F32)).astype(BF16)
        nat[lane] = mixed.astype(F32)
        for seg, (start, rows) in enumerate(segments):
            steps = rows // BLOCKS
            for part in range(2):
                decays = [spread(a_ref, part * half + m, lanes) for m in range(half)]
                weights = [spread(r_ref, part * half + m, lanes) for m in range(half)]

                def body(outer, carry):
                    h, e = list(carry[0]), list(carry[1])
                    for q in range(unroll):
                        i = outer * unroll + q
                        here = pl.ds(pl.multiple_of(start + i * BLOCKS, BLOCKS), BLOCKS)
                        if part == 0:
                            x = nat[lane, pl.ds(start + i, BLOCKS, stride=steps), :]
                            xperm_ref[lane, here, :] = x
                        else:
                            x = xperm_ref[lane, here, :]
                        y = None
                        for m in range(half):
                            e[m] = decays[m] * e[m] + h[m]
                            h[m] = decays[m] * h[m] + x
                            term = weights[m] * h[m]
                            y = term if y is None else y + term
                        if part == 1:
                            y = y + yloc_ref[lane, here, :]
                        yloc_ref[lane, here, :] = y
                    return tuple(h), tuple(e)

                zero = (jnp.zeros((BLOCKS, LANES), F32),) * half
                h, e = lax.fori_loop(0, steps // unroll, body, (zero, zero))
                for m in range(half):
                    row = pl.ds(part * half + m, BLOCKS, stride=modes)
                    hb_ref[lane, seg, row, :] = h[m]
                    eb_ref[lane, seg, row, :] = e[m]
        a = a_ref[:, lanes]
        state = jnp.zeros((modes, LANES), F32)
        moment = jnp.zeros((modes, LANES), F32)
        for seg, (start, rows) in enumerate(segments):
            steps = rows // BLOCKS
            power = jnp.exp(-decay_ref[:, lanes] * steps)
            for b in range(BLOCKS):
                rowsb = pl.ds(b * modes, modes)
                moment = power * (moment + steps * state) + a * eb_ref[lane, seg, rowsb, :]
                state = power * state + hb_ref[lane, seg, rowsb, :]
        total_ref[pl.ds(0, modes), lanes] = state
        total_ref[pl.ds(modes, modes), lanes] = moment


def respond_body(segments, modes, hb_ref, eb_ref, yloc_ref, a_ref, r_ref, decay_ref, carry_ref,
                 resp_ref, hin_ref, kin_ref):
    channels = a_ref.shape[1]
    unroll = 4
    for lane in range(channels // LANES):
        lanes = pl.ds(lane * LANES, LANES)
        a = a_ref[:, lanes]
        state = carry_ref[pl.ds(0, modes), lanes]
        moment = carry_ref[pl.ds(modes, modes), lanes]
        for seg, (start, rows) in enumerate(segments):
            steps = rows // BLOCKS
            power = jnp.exp(-decay_ref[:, lanes] * steps)
            for b in range(BLOCKS):
                rowsb = pl.ds(b * modes, modes)
                hin_ref[lane, seg, rowsb, :] = state
                kin_ref[lane, seg, rowsb, :] = moment
                moment = power * (moment + steps * state) + a * eb_ref[lane, seg, rowsb, :]
                state = power * state + hb_ref[lane, seg, rowsb, :]
        decays = [spread(a_ref, m, lanes) for m in range(modes)]
        for seg, (start, rows) in enumerate(segments):
            steps = rows // BLOCKS
            edge = tuple(
                spread(r_ref, m, lanes) * decays[m]
                * hin_ref[lane, seg, pl.ds(m, BLOCKS, stride=modes), :]
                for m in range(modes)
            )

            def body(outer, edge):
                edge = list(edge)
                for q in range(unroll):
                    i = outer * unroll + q
                    here = pl.ds(pl.multiple_of(start + i * BLOCKS, BLOCKS), BLOCKS)
                    y = yloc_ref[lane, here, :]
                    for m in range(modes):
                        y = y + edge[m]
                        edge[m] = edge[m] * decays[m]
                    resp_ref[lane, pl.ds(start + i, BLOCKS, stride=steps), :] = y
                return tuple(edge)

            lax.fori_loop(0, steps // unroll, body, edge)


def adjoint_body(segment, modes, own_ref, recv_ref, x1_ref, resp_ref, xperm_ref, hin_ref, kin_ref,
                 a_ref, r_ref, grad_ref, aloc_ref, gb_ref, sums_ref, nat, uperm, db, rb, mb):
    seg, start, rows = segment
    steps = rows // BLOCKS
    channels = own_ref.shape[1]
    unroll = 4
    half = modes // 2
    for lane in range(channels // LANES):
        lanes = pl.ds(lane * LANES, LANES)
        grad_in = own_ref[:, lanes] + recv_ref[:, lanes].astype(F32)
        window = pl.ds(start, rows)
        grad_ref[:, lanes] = (grad_in * resp_ref[lane, window, :]).astype(BF16)
        nat[lane] = (grad_in * x1_ref[window, lanes].astype(F32)).astype(BF16).astype(F32)
        for part in range(2):
            decays = [spread(a_ref, part * half + m, lanes) for m in range(half)]
            weights = [spread(r_ref, part * half + m, lanes) for m in range(half)]

            def body(outer, carry):
                g, d, racc, macc = (list(item) for item in carry)
                for q in range(unroll):
                    i = steps - 1 - (outer * unroll + q)
                    here = pl.ds(pl.multiple_of(i * BLOCKS, BLOCKS), BLOCKS)
                    if part == 0:
                        u = nat[lane, pl.ds(i, BLOCKS, stride=steps), :]
                        uperm[lane, here, :] = u
                    else:
                        u = uperm[lane, here, :]
                    x = xperm_ref[lane, pl.ds(pl.multiple_of(start + i * BLOCKS, BLOCKS), BLOCKS), :]
                    y = None
                    for m in range(half):
                        d[m] = decays[m] * d[m] + g[m]
                        g[m] = decays[m] * g[m] + u
                        racc[m] = racc[m] + x * g[m]
                        macc[m] = macc[m] + x * d[m]
                        term = weights[m] * g[m]
                        y = term if y is None else y + term
                    if part == 1:
                        y = y + aloc_ref[lane, here, :]
                    aloc_ref[lane, here, :] = y
                return tuple(g), tuple(d), tuple(racc), tuple(macc)

            zero = (jnp.zeros((BLOCKS, LANES), F32),) * half
            g, d, racc, macc = lax.fori_loop(0, steps // unroll, body, (zero,) * 4)
            for m in range(half):
                row = pl.ds(part * half + m, BLOCKS, stride=modes)
                gb_ref[lane, row, :] = g[m]
                db[row, :] = d[m]
                rb[row, :] = racc[m]
                mb[row, :] = macc[m]
        a = a_ref[:, lanes]
        total = jnp.zeros((modes, LANES), F32)
        moment = jnp.zeros((modes, LANES), F32)
        for b in range(BLOCKS):
            rowsb = pl.ds(b * modes, modes)
            hin = hin_ref[lane, seg, rowsb, :]
            ag = a * gb_ref[lane, rowsb, :]
            total = total + rb[rowsb, :] + ag * hin
            moment = moment + a * mb[rowsb, :] + (ag + a * a * db[rowsb, :]) * hin
            moment = moment + ag * kin_ref[lane, seg, rowsb, :]
        sums_ref[pl.ds(0, modes), lanes] = total
        sums_ref[pl.ds(modes, modes), lanes] = moment


def gather_body(segments, modes, *refs):
    count = len(segments)
    gb_refs, sums_refs = refs[:count], refs[count:2 * count]
    decay_ref, out_ref = refs[2 * count:]
    channels = decay_ref.shape[1]
    for lane in range(channels // LANES):
        lanes = pl.ds(lane * LANES, LANES)
        state = jnp.zeros((modes, LANES), F32)
        for seg in reversed(range(count)):
            power = jnp.exp(-decay_ref[:, lanes] * (segments[seg][1] // BLOCKS))
            for b in reversed(range(BLOCKS)):
                state = power * state + gb_refs[seg][lane, pl.ds(b * modes, modes), :]
        out_ref[pl.ds(0, modes), lanes] = state
    out_ref[pl.ds(modes, 2 * modes), :] = sum(ref[...] for ref in sums_refs)


def finish_body(segments, modes, length, index_ref, *refs):
    count = len(segments)
    aloc_refs, gb_refs = refs[:count], refs[count:2 * count]
    (a_ref, r_ref, decay_ref, carry_ref, sums_ref, x2_ref, v_ref,
     gx2_ref, gv_ref, rgrad_ref, dgrad_ref, gin, nat) = refs[2 * count:]
    channels = a_ref.shape[1]
    unroll = 4
    for lane in range(channels // LANES):
        lanes = pl.ds(lane * LANES, LANES)
        decays = [spread(a_ref, m, lanes) for m in range(modes)]
        state = carry_ref[:, lanes]
        for seg in reversed(range(count)):
            start, rows = segments[seg]
            steps = rows // BLOCKS
            power = jnp.exp(-decay_ref[:, lanes] * steps)
            for b in reversed(range(BLOCKS)):
                rowsb = pl.ds(b * modes, modes)
                gin[rowsb, :] = state
                state = power * state + gb_refs[seg][lane, rowsb, :]
            edge = tuple(
                spread(r_ref, m, lanes) * decays[m] * gin[pl.ds(m, BLOCKS, stride=modes), :]
                for m in range(modes)
            )

            def body(outer, edge):
                edge = list(edge)
                for q in range(unroll):
                    i = steps - 1 - (outer * unroll + q)
                    here = pl.ds(pl.multiple_of(i * BLOCKS, BLOCKS), BLOCKS)
                    y = aloc_refs[seg][lane, here, :]
                    for m in range(modes):
                        y = y + edge[m]
                        edge[m] = edge[m] * decays[m]
                    nat[lane, pl.ds(start + i, BLOCKS, stride=steps), :] = y
                return tuple(edge)

            lax.fori_loop(0, steps // unroll, body, edge)
        gx2_ref[:, lanes] = (nat[lane] * v_ref[:, lanes].astype(F32)).astype(BF16)
        gv_ref[:, lanes] = (nat[lane] * x2_ref[:, lanes].astype(F32)).astype(BF16)
    owned = rgrad_ref.shape[0]
    row = lax.broadcasted_iota(jnp.int32, (owned, channels), 0) + index_ref[0] * owned
    column = lax.broadcasted_iota(jnp.int32, (owned, channels), 1)
    pick = (row == column).astype(F32)

    def choose(values):
        return lax.dot_general(
            pick, values, (((1,), (1,)), ((), ())),
            precision=lax.Precision.HIGHEST, preferred_element_type=F32,
        )

    rgrad_ref[...] = choose(sums_ref[pl.ds(0, modes), :]) / length
    scale = r_ref[...] * decay_ref[...] * (float(length) ** 0.5)
    dgrad_ref[...] = -choose(scale * sums_ref[pl.ds(modes, modes), :]) / length


def on_device(g_out, w_out, gate_x1, gate_x2, value_v, residue, decay):
    tokens, channels = gate_x1.shape
    context_size = lax.axis_size("ctx")
    ch_size = lax.axis_size("ch")
    length = tokens * context_size
    modes = residue.shape[1]
    lane_tiles = channels // LANES
    context_index = lax.axis_index("ctx")
    ch_index = lax.axis_index("ch")
    owned = channels // context_size

    bits = [1 << bit for bit in range(ch_size.bit_length() - 1)]
    half_rows = tokens // 2
    chunks = [(0, half_rows, bits), (half_rows, half_rows, bits[::-1])]
    segments = [(start, rows) for start, rows, _ in chunks]
    count = len(chunks)

    sending, keeping = [], []
    for start, rows, order in chunks:
        offsets = halving_layout(order)
        cut = len(offsets) // 2
        which = jnp.array(offsets, jnp.int32) ^ ch_index
        sent = project(which[:cut], g_out, w_out, start, rows, channels, BF16)
        sending.append(lax.ppermute(sent, "ch", xor_pairs(ch_size, order[0])))
        keeping.append((which[cut:], start, rows, order))
    keeping = [
        (project(which, g_out, w_out, start, rows, channels, F32), order)
        for which, start, rows, order in keeping
    ]

    decay_t = decay.T
    residue_t = residue.T
    a = jnp.exp(-decay_t)
    r = residue_t * length ** (-0.5)

    state_shape = jax.ShapeDtypeStruct((lane_tiles, count, BLOCKS * modes, LANES), F32)
    perm_shape = jax.ShapeDtypeStruct((lane_tiles, tokens, LANES), F32)
    work = tokens * channels * modes
    xperm, yloc, hb, eb, total = pl.pallas_call(
        functools.partial(forward_body, segments, modes),
        out_shape=[perm_shape, perm_shape, state_shape, state_shape,
                   jax.ShapeDtypeStruct((2 * modes, channels), F32)],
        scratch_shapes=[pltpu.VMEM((lane_tiles, tokens, LANES), F32)],
        compiler_params=params(),
        cost_estimate=pl.CostEstimate(flops=work * 6, bytes_accessed=tokens * channels * 12, transcendentals=0),
        name="forward",
    )(gate_x2, value_v, a, r, decay_t)

    pair = context_index // 2
    core = context_index % 2
    pairs = context_size // 2
    whole_power = jnp.exp(-decay_t * tokens)

    partner = lax.ppermute(total, "ctx", xor_pairs(context_size, 1))
    first = jnp.where(core == 0, total, partner)
    second = jnp.where(core == 0, partner, total)
    pair_h = second[:modes] + whole_power * first[:modes]
    pair_k = second[modes:] + whole_power * (first[modes:] + tokens * first[:modes])
    both = jnp.concatenate([pair_h, pair_k], 0)
    carry_h = jnp.where(core == 1, first[:modes], 0.0)
    carry_k = jnp.where(core == 1, first[modes:], 0.0)
    for step in range(1, pairs):
        other = pair ^ step
        got = lax.ppermute(both, "ctx", xor_pairs(context_size, 2 * step))
        gap = ((2 * (pair - other - 1) + core) * tokens).astype(F32)
        weight = jnp.where(other < pair, jnp.exp(-decay_t * jnp.maximum(gap, 0.0)), 0.0)
        carry_h = carry_h + weight * got[:modes]
        carry_k = carry_k + weight * (got[modes:] + gap * got[:modes])
    carry = jnp.concatenate([carry_h, carry_k], 0)

    resp, hin, kin = pl.pallas_call(
        functools.partial(respond_body, segments, modes),
        out_shape=[perm_shape, state_shape, state_shape],
        compiler_params=params(),
        cost_estimate=pl.CostEstimate(flops=work * 2, bytes_accessed=tokens * channels * 8, transcendentals=0),
        name="respond",
    )(hb, eb, yloc, a, r, decay_t, carry)

    grads, alocs, gbs, sums = [], [], [], []
    arrived = []
    stages = [(sent, kept, order) for sent, (kept, order) in zip(sending, keeping)]
    for level in range(1, len(bits)):
        following = []
        for sent, kept, order in stages:
            cut = kept.shape[1] // 2
            away = (kept[:, :cut] + sent[:, :cut].astype(F32)).astype(BF16)
            stay = kept[:, cut:] + sent[:, cut:].astype(F32)
            moved = lax.ppermute(away, "ch", xor_pairs(ch_size, order[level]))
            following.append((moved, stay, order))
        stages = following
    for seg, (moved, stay, _) in enumerate(stages):
        start, rows = segments[seg]
        block_shape = jax.ShapeDtypeStruct((lane_tiles, BLOCKS * modes, LANES), F32)
        grad_x1, aloc, gb, partial_sums = pl.pallas_call(
            functools.partial(adjoint_body, (seg, start, rows), modes),
            out_shape=[jax.ShapeDtypeStruct((rows, channels), BF16),
                       jax.ShapeDtypeStruct((lane_tiles, rows, LANES), F32),
                       block_shape,
                       jax.ShapeDtypeStruct((2 * modes, channels), F32)],
            scratch_shapes=[pltpu.VMEM((lane_tiles, rows, LANES), F32)] * 2
            + [pltpu.VMEM((BLOCKS * modes, LANES), F32)] * 3,
            compiler_params=params(),
            cost_estimate=pl.CostEstimate(flops=rows * channels * modes * 10, bytes_accessed=rows * channels * 16, transcendentals=0),
            name="adjoint",
        )(stay, moved, gate_x1, resp, xperm, hin, kin, a, r)
        grads.append(grad_x1)
        alocs.append(aloc)
        gbs.append(gb)
        sums.append(partial_sums)

    message = pl.pallas_call(
        functools.partial(gather_body, segments, modes),
        out_shape=jax.ShapeDtypeStruct((3 * modes, channels), F32),
        compiler_params=params(),
        name="totals",
    )(*gbs, *sums, decay_t)
    partner = lax.ppermute(message, "ctx", xor_pairs(context_size, 1))
    first = jnp.where(core == 0, message[:modes], partner[:modes])
    second = jnp.where(core == 0, partner[:modes], message[:modes])
    both = jnp.concatenate([first + whole_power * second, message[modes:] + partner[modes:]], 0)
    carry_g = jnp.where(core == 0, second, 0.0)
    param_sums = both[modes:]
    for step in range(1, pairs):
        other = pair ^ step
        got = lax.ppermute(both, "ctx", xor_pairs(context_size, 2 * step))
        gap = ((2 * (other - pair - 1) + 1 - core) * tokens).astype(F32)
        weight = jnp.where(other > pair, jnp.exp(-decay_t * jnp.maximum(gap, 0.0)), 0.0)
        carry_g = carry_g + weight * got[:modes]
        param_sums = param_sums + got[modes:]

    vmem = pl.BlockSpec(memory_space=pltpu.VMEM)
    grad_x2, grad_v, residue_grad, decay_grad = pl.pallas_call(
        functools.partial(finish_body, segments, modes, length),
        in_specs=[pl.BlockSpec(memory_space=pltpu.SMEM)] + [vmem] * (2 * count + 7),
        out_specs=[vmem] * 4,
        out_shape=[jax.ShapeDtypeStruct((tokens, channels), BF16)] * 2
        + [jax.ShapeDtypeStruct((owned, modes), F32)] * 2,
        scratch_shapes=[pltpu.VMEM((BLOCKS * modes, LANES), F32),
                        pltpu.VMEM((lane_tiles, tokens, LANES), F32)],
        compiler_params=params(),
        cost_estimate=pl.CostEstimate(flops=work * 2, bytes_accessed=tokens * channels * 12, transcendentals=0),
        name="finish",
    )(context_index.reshape(1), *alocs, *gbs, a, r, decay_t, carry_g, param_sums, gate_x2, value_v)
    return jnp.concatenate(grads, 0), grad_x2, grad_v, residue_grad, decay_grad


def solution(mesh):
    return jax.shard_map(
        on_device,
        mesh=mesh,
        in_specs=(
            P("ctx", "ch"),
            P(None, "ch"),
            P("ctx", "ch"),
            P("ctx", "ch"),
            P("ctx", "ch"),
            P("ch", None),
            P("ch", None),
        ),
        out_specs=(
            P("ctx", "ch"),
            P("ctx", "ch"),
            P("ctx", "ch"),
            P(("ch", "ctx"), None),
            P(("ch", "ctx"), None),
        ),
        check_vma=False,
    )
```

```python
import functools

import jax
import jax.numpy as jnp
from jax import lax
from jax.experimental import pallas as pl
from jax.experimental.pallas import tpu as pltpu
from jax.sharding import PartitionSpec as P

LANES = 128
PIECES = 2
BLOCKS = 8
F32 = jnp.float32
BF16 = jnp.bfloat16


def halving_layout(order):
    if not order:
        return [0]
    rest = halving_layout(order[1:])
    return [offset ^ order[0] for offset in rest] + rest


def xor_pairs(count, step):
    return [(index, index ^ step) for index in range(count)]


HBM = pltpu.MemorySpace.HBM
VMEM = pltpu.MemorySpace.VMEM
CONTRACT_LAST = (((1,), (1,)), ((), ()))


def params(mebibytes=24):
    return pltpu.CompilerParams(vmem_limit_bytes=mebibytes * 2**20)


def in_vmem(count):
    return [pl.BlockSpec(memory_space=VMEM)] * count


def block_rows(offset, width):
    block = lax.axis_index("ch") ^ offset
    return pl.ds(pl.multiple_of(block * width, width), width)


def project_body(work, width, pieces, g_ref, w_ref, *refs):
    count = len(work)
    out_refs = refs[:count]
    g_here, w_here, total, g_sems, w_sems = refs[count:]
    depth = g_ref.shape[1] // pieces
    pending = {}

    def g_copy(rows, piece):
        columns = pl.ds(piece * depth, depth)
        return pltpu.make_async_copy(
            g_ref.at[rows, columns], g_here.at[rows, columns], g_sems.at[rows.start // rows.size, piece])

    def w_copy(offset, piece):
        columns = pl.ds(piece * depth, depth)
        here = block_rows(offset, width)
        return pltpu.make_async_copy(
            w_ref.at[here, columns], w_here.at[here, columns], w_sems.at[offset, piece])

    for start, rows, offsets in work:
        for piece in range(pieces):
            for key, copy in [((start, piece), lambda: g_copy(pl.ds(start, rows), piece))] + [
                    ((-1 - offset, piece), functools.partial(w_copy, offset, piece)) for offset in offsets]:
                if key not in pending:
                    pending[key] = copy()
                    pending[key].start()
    for (start, rows, offsets), out_ref in zip(work, out_refs):
        for piece in range(pieces):
            columns = pl.ds(piece * depth, depth)
            for key in [(start, piece)] + [(-1 - offset, piece) for offset in offsets]:
                copy = pending.pop(key, None)
                if copy is not None:
                    copy.wait()
            for j, offset in enumerate(offsets):
                here = pl.ds(j * width, width)
                product = lax.dot_general(
                    g_here[pl.ds(start, rows), columns], w_here[block_rows(offset, width), columns],
                    CONTRACT_LAST, preferred_element_type=F32)
                if piece > 0:
                    product = product + total[:, here]
                if piece < pieces - 1:
                    total[:, here] = product
                else:
                    out_ref[:, here] = product.astype(out_ref.dtype)


def project(g_out, w_out, work, width):
    blocks = w_out.shape[0] // width
    pieces = PIECES
    shapes = [jax.ShapeDtypeStruct((rows, len(offsets) * width), BF16) for _, rows, offsets in work]
    groups = g_out.shape[0] // work[0][1]
    return pl.pallas_call(
        functools.partial(project_body, work, width, pieces),
        in_specs=[pl.BlockSpec(memory_space=HBM)] * 2,
        out_specs=in_vmem(len(work)),
        out_shape=shapes,
        scratch_shapes=[
            pltpu.VMEM(g_out.shape, BF16),
            pltpu.VMEM(w_out.shape, BF16),
            pltpu.VMEM(shapes[0].shape, F32),
            pltpu.SemaphoreType.DMA((groups, pieces)),
            pltpu.SemaphoreType.DMA((blocks, pieces)),
        ],
        compiler_params=params(60),
        name="project",
    )(g_out, w_out)


def spread(ref, row, lanes):
    return jnp.broadcast_to(ref[pl.ds(row, 1), lanes], (BLOCKS, LANES))


def forward_body(segments, modes, x2_ref, v_ref, a_ref, r_ref, decay_ref,
                 xperm_ref, yloc_ref, hb_ref, eb_ref, total_ref, nat):
    channels = x2_ref.shape[1]
    unroll = 4
    half = modes // 2
    for lane in range(channels // LANES):
        lanes = pl.ds(lane * LANES, LANES)
        mixed = (x2_ref[:, lanes].astype(F32) * v_ref[:, lanes].astype(F32)).astype(BF16)
        nat[lane] = mixed.astype(F32)
        for seg, (start, rows) in enumerate(segments):
            steps = rows // BLOCKS
            for part in range(2):
                decays = [spread(a_ref, part * half + m, lanes) for m in range(half)]
                weights = [spread(r_ref, part * half + m, lanes) for m in range(half)]

                def body(outer, carry):
                    h, e = list(carry[0]), list(carry[1])
                    for q in range(unroll):
                        i = outer * unroll + q
                        here = pl.ds(pl.multiple_of(start + i * BLOCKS, BLOCKS), BLOCKS)
                        if part == 0:
                            x = nat[lane, pl.ds(start + i, BLOCKS, stride=steps), :]
                            xperm_ref[lane, here, :] = x
                        else:
                            x = xperm_ref[lane, here, :]
                        y = None
                        for m in range(half):
                            e[m] = decays[m] * e[m] + h[m]
                            h[m] = decays[m] * h[m] + x
                            term = weights[m] * h[m]
                            y = term if y is None else y + term
                        if part == 1:
                            y = y + yloc_ref[lane, here, :]
                        yloc_ref[lane, here, :] = y
                    return tuple(h), tuple(e)

                zero = (jnp.zeros((BLOCKS, LANES), F32),) * half
                h, e = lax.fori_loop(0, steps // unroll, body, (zero, zero))
                for m in range(half):
                    row = pl.ds(part * half + m, BLOCKS, stride=modes)
                    hb_ref[lane, seg, row, :] = h[m]
                    eb_ref[lane, seg, row, :] = e[m]
        a = a_ref[:, lanes]
        state = jnp.zeros((modes, LANES), F32)
        moment = jnp.zeros((modes, LANES), F32)
        for seg, (start, rows) in enumerate(segments):
            steps = rows // BLOCKS
            power = jnp.exp(-decay_ref[:, lanes] * steps)
            for b in range(BLOCKS):
                rowsb = pl.ds(b * modes, modes)
                moment = power * (moment + steps * state) + a * eb_ref[lane, seg, rowsb, :]
                state = power * state + hb_ref[lane, seg, rowsb, :]
        total_ref[pl.ds(0, modes), lanes] = state
        total_ref[pl.ds(modes, modes), lanes] = moment


def place():
    index = lax.axis_index("ctx")
    return index // 2, index % 2


def forward_pair_body(modes, tokens, total_ref, partner_ref, decay_ref, both_ref):
    _, core = place()
    state, moment = pl.ds(0, modes), pl.ds(modes, modes)
    power = jnp.exp(-decay_ref[...] * tokens)
    later = core == 1
    first_h = jnp.where(later, partner_ref[state, :], total_ref[state, :])
    first_k = jnp.where(later, partner_ref[moment, :], total_ref[moment, :])
    second_h = jnp.where(later, total_ref[state, :], partner_ref[state, :])
    second_k = jnp.where(later, total_ref[moment, :], partner_ref[moment, :])
    both_ref[state, :] = second_h + power * first_h
    both_ref[moment, :] = second_k + power * (first_k + tokens * first_h)


def respond_body(segments, modes, tokens, hb_ref, eb_ref, yloc_ref, a_ref, r_ref, decay_ref, partner_ref, *refs):
    got_refs, (resp_ref, hin_ref, kin_ref) = refs[:-3], refs[-3:]
    pair, core = place()
    channels = a_ref.shape[1]
    unroll = 4
    for lane in range(channels // LANES):
        lanes = pl.ds(lane * LANES, LANES)
        a = a_ref[:, lanes]
        state = jnp.where(core == 1, partner_ref[pl.ds(0, modes), lanes], 0.0)
        moment = jnp.where(core == 1, partner_ref[pl.ds(modes, modes), lanes], 0.0)
        for step, got_ref in enumerate(got_refs, 1):
            other = pair ^ step
            gap = jnp.maximum((2 * (pair - other - 1) + core) * tokens, 0).astype(F32)
            weight = jnp.where(other < pair, jnp.exp(-decay_ref[:, lanes] * gap), 0.0)
            got = got_ref[pl.ds(0, modes), lanes]
            state = state + weight * got
            moment = moment + weight * (got_ref[pl.ds(modes, modes), lanes] + gap * got)
        for seg, (start, rows) in enumerate(segments):
            steps = rows // BLOCKS
            power = jnp.exp(-decay_ref[:, lanes] * steps)
            for b in range(BLOCKS):
                rowsb = pl.ds(b * modes, modes)
                hin_ref[lane, seg, rowsb, :] = state
                kin_ref[lane, seg, rowsb, :] = moment
                moment = power * (moment + steps * state) + a * eb_ref[lane, seg, rowsb, :]
                state = power * state + hb_ref[lane, seg, rowsb, :]
        decays = [spread(a_ref, m, lanes) for m in range(modes)]
        for seg, (start, rows) in enumerate(segments):
            steps = rows // BLOCKS
            edge = tuple(
                spread(r_ref, m, lanes) * decays[m]
                * hin_ref[lane, seg, pl.ds(m, BLOCKS, stride=modes), :]
                for m in range(modes)
            )

            def body(outer, edge):
                edge = list(edge)
                for q in range(unroll):
                    i = outer * unroll + q
                    here = pl.ds(pl.multiple_of(start + i * BLOCKS, BLOCKS), BLOCKS)
                    y = yloc_ref[lane, here, :]
                    for m in range(modes):
                        y = y + edge[m]
                        edge[m] = edge[m] * decays[m]
                    resp_ref[lane, pl.ds(start + i, BLOCKS, stride=steps), :] = y
                return tuple(edge)

            lax.fori_loop(0, steps // unroll, body, edge)


def adjoint_body(segment, modes, received, has_previous, kept_ref, *refs):
    seg, start, rows = segment
    recv_refs = refs[:received]
    refs = refs[received + has_previous:]
    (x1_ref, resp_ref, xperm_ref, hin_ref, kin_ref, a_ref, r_ref,
     grad_ref, aloc_ref, gb_ref, sums_ref, nat, uperm, db, rb, mb, grad_here, sem) = refs
    steps = rows // BLOCKS
    channels = x1_ref.shape[1]
    unroll = 4
    half = modes // 2
    window = pl.ds(start, rows)
    for lane in range(channels // LANES):
        lanes = pl.ds(lane * LANES, LANES)

        def own(ref):
            return ref[:, pl.ds(ref.shape[1] - channels + lane * LANES, LANES)]

        grad_in = own(kept_ref).astype(F32)
        for recv_ref in recv_refs:
            grad_in = grad_in + own(recv_ref).astype(F32)
        grad_here[:, lanes] = (grad_in * resp_ref[lane, window, :]).astype(BF16)
        nat[lane] = (grad_in * x1_ref[window, lanes].astype(F32)).astype(BF16).astype(F32)
    copy = pltpu.make_async_copy(grad_here, grad_ref.at[window, :], sem)
    copy.start()
    for lane in range(channels // LANES):
        lanes = pl.ds(lane * LANES, LANES)
        for part in range(2):
            decays = [spread(a_ref, part * half + m, lanes) for m in range(half)]
            weights = [spread(r_ref, part * half + m, lanes) for m in range(half)]

            def body(outer, carry):
                g, d, racc, macc = (list(item) for item in carry)
                for q in range(unroll):
                    i = steps - 1 - (outer * unroll + q)
                    here = pl.ds(pl.multiple_of(i * BLOCKS, BLOCKS), BLOCKS)
                    if part == 0:
                        u = nat[lane, pl.ds(i, BLOCKS, stride=steps), :]
                        uperm[lane, here, :] = u
                    else:
                        u = uperm[lane, here, :]
                    x = xperm_ref[lane, pl.ds(pl.multiple_of(start + i * BLOCKS, BLOCKS), BLOCKS), :]
                    y = None
                    for m in range(half):
                        d[m] = decays[m] * d[m] + g[m]
                        g[m] = decays[m] * g[m] + u
                        racc[m] = racc[m] + x * g[m]
                        macc[m] = macc[m] + x * d[m]
                        term = weights[m] * g[m]
                        y = term if y is None else y + term
                    if part == 1:
                        y = y + aloc_ref[lane, here, :]
                    aloc_ref[lane, here, :] = y
                return tuple(g), tuple(d), tuple(racc), tuple(macc)

            zero = (jnp.zeros((BLOCKS, LANES), F32),) * half
            g, d, racc, macc = lax.fori_loop(0, steps // unroll, body, (zero,) * 4)
            for m in range(half):
                row = pl.ds(part * half + m, BLOCKS, stride=modes)
                gb_ref[lane, row, :] = g[m]
                db[row, :] = d[m]
                rb[row, :] = racc[m]
                mb[row, :] = macc[m]
        a = a_ref[:, lanes]
        total = jnp.zeros((modes, LANES), F32)
        moment = jnp.zeros((modes, LANES), F32)
        for b in range(BLOCKS):
            rowsb = pl.ds(b * modes, modes)
            hin = hin_ref[lane, seg, rowsb, :]
            ag = a * gb_ref[lane, rowsb, :]
            total = total + rb[rowsb, :] + ag * hin
            moment = moment + a * mb[rowsb, :] + (ag + a * a * db[rowsb, :]) * hin
            moment = moment + ag * kin_ref[lane, seg, rowsb, :]
        sums_ref[pl.ds(0, modes), lanes] = total
        sums_ref[pl.ds(modes, modes), lanes] = moment
    copy.wait()


def gather_body(segments, modes, *refs):
    count = len(segments)
    gb_refs, sums_refs = refs[:count], refs[count:2 * count]
    decay_ref, out_ref = refs[2 * count:]
    channels = decay_ref.shape[1]
    for lane in range(channels // LANES):
        lanes = pl.ds(lane * LANES, LANES)
        state = jnp.zeros((modes, LANES), F32)
        for seg in reversed(range(count)):
            power = jnp.exp(-decay_ref[:, lanes] * (segments[seg][1] // BLOCKS))
            for b in reversed(range(BLOCKS)):
                state = power * state + gb_refs[seg][lane, pl.ds(b * modes, modes), :]
        out_ref[pl.ds(0, modes), lanes] = state
    out_ref[pl.ds(modes, 2 * modes), :] = sum(ref[...] for ref in sums_refs)


def backward_pair_body(modes, tokens, message_ref, partner_ref, decay_ref, both_ref):
    _, core = place()
    state, sums = pl.ds(0, modes), pl.ds(modes, 2 * modes)
    first = jnp.where(core == 0, message_ref[state, :], partner_ref[state, :])
    second = jnp.where(core == 0, partner_ref[state, :], message_ref[state, :])
    both_ref[state, :] = first + jnp.exp(-decay_ref[...] * tokens) * second
    both_ref[sums, :] = message_ref[sums, :] + partner_ref[sums, :]


def finish_body(segments, modes, tokens, length, pairs, *refs):
    count = len(segments)
    aloc_refs, gb_refs = refs[:count], refs[count:2 * count]
    a_ref, r_ref, decay_ref, x2_ref, v_ref, partner_ref, both_ref = refs[2 * count:2 * count + 7]
    got_refs = refs[2 * count + 7:2 * count + 6 + pairs]
    (gx2_ref, gv_ref, rgrad_ref, dgrad_ref, gin, nat, gx2_here, gv_here, sems) = refs[2 * count + 6 + pairs:]
    channels = a_ref.shape[1]
    unroll = 4
    pair, core = place()
    states = []
    for lane in range(channels // LANES):
        lanes = pl.ds(lane * LANES, LANES)
        state = jnp.where(core == 0, partner_ref[pl.ds(0, modes), lanes], 0.0)
        for step, got_ref in enumerate(got_refs, 1):
            other = pair ^ step
            gap = jnp.maximum((2 * (other - pair - 1) + 1 - core) * tokens, 0).astype(F32)
            weight = jnp.where(other > pair, jnp.exp(-decay_ref[:, lanes] * gap), 0.0)
            state = state + weight * got_ref[pl.ds(0, modes), lanes]
        states.append(state)
    copies = []
    for seg in reversed(range(count)):
        start, rows = segments[seg]
        steps = rows // BLOCKS
        window = pl.ds(start, rows)
        for lane in range(channels // LANES):
            lanes = pl.ds(lane * LANES, LANES)
            decays = [spread(a_ref, m, lanes) for m in range(modes)]
            state = states[lane]
            power = jnp.exp(-decay_ref[:, lanes] * steps)
            for b in reversed(range(BLOCKS)):
                rowsb = pl.ds(b * modes, modes)
                gin[rowsb, :] = state
                state = power * state + gb_refs[seg][lane, rowsb, :]
            states[lane] = state
            edge = tuple(
                spread(r_ref, m, lanes) * decays[m] * gin[pl.ds(m, BLOCKS, stride=modes), :]
                for m in range(modes)
            )

            def body(outer, edge):
                edge = list(edge)
                for q in range(unroll):
                    i = steps - 1 - (outer * unroll + q)
                    here = pl.ds(pl.multiple_of(i * BLOCKS, BLOCKS), BLOCKS)
                    y = aloc_refs[seg][lane, here, :]
                    for m in range(modes):
                        y = y + edge[m]
                        edge[m] = edge[m] * decays[m]
                    nat[lane, pl.ds(start + i, BLOCKS, stride=steps), :] = y
                return tuple(edge)

            lax.fori_loop(0, steps // unroll, body, edge)
            adjoint = nat[lane, window, :]
            gx2_here[window, lanes] = (adjoint * v_ref[window, lanes].astype(F32)).astype(BF16)
            gv_here[window, lanes] = (adjoint * x2_ref[window, lanes].astype(F32)).astype(BF16)
        for j, (here, there) in enumerate(((gx2_here, gx2_ref), (gv_here, gv_ref))):
            copy = pltpu.make_async_copy(here.at[window, :], there.at[window, :], sems.at[seg, j])
            copy.start()
            copies.append(copy)
    sums = both_ref[pl.ds(modes, 2 * modes), :]
    for got_ref in got_refs:
        sums = sums + got_ref[pl.ds(modes, 2 * modes), :]
    owned = rgrad_ref.shape[0]
    row = lax.broadcasted_iota(jnp.int32, (owned, channels), 0) + lax.axis_index("ctx") * owned
    column = lax.broadcasted_iota(jnp.int32, (owned, channels), 1)
    pick = (row == column).astype(F32)

    def choose(values):
        return lax.dot_general(
            pick, values, (((1,), (1,)), ((), ())),
            precision=lax.Precision.HIGHEST, preferred_element_type=F32,
        )

    rgrad_ref[...] = choose(sums[:modes]) / length
    scale = r_ref[...] * decay_ref[...] * (float(length) ** 0.5)
    dgrad_ref[...] = -choose(scale * sums[modes:]) / length
    for copy in copies:
        copy.wait()


def on_device(g_out, w_out, gate_x1, gate_x2, value_v, residue, decay):
    tokens, channels = gate_x1.shape
    context_size = lax.axis_size("ctx")
    ch_size = lax.axis_size("ch")
    length = tokens * context_size
    modes = residue.shape[1]
    lane_tiles = channels // LANES
    owned = channels // context_size

    bits = [1 << bit for bit in range(ch_size.bit_length() - 1)]
    half_rows = tokens // 2
    chunks = [(0, half_rows, bits), (half_rows, half_rows, bits[::-1])]
    segments = [(start, rows) for start, rows, _ in chunks]
    count = len(chunks)
    layouts = [halving_layout(order) for _, _, order in chunks]
    cut = ch_size // 2

    rows_of = [(start, rows) for start, rows, _ in chunks]
    projected = project(
        g_out, w_out,
        [(*where, layout[:cut]) for where, layout in zip(rows_of, layouts)]
        + [(*where, layout[cut:]) for where, layout in zip(rows_of, layouts)], channels)
    sent = [lax.ppermute(piece, "ch", xor_pairs(ch_size, order[0]))
            for piece, (_, _, order) in zip(projected, chunks)]
    kept = projected[count:]

    decay_t = decay.T
    residue_t = residue.T
    a = jnp.exp(-decay_t)
    r = residue_t * length ** (-0.5)

    state_shape = jax.ShapeDtypeStruct((lane_tiles, count, BLOCKS * modes, LANES), F32)
    perm_shape = jax.ShapeDtypeStruct((lane_tiles, tokens, LANES), F32)
    work = tokens * channels * modes
    xperm, yloc, hb, eb, total = pl.pallas_call(
        functools.partial(forward_body, segments, modes),
        out_shape=[perm_shape, perm_shape, state_shape, state_shape,
                   jax.ShapeDtypeStruct((2 * modes, channels), F32)],
        scratch_shapes=[pltpu.VMEM((lane_tiles, tokens, LANES), F32)],
        compiler_params=params(),
        cost_estimate=pl.CostEstimate(flops=work * 6, bytes_accessed=tokens * channels * 12, transcendentals=0),
        name="forward",
    )(gate_x2, value_v, a, r, decay_t)

    pairs = context_size // 2
    partner = lax.ppermute(total, "ctx", xor_pairs(context_size, 1))
    both = pl.pallas_call(
        functools.partial(forward_pair_body, modes, tokens),
        out_shape=jax.ShapeDtypeStruct((2 * modes, channels), F32),
        compiler_params=params(),
        name="forward_pair",
    )(total, partner, decay_t)
    got = [lax.ppermute(both, "ctx", xor_pairs(context_size, 2 * step)) for step in range(1, pairs)]

    resp, hin, kin = pl.pallas_call(
        functools.partial(respond_body, segments, modes, tokens),
        out_shape=[perm_shape, state_shape, state_shape],
        compiler_params=params(),
        cost_estimate=pl.CostEstimate(flops=work * 2, bytes_accessed=tokens * channels * 8, transcendentals=0),
        name="respond",
    )(hb, eb, yloc, a, r, decay_t, partner, *got)

    alocs, gbs, sums = [], [], []
    *sent, _ = lax.optimization_barrier((*sent, got))
    arrived = [[piece] for piece in sent]
    for level in range(1, len(bits)):
        for which, (_, _, order) in enumerate(chunks):
            stop = cut >> level
            width = kept[which].shape[1]
            left = width - 2 * stop * channels
            away = kept[which][:, left:left + stop * channels].astype(F32)
            for piece in arrived[which]:
                left = piece.shape[1] - 2 * stop * channels
                away = away + piece[:, left:left + stop * channels].astype(F32)
            arrived[which].append(
                lax.ppermute(away.astype(BF16), "ch", xor_pairs(ch_size, order[level])))
    previous = []
    for seg, (start, rows) in enumerate(segments):
        block_shape = jax.ShapeDtypeStruct((lane_tiles, BLOCKS * modes, LANES), F32)
        pieces = arrived[seg]
        grad_x1, aloc, gb, partial_sums = pl.pallas_call(
            functools.partial(adjoint_body, (seg, start, rows), modes, len(pieces), len(previous)),
            in_specs=in_vmem(1 + len(pieces)) + [pl.BlockSpec(memory_space=HBM)] * len(previous) + in_vmem(7),
            out_specs=[pl.BlockSpec(memory_space=HBM)] + in_vmem(3),
            out_shape=[jax.ShapeDtypeStruct((tokens, channels), BF16),
                       jax.ShapeDtypeStruct((lane_tiles, rows, LANES), F32),
                       block_shape,
                       jax.ShapeDtypeStruct((2 * modes, channels), F32)],
            scratch_shapes=[pltpu.VMEM((lane_tiles, rows, LANES), F32)] * 2
            + [pltpu.VMEM((BLOCKS * modes, LANES), F32)] * 3
            + [pltpu.VMEM((rows, channels), BF16), pltpu.SemaphoreType.DMA(())],
            input_output_aliases={1 + len(pieces): 0} if previous else {},
            compiler_params=params(),
            cost_estimate=pl.CostEstimate(flops=rows * channels * modes * 10, bytes_accessed=rows * channels * 16, transcendentals=0),
            name="adjoint",
        )(kept[seg], *pieces, *previous, gate_x1, resp, xperm, hin, kin, a, r)
        previous = [grad_x1]
        alocs.append(aloc)
        gbs.append(gb)
        sums.append(partial_sums)

    message = pl.pallas_call(
        functools.partial(gather_body, segments, modes),
        out_shape=jax.ShapeDtypeStruct((3 * modes, channels), F32),
        compiler_params=params(),
        name="totals",
    )(*gbs, *sums, decay_t)
    partner = lax.ppermute(message, "ctx", xor_pairs(context_size, 1))
    both = pl.pallas_call(
        functools.partial(backward_pair_body, modes, tokens),
        out_shape=jax.ShapeDtypeStruct((3 * modes, channels), F32),
        compiler_params=params(),
        name="backward_pair",
    )(message, partner, decay_t)
    got = [lax.ppermute(both, "ctx", xor_pairs(context_size, 2 * step)) for step in range(1, pairs)]

    grad_x2, grad_v, residue_grad, decay_grad = pl.pallas_call(
        functools.partial(finish_body, segments, modes, tokens, length, pairs),
        in_specs=in_vmem(2 * count + 6 + pairs),
        out_specs=[pl.BlockSpec(memory_space=HBM)] * 2 + in_vmem(2),
        out_shape=[jax.ShapeDtypeStruct((tokens, channels), BF16)] * 2
        + [jax.ShapeDtypeStruct((owned, modes), F32)] * 2,
        scratch_shapes=[pltpu.VMEM((BLOCKS * modes, LANES), F32),
                        pltpu.VMEM((lane_tiles, tokens, LANES), F32),
                        pltpu.VMEM((tokens, channels), BF16),
                        pltpu.VMEM((tokens, channels), BF16),
                        pltpu.SemaphoreType.DMA((count, 2))],
        compiler_params=params(),
        cost_estimate=pl.CostEstimate(flops=work * 2, bytes_accessed=tokens * channels * 12, transcendentals=0),
        name="finish",
    )(*alocs, *gbs, a, r, decay_t, gate_x2, value_v, partner, both, *got)
    return grad_x1, grad_x2, grad_v, residue_grad, decay_grad


def solution(mesh):
    return jax.shard_map(
        on_device,
        mesh=mesh,
        in_specs=(
            P("ctx", "ch"),
            P(None, "ch"),
            P("ctx", "ch"),
            P("ctx", "ch"),
            P("ctx", "ch"),
            P("ch", None),
            P("ch", None),
        ),
        out_specs=(
            P("ctx", "ch"),
            P("ctx", "ch"),
            P("ctx", "ch"),
            P(("ch", "ctx"), None),
            P(("ch", "ctx"), None),
        ),
        check_vma=False,
    )
```

```python
import functools

import jax
import jax.numpy as jnp
from jax import lax
from jax.experimental import pallas as pl
from jax.experimental.pallas import tpu as pltpu
from jax.sharding import PartitionSpec as P

LANES = 128
PIECES = 2
FPARTS = 1
BLOCKS = 8
F32 = jnp.float32
BF16 = jnp.bfloat16


def halving_layout(order):
    if not order:
        return [0]
    rest = halving_layout(order[1:])
    return [offset ^ order[0] for offset in rest] + rest


def xor_pairs(count, step):
    return [(index, index ^ step) for index in range(count)]


HBM = pltpu.MemorySpace.HBM
VMEM = pltpu.MemorySpace.VMEM
CONTRACT_LAST = (((1,), (1,)), ((), ()))


def params(mebibytes=24):
    return pltpu.CompilerParams(vmem_limit_bytes=mebibytes * 2**20)


def in_vmem(count):
    return [pl.BlockSpec(memory_space=VMEM)] * count


def block_rows(offset, width):
    block = lax.axis_index("ch") ^ offset
    return pl.ds(pl.multiple_of(block * width, width), width)


def arrange(count):
    return [1, 3, 2, 0] if count == 4 else list(range(count))


def block_runs(offsets, arranged):
    places = sorted((arranged.index(offset), spot) for spot, offset in enumerate(offsets))
    runs = []
    for where, spot in places:
        if runs and runs[-1][1] + len(runs[-1][0]) == where:
            runs[-1][0].append(spot)
        else:
            runs.append(([spot], where))
    return runs


def project_body(work, width, pieces, g_ref, w_ref, *refs):
    count = len(work)
    out_refs = refs[:count]
    g_here, w_here, total, g_sems, w_sems = refs[count:]
    depth = g_ref.shape[1] // pieces
    arranged = arrange(w_ref.shape[0] // width)
    pending = {}

    def g_copy(rows, piece):
        columns = pl.ds(piece * depth, depth)
        return pltpu.make_async_copy(
            g_ref.at[rows, columns], g_here.at[rows, columns], g_sems.at[rows.start // rows.size, piece])

    def w_copy(offset, piece):
        columns = pl.ds(piece * depth, depth)
        there = pl.ds(arranged.index(offset) * width, width)
        return pltpu.make_async_copy(
            w_ref.at[block_rows(offset, width), columns], w_here.at[there, columns],
            w_sems.at[offset, piece])

    for start, rows, offsets in work:
        for piece in range(pieces):
            for key, copy in [((start, piece), lambda: g_copy(pl.ds(start, rows), piece))] + [
                    ((-1 - offset, piece), functools.partial(w_copy, offset, piece)) for offset in offsets]:
                if key not in pending:
                    pending[key] = copy()
                    pending[key].start()
    for (start, rows, offsets), out_ref in zip(work, out_refs):
        for piece in range(pieces):
            columns = pl.ds(piece * depth, depth)
            for key in [(start, piece)] + [(-1 - offset, piece) for offset in offsets]:
                copy = pending.pop(key, None)
                if copy is not None:
                    copy.wait()
            for spots, where in block_runs(offsets, arranged):
                product = lax.dot_general(
                    g_here[pl.ds(start, rows), columns],
                    w_here[pl.ds(where * width, len(spots) * width), columns],
                    CONTRACT_LAST, preferred_element_type=F32)
                for k, spot in enumerate(spots):
                    here = pl.ds(spot * width, width)
                    value = product[:, k * width:(k + 1) * width]
                    if piece > 0:
                        value = value + total[:, here]
                    if piece < pieces - 1:
                        total[:, here] = value
                    else:
                        out_ref[:, here] = value.astype(out_ref.dtype)


def project(g_out, w_out, work, width):
    blocks = w_out.shape[0] // width
    pieces = PIECES
    shapes = [jax.ShapeDtypeStruct((rows, len(offsets) * width), BF16) for _, rows, offsets in work]
    groups = g_out.shape[0] // work[0][1]
    return pl.pallas_call(
        functools.partial(project_body, work, width, pieces),
        in_specs=[pl.BlockSpec(memory_space=HBM)] * 2,
        out_specs=in_vmem(len(work)),
        out_shape=shapes,
        scratch_shapes=[
            pltpu.VMEM(g_out.shape, BF16),
            pltpu.VMEM(w_out.shape, BF16),
            pltpu.VMEM(shapes[0].shape, F32),
            pltpu.SemaphoreType.DMA((groups, pieces)),
            pltpu.SemaphoreType.DMA((blocks, pieces)),
        ],
        compiler_params=params(60),
        name="project",
    )(g_out, w_out)


def spread(ref, row, lanes):
    return jnp.broadcast_to(ref[pl.ds(row, 1), lanes], (BLOCKS, LANES))


def forward_body(segments, modes, x2_ref, v_ref, a_ref, decay_ref,
                 xperm_ref, hb_ref, eb_ref, total_ref, nat):
    channels = x2_ref.shape[1]
    unroll = 4
    group = modes // FPARTS
    for lane in range(channels // LANES):
        lanes = pl.ds(lane * LANES, LANES)
        mixed = (x2_ref[:, lanes].astype(F32) * v_ref[:, lanes].astype(F32)).astype(BF16)
        nat[lane] = mixed.astype(F32)
        for seg, (start, rows) in enumerate(segments):
            steps = rows // BLOCKS
            for part in range(FPARTS):
                decays = [spread(a_ref, part * group + m, lanes) for m in range(group)]

                def body(outer, carry):
                    h, e = list(carry[0]), list(carry[1])
                    for q in range(unroll):
                        i = outer * unroll + q
                        here = pl.ds(pl.multiple_of(start + i * BLOCKS, BLOCKS), BLOCKS)
                        if part == 0:
                            x = nat[lane, pl.ds(start + i, BLOCKS, stride=steps), :]
                            xperm_ref[lane, here, :] = x
                        else:
                            x = xperm_ref[lane, here, :]
                        for m in range(group):
                            e[m] = decays[m] * e[m] + h[m]
                            h[m] = decays[m] * h[m] + x
                    return tuple(h), tuple(e)

                zero = (jnp.zeros((BLOCKS, LANES), F32),) * group
                h, e = lax.fori_loop(0, steps // unroll, body, (zero, zero))
                for m in range(group):
                    row = pl.ds(part * group + m, BLOCKS, stride=modes)
                    hb_ref[lane, seg, row, :] = h[m]
                    eb_ref[lane, seg, row, :] = e[m]
        a = a_ref[:, lanes]
        state = jnp.zeros((modes, LANES), F32)
        moment = jnp.zeros((modes, LANES), F32)
        for seg, (start, rows) in enumerate(segments):
            steps = rows // BLOCKS
            power = jnp.exp(-decay_ref[:, lanes] * steps)
            for b in range(BLOCKS):
                rowsb = pl.ds(b * modes, modes)
                moment = power * (moment + steps * state) + a * eb_ref[lane, seg, rowsb, :]
                state = power * state + hb_ref[lane, seg, rowsb, :]
        total_ref[pl.ds(0, modes), lanes] = state
        total_ref[pl.ds(modes, modes), lanes] = moment


def place():
    index = lax.axis_index("ctx")
    return index // 2, index % 2


def forward_pair_body(modes, tokens, total_ref, partner_ref, decay_ref, both_ref):
    _, core = place()
    state, moment = pl.ds(0, modes), pl.ds(modes, modes)
    power = jnp.exp(-decay_ref[...] * tokens)
    later = core == 1
    first_h = jnp.where(later, partner_ref[state, :], total_ref[state, :])
    first_k = jnp.where(later, partner_ref[moment, :], total_ref[moment, :])
    second_h = jnp.where(later, total_ref[state, :], partner_ref[state, :])
    second_k = jnp.where(later, total_ref[moment, :], partner_ref[moment, :])
    both_ref[state, :] = second_h + power * first_h
    both_ref[moment, :] = second_k + power * (first_k + tokens * first_h)


def respond_body(segments, modes, tokens, hb_ref, eb_ref, xperm_ref, a_ref, r_ref, decay_ref, partner_ref, *refs):
    got_refs, (resp_ref, store_ref, hin_ref, kin_ref, yloc) = refs[:-5], refs[-5:]
    half = modes // 2
    pair, core = place()
    channels = a_ref.shape[1]
    unroll = 4
    for lane in range(channels // LANES):
        lanes = pl.ds(lane * LANES, LANES)
        a = a_ref[:, lanes]
        state = jnp.where(core == 1, partner_ref[pl.ds(0, modes), lanes], 0.0)
        moment = jnp.where(core == 1, partner_ref[pl.ds(modes, modes), lanes], 0.0)
        for step, got_ref in enumerate(got_refs, 1):
            other = pair ^ step
            gap = jnp.maximum((2 * (pair - other - 1) + core) * tokens, 0).astype(F32)
            weight = jnp.where(other < pair, jnp.exp(-decay_ref[:, lanes] * gap), 0.0)
            got = got_ref[pl.ds(0, modes), lanes]
            state = state + weight * got
            moment = moment + weight * (got_ref[pl.ds(modes, modes), lanes] + gap * got)
        for seg, (start, rows) in enumerate(segments):
            steps = rows // BLOCKS
            power = jnp.exp(-decay_ref[:, lanes] * steps)
            for b in range(BLOCKS):
                rowsb = pl.ds(b * modes, modes)
                hin_ref[lane, seg, rowsb, :] = state
                kin_ref[lane, seg, rowsb, :] = moment
                moment = power * (moment + steps * state) + a * eb_ref[lane, seg, rowsb, :]
                state = power * state + hb_ref[lane, seg, rowsb, :]
        for seg, (start, rows) in enumerate(segments):
            steps = rows // BLOCKS
            for part in range(2):
                decays = [spread(a_ref, part * half + m, lanes) for m in range(half)]
                weights = [spread(r_ref, part * half + m, lanes) for m in range(half)]

                def body(outer, h):
                    h = list(h)
                    for q in range(unroll):
                        i = outer * unroll + q
                        here = pl.ds(pl.multiple_of(start + i * BLOCKS, BLOCKS), BLOCKS)
                        x = xperm_ref[lane, here, :]
                        y = None
                        for m in range(half):
                            h[m] = decays[m] * h[m] + x
                            store_ref[lane, part * half + m, here, :] = h[m]
                            term = weights[m] * h[m]
                            y = term if y is None else y + term
                        if part == 0:
                            yloc[here, :] = y
                        else:
                            y = y + yloc[here, :]
                            resp_ref[lane, pl.ds(start + i, BLOCKS, stride=steps), :] = y
                    return tuple(h)

                begin = tuple(
                    hin_ref[lane, seg, pl.ds(part * half + m, BLOCKS, stride=modes), :]
                    for m in range(half))
                lax.fori_loop(0, steps // unroll, body, begin)


def adjoint_body(segment, modes, received, has_previous, kept_ref, *refs):
    seg, start, rows = segment
    recv_refs = refs[:received]
    refs = refs[received + has_previous:]
    x1_ref, resp_ref, store_ref, hin_ref, kin_ref, a_ref, r_ref, grad_ref = refs[:8]
    aloc_ref, gb_ref, sums_ref, nat, uperm, rb, qb, grad_here, sem = refs[-9:]
    steps = rows // BLOCKS
    channels = x1_ref.shape[1]
    unroll = 4
    half = modes // 2
    window = pl.ds(start, rows)
    for lane in range(channels // LANES):
        lanes = pl.ds(lane * LANES, LANES)

        def own(ref):
            return ref[:, pl.ds(ref.shape[1] - channels + lane * LANES, LANES)]

        grad_in = own(kept_ref).astype(F32)
        for recv_ref in recv_refs:
            grad_in = grad_in + own(recv_ref).astype(F32)
        grad_here[:, lanes] = (grad_in * resp_ref[lane, window, :]).astype(BF16)
        nat[lane] = (grad_in * x1_ref[window, lanes].astype(F32)).astype(BF16).astype(F32)
    copy = pltpu.make_async_copy(grad_here, grad_ref.at[window, :], sem)
    copy.start()
    for lane in range(channels // LANES):
        lanes = pl.ds(lane * LANES, LANES)
        for part in range(2):
            decays = [spread(a_ref, part * half + m, lanes) for m in range(half)]
            weights = [spread(r_ref, part * half + m, lanes) for m in range(half)]

            def body(outer, carry):
                g, racc, qacc = (list(item) for item in carry)
                for q in range(unroll):
                    i = steps - 1 - (outer * unroll + q)
                    here = pl.ds(pl.multiple_of(i * BLOCKS, BLOCKS), BLOCKS)
                    if part == 0:
                        u = nat[lane, pl.ds(i, BLOCKS, stride=steps), :]
                        uperm[lane, here, :] = u
                    else:
                        u = uperm[lane, here, :]
                    there = pl.ds(pl.multiple_of(start + i * BLOCKS, BLOCKS), BLOCKS)
                    y = None
                    for m in range(half):
                        h = store_ref[lane, part * half + m, there, :]
                        g[m] = decays[m] * g[m] + u
                        racc[m] = racc[m] + u * h
                        qacc[m] = qacc[m] + g[m] * h
                        term = weights[m] * g[m]
                        y = term if y is None else y + term
                    if part == 1:
                        y = y + aloc_ref[lane, here, :]
                    aloc_ref[lane, here, :] = y
                return tuple(g), tuple(racc), tuple(qacc)

            zero = (jnp.zeros((BLOCKS, LANES), F32),) * half
            g, racc, qacc = lax.fori_loop(0, steps // unroll, body, (zero,) * 3)
            for m in range(half):
                row = pl.ds(part * half + m, BLOCKS, stride=modes)
                gb_ref[lane, row, :] = g[m]
                rb[row, :] = racc[m]
                qb[row, :] = qacc[m]
        a = a_ref[:, lanes]
        total = jnp.zeros((modes, LANES), F32)
        moment = jnp.zeros((modes, LANES), F32)
        for b in range(BLOCKS):
            rowsb = pl.ds(b * modes, modes)
            before = hin_ref[lane, seg, rowsb, :] + kin_ref[lane, seg, rowsb, :]
            total = total + rb[rowsb, :]
            moment = moment + qb[rowsb, :] - rb[rowsb, :] + a * gb_ref[lane, rowsb, :] * before
        sums_ref[pl.ds(0, modes), lanes] = total
        sums_ref[pl.ds(modes, modes), lanes] = moment
    copy.wait()


def gather_body(segments, modes, *refs):
    count = len(segments)
    gb_refs, sums_refs = refs[:count], refs[count:2 * count]
    scale_ref, decay_ref, out_ref = refs[2 * count:]
    channels = decay_ref.shape[1]
    for lane in range(channels // LANES):
        lanes = pl.ds(lane * LANES, LANES)
        state = jnp.zeros((modes, LANES), F32)
        for seg in reversed(range(count)):
            power = jnp.exp(-decay_ref[:, lanes] * (segments[seg][1] // BLOCKS))
            for b in reversed(range(BLOCKS)):
                state = power * state + gb_refs[seg][lane, pl.ds(b * modes, modes), :]
        out_ref[pl.ds(0, modes), lanes] = state
    sums = sum(ref[...] for ref in sums_refs)
    out_ref[pl.ds(modes, modes), :] = sums[:modes]
    out_ref[pl.ds(2 * modes, modes), :] = sums[modes:] * scale_ref[...]


def three_parts(values):
    parts = []
    for _ in range(3):
        parts.append(values.astype(BF16))
        values = values - parts[-1].astype(F32)
    return parts


def pick(values, chosen, dims):
    return sum(
        lax.dot_general(part, chosen, dims, preferred_element_type=F32)
        for part in three_parts(values)
    )


def backward_pair_body(modes, tokens, owned, message_ref, partner_ref, decay_ref, both_ref):
    _, core = place()
    channels = decay_ref.shape[1]
    state, sums = pl.ds(0, modes), pl.ds(modes, 2 * modes)
    first = jnp.where(core == 0, message_ref[state, :], partner_ref[state, :])
    second = jnp.where(core == 0, partner_ref[state, :], message_ref[state, :])
    both_ref[state, :] = first + jnp.exp(-decay_ref[...] * tokens) * second
    channel = lax.broadcasted_iota(jnp.int32, (channels, LANES), 0)
    lane = lax.broadcasted_iota(jnp.int32, (channels, LANES), 1)
    wanted = (2 * (lane // owned) + core) * owned + lane % owned
    picked = pick(message_ref[sums, :] + partner_ref[sums, :], (channel == wanted).astype(BF16),
                  (((1,), (0,)), ((), ())))
    tiles = channels // LANES
    rows = 2 * modes // tiles
    for tile in range(tiles):
        both_ref[pl.ds(modes, rows), pl.ds(tile * LANES, LANES)] = picked[tile * rows:(tile + 1) * rows]


def finish_body(segments, modes, tokens, length, pairs, *refs):
    count = len(segments)
    aloc_refs, gb_refs = refs[:count], refs[count:2 * count]
    a_ref, r_ref, decay_ref, x2_ref, v_ref, partner_ref, both_ref = refs[2 * count:2 * count + 7]
    got_refs = refs[2 * count + 7:2 * count + 6 + pairs]
    gx2_ref, gv_ref, rgrad_ref, dgrad_ref, gin, nat, gx2_here, gv_here, sems = refs[-9:]
    channels = a_ref.shape[1]
    unroll = 4
    pair, core = place()
    states = []
    for lane in range(channels // LANES):
        lanes = pl.ds(lane * LANES, LANES)
        state = jnp.where(core == 0, partner_ref[pl.ds(0, modes), lanes], 0.0)
        for step, got_ref in enumerate(got_refs, 1):
            other = pair ^ step
            gap = jnp.maximum((2 * (other - pair - 1) + 1 - core) * tokens, 0).astype(F32)
            weight = jnp.where(other > pair, jnp.exp(-decay_ref[:, lanes] * gap), 0.0)
            state = state + weight * got_ref[pl.ds(0, modes), lanes]
        states.append(state)
    copies = []
    for seg in reversed(range(count)):
        start, rows = segments[seg]
        steps = rows // BLOCKS
        window = pl.ds(start, rows)
        for lane in range(channels // LANES):
            lanes = pl.ds(lane * LANES, LANES)
            decays = [spread(a_ref, m, lanes) for m in range(modes)]
            state = states[lane]
            power = jnp.exp(-decay_ref[:, lanes] * steps)
            for b in reversed(range(BLOCKS)):
                rowsb = pl.ds(b * modes, modes)
                gin[rowsb, :] = state
                state = power * state + gb_refs[seg][lane, rowsb, :]
            states[lane] = state
            edge = tuple(
                spread(r_ref, m, lanes) * decays[m] * gin[pl.ds(m, BLOCKS, stride=modes), :]
                for m in range(modes)
            )

            def body(outer, edge):
                edge = list(edge)
                for q in range(unroll):
                    i = steps - 1 - (outer * unroll + q)
                    here = pl.ds(pl.multiple_of(i * BLOCKS, BLOCKS), BLOCKS)
                    y = aloc_refs[seg][lane, here, :]
                    for m in range(modes):
                        y = y + edge[m]
                        edge[m] = edge[m] * decays[m]
                    nat[lane, pl.ds(start + i, BLOCKS, stride=steps), :] = y
                return tuple(edge)

            lax.fori_loop(0, steps // unroll, body, edge)
            adjoint = nat[lane, window, :]
            gx2_here[window, lanes] = (adjoint * v_ref[window, lanes].astype(F32)).astype(BF16)
            gv_here[window, lanes] = (adjoint * x2_ref[window, lanes].astype(F32)).astype(BF16)
        for j, (here, there) in enumerate(((gx2_here, gx2_ref), (gv_here, gv_ref))):
            copy = pltpu.make_async_copy(here.at[window, :], there.at[window, :], sems.at[seg, j])
            copy.start()
            copies.append(copy)
    owned = rgrad_ref.shape[0]
    tiles = channels // LANES
    lower = pl.ds(modes, 2 * modes // tiles)
    sums = both_ref[lower, :]
    for got_ref in got_refs:
        sums = sums + got_ref[lower, :]
    row = lax.broadcasted_iota(jnp.int32, (owned, LANES), 0)
    column = lax.broadcasted_iota(jnp.int32, (owned, LANES), 1)
    chosen = (column == pair * owned + row).astype(BF16)

    def choose(values):
        return sum(
            lax.dot_general(chosen, part, CONTRACT_LAST, preferred_element_type=F32)
            for part in three_parts(values)
        )

    if tiles == 1:
        residue_sums, decay_sums = sums[:modes], sums[modes:]
    else:
        residue_sums, decay_sums = sums[:, :LANES], sums[:, LANES:]
    rgrad_ref[...] = choose(residue_sums) / length
    dgrad_ref[...] = choose(decay_sums) / length
    for copy in copies:
        copy.wait()


def on_device(g_out, w_out, gate_x1, gate_x2, value_v, residue, decay):
    tokens, channels = gate_x1.shape
    context_size = lax.axis_size("ctx")
    ch_size = lax.axis_size("ch")
    length = tokens * context_size
    modes = residue.shape[1]
    lane_tiles = channels // LANES
    owned = channels // context_size

    bits = [1 << bit for bit in range(ch_size.bit_length() - 1)]
    half_rows = tokens // 2
    chunks = [(0, half_rows, bits), (half_rows, half_rows, bits[::-1])]
    segments = [(start, rows) for start, rows, _ in chunks]
    count = len(chunks)
    layouts = [halving_layout(order) for _, _, order in chunks]
    cut = ch_size // 2

    rows_of = [(start, rows) for start, rows, _ in chunks]
    projected = project(
        g_out, w_out,
        [(*where, layout[:cut]) for where, layout in zip(rows_of, layouts)]
        + [(*where, layout[cut:]) for where, layout in zip(rows_of, layouts)], channels)
    sent = [lax.ppermute(piece, "ch", xor_pairs(ch_size, order[0]))
            for piece, (_, _, order) in zip(projected, chunks)]
    kept = projected[count:]

    decay_t = decay.T
    residue_t = residue.T
    a = jnp.exp(-decay_t)
    r = residue_t * length ** (-0.5)
    scale = -residue_t * decay_t

    state_shape = jax.ShapeDtypeStruct((lane_tiles, count, BLOCKS * modes, LANES), F32)
    perm_shape = jax.ShapeDtypeStruct((lane_tiles, tokens, LANES), F32)
    work = tokens * channels * modes
    xperm, hb, eb, total = pl.pallas_call(
        functools.partial(forward_body, segments, modes),
        out_shape=[perm_shape, state_shape, state_shape,
                   jax.ShapeDtypeStruct((2 * modes, channels), F32)],
        scratch_shapes=[pltpu.VMEM((lane_tiles, tokens, LANES), F32)],
        compiler_params=params(),
        cost_estimate=pl.CostEstimate(flops=work * 6, bytes_accessed=tokens * channels * 12, transcendentals=0),
        name="forward",
    )(gate_x2, value_v, a, decay_t)

    pairs = context_size // 2
    partner = lax.ppermute(total, "ctx", xor_pairs(context_size, 1))
    both = pl.pallas_call(
        functools.partial(forward_pair_body, modes, tokens),
        out_shape=jax.ShapeDtypeStruct((2 * modes, channels), F32),
        compiler_params=params(),
        name="forward_pair",
    )(total, partner, decay_t)
    got = [lax.ppermute(both, "ctx", xor_pairs(context_size, 2 * step)) for step in range(1, pairs)]

    store_shape = jax.ShapeDtypeStruct((lane_tiles, modes, tokens, LANES), F32)
    resp, store, hin, kin = pl.pallas_call(
        functools.partial(respond_body, segments, modes, tokens),
        out_shape=[perm_shape, store_shape, state_shape, state_shape],
        scratch_shapes=[pltpu.VMEM((tokens, LANES), F32)],
        compiler_params=params(),
        cost_estimate=pl.CostEstimate(flops=work * 4, bytes_accessed=tokens * channels * 8, transcendentals=0),
        name="respond",
    )(hb, eb, xperm, a, r, decay_t, partner, *got)

    alocs, gbs, sums = [], [], []
    *sent, _ = lax.optimization_barrier((*sent, got))
    arrived = [[piece] for piece in sent]
    for level in range(1, len(bits)):
        for which, (_, _, order) in enumerate(chunks):
            stop = cut >> level
            width = kept[which].shape[1]
            left = width - 2 * stop * channels
            away = kept[which][:, left:left + stop * channels].astype(F32)
            for piece in arrived[which]:
                left = piece.shape[1] - 2 * stop * channels
                away = away + piece[:, left:left + stop * channels].astype(F32)
            arrived[which].append(
                lax.ppermute(away.astype(BF16), "ch", xor_pairs(ch_size, order[level])))
    previous = []
    for seg, (start, rows) in enumerate(segments):
        block_shape = jax.ShapeDtypeStruct((lane_tiles, BLOCKS * modes, LANES), F32)
        pieces = arrived[seg]
        *buffers, aloc, gb, partial_sums = pl.pallas_call(
            functools.partial(adjoint_body, (seg, start, rows), modes, len(pieces), len(previous)),
            in_specs=in_vmem(1 + len(pieces)) + [pl.BlockSpec(memory_space=HBM)] * len(previous) + in_vmem(7),
            out_specs=[pl.BlockSpec(memory_space=HBM)] * 3 + in_vmem(3),
            out_shape=[jax.ShapeDtypeStruct((tokens, channels), BF16)] * 3
            + [
                       jax.ShapeDtypeStruct((lane_tiles, rows, LANES), F32),
                       block_shape,
                       jax.ShapeDtypeStruct((2 * modes, channels), F32)],
            scratch_shapes=[pltpu.VMEM((lane_tiles, rows, LANES), F32)] * 2
            + [pltpu.VMEM((BLOCKS * modes, LANES), F32)] * 2
            + [pltpu.VMEM((rows, channels), BF16), pltpu.SemaphoreType.DMA(())],
            input_output_aliases={1 + len(pieces) + j: j for j in range(len(previous))},
            compiler_params=params(),
            cost_estimate=pl.CostEstimate(flops=rows * channels * modes * 8, bytes_accessed=rows * channels * 16, transcendentals=0),
            name="adjoint",
        )(kept[seg], *pieces, *previous, gate_x1, resp, store, hin, kin, a, r)
        previous = buffers
        alocs.append(aloc)
        gbs.append(gb)
        sums.append(partial_sums)

    message = pl.pallas_call(
        functools.partial(gather_body, segments, modes),
        out_shape=jax.ShapeDtypeStruct((3 * modes, channels), F32),
        compiler_params=params(),
        name="totals",
    )(*gbs, *sums, scale, decay_t)
    partner = lax.ppermute(message, "ctx", xor_pairs(context_size, 1))
    both = pl.pallas_call(
        functools.partial(backward_pair_body, modes, tokens, owned),
        out_shape=jax.ShapeDtypeStruct((modes + 2 * modes // lane_tiles, channels), F32),
        compiler_params=params(),
        name="backward_pair",
    )(message, partner, decay_t)
    got = [lax.ppermute(both, "ctx", xor_pairs(context_size, 2 * step)) for step in range(1, pairs)]

    grad_x2, grad_v, residue_grad, decay_grad = pl.pallas_call(
        functools.partial(finish_body, segments, modes, tokens, length, pairs),
        in_specs=in_vmem(2 * count + 6 + pairs) + [pl.BlockSpec(memory_space=HBM)] * 2,
        out_specs=[pl.BlockSpec(memory_space=HBM)] * 2 + in_vmem(2),
        out_shape=[jax.ShapeDtypeStruct((tokens, channels), BF16)] * 2
        + [jax.ShapeDtypeStruct((owned, modes), F32)] * 2,
        scratch_shapes=[pltpu.VMEM((BLOCKS * modes, LANES), F32),
                        pltpu.VMEM((lane_tiles, tokens, LANES), F32),
                        pltpu.VMEM((tokens, channels), BF16),
                        pltpu.VMEM((tokens, channels), BF16),
                        pltpu.SemaphoreType.DMA((count, 2))],
        input_output_aliases={2 * count + 6 + pairs: 0, 2 * count + 7 + pairs: 1},
        compiler_params=params(),
        cost_estimate=pl.CostEstimate(flops=work * 2, bytes_accessed=tokens * channels * 12, transcendentals=0),
        name="finish",
    )(*alocs, *gbs, a, r, decay_t, gate_x2, value_v, partner, both, *got, *previous[1:])
    return previous[0], grad_x2, grad_v, residue_grad, decay_grad


def solution(mesh):
    return jax.shard_map(
        on_device,
        mesh=mesh,
        in_specs=(
            P("ctx", "ch"),
            P(None, "ch"),
            P("ctx", "ch"),
            P("ctx", "ch"),
            P("ctx", "ch"),
            P("ch", None),
            P("ch", None),
        ),
        out_specs=(
            P("ctx", "ch"),
            P("ctx", "ch"),
            P("ctx", "ch"),
            P(("ch", "ctx"), None),
            P(("ch", "ctx"), None),
        ),
        check_vma=False,
    )
```

```python
import functools

import jax
import jax.numpy as jnp
from jax import lax
from jax.experimental import pallas as pl
from jax.experimental.pallas import tpu as pltpu
from jax.sharding import PartitionSpec as P

LANES = 128
PIECES = 2
FPARTS = 2
KEPT = jnp.bfloat16
BLOCKS = 8
F32 = jnp.float32
BF16 = jnp.bfloat16


def halving_layout(order):
    if not order:
        return [0]
    rest = halving_layout(order[1:])
    return [offset ^ order[0] for offset in rest] + rest


def xor_pairs(count, step):
    return [(index, index ^ step) for index in range(count)]


HBM = pltpu.MemorySpace.HBM
VMEM = pltpu.MemorySpace.VMEM
CONTRACT_LAST = (((1,), (1,)), ((), ()))


def params(mebibytes=24):
    return pltpu.CompilerParams(vmem_limit_bytes=mebibytes * 2**20)


def cost(microseconds):
    return pl.CostEstimate(flops=int(microseconds * 1.1e9), bytes_accessed=0, transcendentals=0)


def in_vmem(count):
    return [pl.BlockSpec(memory_space=VMEM)] * count


def block_rows(offset, width):
    block = lax.axis_index("ch") ^ offset
    return pl.ds(pl.multiple_of(block * width, width), width)


def arrange(count):
    return [1, 3, 2, 0] if count == 4 else list(range(count))


def block_runs(offsets, arranged):
    places = sorted((arranged.index(offset), spot) for spot, offset in enumerate(offsets))
    runs = []
    for where, spot in places:
        if runs and runs[-1][1] + len(runs[-1][0]) == where:
            runs[-1][0].append(spot)
        else:
            runs.append(([spot], where))
    return runs


def project_body(work, width, pieces, g_ref, w_ref, *refs):
    count = len(work)
    out_refs = refs[:count]
    out_here = refs[count:2 * count]
    g_here, w_here, total, g_sems, w_sems, out_sems = refs[2 * count:]
    depth = g_ref.shape[1] // pieces
    arranged = arrange(w_ref.shape[0] // width)
    pending = {}

    def g_copy(rows, piece):
        columns = pl.ds(piece * depth, depth)
        return pltpu.make_async_copy(
            g_ref.at[rows, columns], g_here.at[rows, columns], g_sems.at[rows.start // rows.size, piece])

    def w_copy(offset, piece):
        columns = pl.ds(piece * depth, depth)
        there = pl.ds(arranged.index(offset) * width, width)
        return pltpu.make_async_copy(
            w_ref.at[block_rows(offset, width), columns], w_here.at[there, columns],
            w_sems.at[offset, piece])

    for start, rows, offsets in work:
        for piece in range(pieces):
            for key, copy in [((start, piece), lambda: g_copy(pl.ds(start, rows), piece))] + [
                    ((-1 - offset, piece), functools.partial(w_copy, offset, piece)) for offset in offsets]:
                if key not in pending:
                    pending[key] = copy()
                    pending[key].start()
    leaving = []
    for which, (start, rows, offsets) in enumerate(work):
        out_ref = out_here[which]
        for piece in range(pieces):
            columns = pl.ds(piece * depth, depth)
            for key in [(start, piece)] + [(-1 - offset, piece) for offset in offsets]:
                copy = pending.pop(key, None)
                if copy is not None:
                    copy.wait()
            for spots, where in block_runs(offsets, arranged):
                product = lax.dot_general(
                    g_here[pl.ds(start, rows), columns],
                    w_here[pl.ds(where * width, len(spots) * width), columns],
                    CONTRACT_LAST, preferred_element_type=F32)
                for k, spot in enumerate(spots):
                    here = pl.ds(spot * width, width)
                    value = product[:, k * width:(k + 1) * width]
                    if piece > 0:
                        value = value + total[:, here]
                    if piece < pieces - 1:
                        total[:, here] = value
                    else:
                        out_ref[:, here] = value.astype(out_ref.dtype)
        leaving.append(pltpu.make_async_copy(out_ref, out_refs[which], out_sems.at[which]))
        leaving[-1].start()
    for copy in leaving:
        copy.wait()


def project(g_out, w_out, work, width):
    blocks = w_out.shape[0] // width
    pieces = PIECES
    shapes = [jax.ShapeDtypeStruct((rows, len(offsets) * width), BF16) for _, rows, offsets in work]
    groups = g_out.shape[0] // work[0][1]
    return pl.pallas_call(
        functools.partial(project_body, work, width, pieces),
        in_specs=[pl.BlockSpec(memory_space=HBM)] * 2,
        out_specs=[pl.BlockSpec(memory_space=HBM)] * len(work),
        out_shape=shapes,
        scratch_shapes=[pltpu.VMEM(shape.shape, BF16) for shape in shapes] + [
            pltpu.VMEM(g_out.shape, BF16),
            pltpu.VMEM(w_out.shape, BF16),
            pltpu.VMEM(shapes[0].shape, F32),
            pltpu.SemaphoreType.DMA((groups, pieces)),
            pltpu.SemaphoreType.DMA((blocks, pieces)),
            pltpu.SemaphoreType.DMA((len(work),)),
        ],
        compiler_params=params(60),
        cost_estimate=cost(5),
        name="project",
    )(g_out, w_out)


def project_kept_body(work, width, g_ref, w_ref, *out_refs):
    for (start, rows, offsets), out_ref in zip(work, out_refs):
        for spot, offset in enumerate(offsets):
            out_ref[:, pl.ds(spot * width, width)] = lax.dot_general(
                g_ref[pl.ds(start, rows), :], w_ref[block_rows(offset, width), :],
                CONTRACT_LAST, preferred_element_type=F32).astype(out_ref.dtype)


def project_kept(g_out, w_out, work, width):
    return pl.pallas_call(
        functools.partial(project_kept_body, work, width),
        in_specs=in_vmem(2),
        out_specs=in_vmem(len(work)),
        out_shape=[jax.ShapeDtypeStruct((rows, len(offsets) * width), KEPT)
                   for _, rows, offsets in work],
        compiler_params=params(),
        cost_estimate=cost(3),
        name="project_kept",
    )(g_out, w_out)


def spread(ref, row, lanes):
    return jnp.broadcast_to(ref[pl.ds(row, 1), lanes], (BLOCKS, LANES))


def forward_body(segments, modes, x2_ref, v_ref, a_ref, decay_ref,
                 xperm_ref, hb_ref, eb_ref, total_ref, nat):
    channels = x2_ref.shape[1]
    unroll = 4
    group = modes // FPARTS
    for lane in range(channels // LANES):
        lanes = pl.ds(lane * LANES, LANES)
        mixed = (x2_ref[:, lanes].astype(F32) * v_ref[:, lanes].astype(F32)).astype(BF16)
        nat[lane] = mixed.astype(F32)
        for seg, (start, rows) in enumerate(segments):
            steps = rows // BLOCKS
            for part in range(FPARTS):
                decays = [spread(a_ref, part * group + m, lanes) for m in range(group)]

                def body(outer, carry):
                    h, e = list(carry[0]), list(carry[1])
                    for q in range(unroll):
                        i = outer * unroll + q
                        here = pl.ds(pl.multiple_of(start + i * BLOCKS, BLOCKS), BLOCKS)
                        if part == 0:
                            x = nat[lane, pl.ds(start + i, BLOCKS, stride=steps), :]
                            xperm_ref[lane, here, :] = x
                        else:
                            x = xperm_ref[lane, here, :]
                        for m in range(group):
                            e[m] = decays[m] * e[m] + h[m]
                            h[m] = decays[m] * h[m] + x
                    return tuple(h), tuple(e)

                zero = (jnp.zeros((BLOCKS, LANES), F32),) * group
                h, e = lax.fori_loop(0, steps // unroll, body, (zero, zero))
                for m in range(group):
                    row = pl.ds(part * group + m, BLOCKS, stride=modes)
                    hb_ref[lane, seg, row, :] = h[m]
                    eb_ref[lane, seg, row, :] = e[m]
        a = a_ref[:, lanes]
        state = jnp.zeros((modes, LANES), F32)
        moment = jnp.zeros((modes, LANES), F32)
        for seg, (start, rows) in enumerate(segments):
            steps = rows // BLOCKS
            power = jnp.exp(-decay_ref[:, lanes] * steps)
            for b in range(BLOCKS):
                rowsb = pl.ds(b * modes, modes)
                moment = power * (moment + steps * state) + a * eb_ref[lane, seg, rowsb, :]
                state = power * state + hb_ref[lane, seg, rowsb, :]
        total_ref[pl.ds(0, modes), lanes] = state
        total_ref[pl.ds(modes, modes), lanes] = moment


def place():
    index = lax.axis_index("ctx")
    return index // 2, index % 2


def forward_pair_body(modes, tokens, total_ref, partner_ref, decay_ref, both_ref):
    _, core = place()
    state, moment = pl.ds(0, modes), pl.ds(modes, modes)
    power = jnp.exp(-decay_ref[...] * tokens)
    later = core == 1
    first_h = jnp.where(later, partner_ref[state, :], total_ref[state, :])
    first_k = jnp.where(later, partner_ref[moment, :], total_ref[moment, :])
    second_h = jnp.where(later, total_ref[state, :], partner_ref[state, :])
    second_k = jnp.where(later, total_ref[moment, :], partner_ref[moment, :])
    both_ref[state, :] = second_h + power * first_h
    both_ref[moment, :] = second_k + power * (first_k + tokens * first_h)


def respond_body(segments, modes, tokens, hb_ref, eb_ref, xperm_ref, a_ref, r_ref, decay_ref, partner_ref, *refs):
    got_refs, (resp_ref, store_ref, hin_ref, kin_ref, yloc) = refs[:-5], refs[-5:]
    half = modes // 2
    pair, core = place()
    channels = a_ref.shape[1]
    unroll = 4
    for lane in range(channels // LANES):
        lanes = pl.ds(lane * LANES, LANES)
        a = a_ref[:, lanes]
        state = jnp.where(core == 1, partner_ref[pl.ds(0, modes), lanes], 0.0)
        moment = jnp.where(core == 1, partner_ref[pl.ds(modes, modes), lanes], 0.0)
        for step, got_ref in enumerate(got_refs, 1):
            other = pair ^ step
            gap = jnp.maximum((2 * (pair - other - 1) + core) * tokens, 0).astype(F32)
            weight = jnp.where(other < pair, jnp.exp(-decay_ref[:, lanes] * gap), 0.0)
            got = got_ref[pl.ds(0, modes), lanes]
            state = state + weight * got
            moment = moment + weight * (got_ref[pl.ds(modes, modes), lanes] + gap * got)
        for seg, (start, rows) in enumerate(segments):
            steps = rows // BLOCKS
            power = jnp.exp(-decay_ref[:, lanes] * steps)
            for b in range(BLOCKS):
                rowsb = pl.ds(b * modes, modes)
                hin_ref[lane, seg, rowsb, :] = state
                kin_ref[lane, seg, rowsb, :] = moment
                moment = power * (moment + steps * state) + a * eb_ref[lane, seg, rowsb, :]
                state = power * state + hb_ref[lane, seg, rowsb, :]
        for seg, (start, rows) in enumerate(segments):
            steps = rows // BLOCKS
            for part in range(2):
                decays = [spread(a_ref, part * half + m, lanes) for m in range(half)]
                weights = [spread(r_ref, part * half + m, lanes) for m in range(half)]

                def body(outer, h):
                    h = list(h)
                    for q in range(unroll):
                        i = outer * unroll + q
                        here = pl.ds(pl.multiple_of(start + i * BLOCKS, BLOCKS), BLOCKS)
                        x = xperm_ref[lane, here, :]
                        y = None
                        for m in range(half):
                            h[m] = decays[m] * h[m] + x
                            store_ref[lane, part * half + m, here, :] = h[m]
                            term = weights[m] * h[m]
                            y = term if y is None else y + term
                        if part == 0:
                            yloc[here, :] = y
                        else:
                            y = y + yloc[here, :]
                            resp_ref[lane, pl.ds(start + i, BLOCKS, stride=steps), :] = y
                    return tuple(h)

                begin = tuple(
                    hin_ref[lane, seg, pl.ds(part * half + m, BLOCKS, stride=modes), :]
                    for m in range(half))
                lax.fori_loop(0, steps // unroll, body, begin)


def adjoint_body(segment, modes, received, has_previous, kept_ref, *refs):
    seg, start, rows = segment
    recv_refs = refs[:received]
    refs = refs[received + has_previous:]
    x1_ref, resp_ref, store_ref, hin_ref, kin_ref, a_ref, grad_ref = refs[:7]
    uperm, gb_ref, sums_ref, nat, rb, qb, grad_here, sem = refs[-8:]
    steps = rows // BLOCKS
    channels = x1_ref.shape[1]
    unroll = 4
    half = modes // 2
    window = pl.ds(start, rows)
    for lane in range(channels // LANES):
        lanes = pl.ds(lane * LANES, LANES)

        def own(ref):
            return ref[:, pl.ds(ref.shape[1] - channels + lane * LANES, LANES)]

        grad_in = own(kept_ref).astype(F32)
        for recv_ref in recv_refs:
            grad_in = grad_in + own(recv_ref).astype(F32)
        grad_here[:, lanes] = (grad_in * resp_ref[lane, window, :]).astype(BF16)
        nat[lane] = (grad_in * x1_ref[window, lanes].astype(F32)).astype(BF16).astype(F32)
    copy = pltpu.make_async_copy(grad_here, grad_ref.at[window, :], sem)
    copy.start()
    for lane in range(channels // LANES):
        lanes = pl.ds(lane * LANES, LANES)
        for part in range(2):
            decays = [spread(a_ref, part * half + m, lanes) for m in range(half)]

            def body(outer, carry):
                g, racc, qacc = (list(item) for item in carry)
                for q in range(unroll):
                    i = steps - 1 - (outer * unroll + q)
                    here = pl.ds(pl.multiple_of(i * BLOCKS, BLOCKS), BLOCKS)
                    if part == 0:
                        u = nat[lane, pl.ds(i, BLOCKS, stride=steps), :]
                        uperm[lane, here, :] = u
                    else:
                        u = uperm[lane, here, :]
                    there = pl.ds(pl.multiple_of(start + i * BLOCKS, BLOCKS), BLOCKS)
                    for m in range(half):
                        h = store_ref[lane, part * half + m, there, :]
                        g[m] = decays[m] * g[m] + u
                        racc[m] = racc[m] + u * h
                        qacc[m] = qacc[m] + g[m] * h
                return tuple(g), tuple(racc), tuple(qacc)

            zero = (jnp.zeros((BLOCKS, LANES), F32),) * half
            g, racc, qacc = lax.fori_loop(0, steps // unroll, body, (zero,) * 3)
            for m in range(half):
                row = pl.ds(part * half + m, BLOCKS, stride=modes)
                gb_ref[lane, row, :] = g[m]
                rb[row, :] = racc[m]
                qb[row, :] = qacc[m]
        a = a_ref[:, lanes]
        total = jnp.zeros((modes, LANES), F32)
        moment = jnp.zeros((modes, LANES), F32)
        for b in range(BLOCKS):
            rowsb = pl.ds(b * modes, modes)
            before = hin_ref[lane, seg, rowsb, :] + kin_ref[lane, seg, rowsb, :]
            total = total + rb[rowsb, :]
            moment = moment + qb[rowsb, :] - rb[rowsb, :] + a * gb_ref[lane, rowsb, :] * before
        sums_ref[pl.ds(0, modes), lanes] = total
        sums_ref[pl.ds(modes, modes), lanes] = moment
    copy.wait()


def local_body(segments, modes, seg, uperm_ref, *refs):
    count = len(segments)
    gb_refs = refs[:count - seg]
    a_ref, r_ref, decay_ref, aloc_ref, gin = refs[count - seg:]
    channels = a_ref.shape[1]
    unroll = 4
    half = modes // 2
    for lane in range(channels // LANES):
        lanes = pl.ds(lane * LANES, LANES)
        state = jnp.zeros((modes, LANES), F32)
        for other in reversed(range(seg, count)):
            steps = segments[other][1] // BLOCKS
            power = jnp.exp(-decay_ref[:, lanes] * steps)
            for b in reversed(range(BLOCKS)):
                rowsb = pl.ds(b * modes, modes)
                if other == seg:
                    gin[rowsb, :] = state
                state = power * state + gb_refs[other - seg][lane, rowsb, :]
        for part in range(2):
            decays = [spread(a_ref, part * half + m, lanes) for m in range(half)]
            weights = [spread(r_ref, part * half + m, lanes) for m in range(half)]

            def body(outer, g):
                g = list(g)
                for q in range(unroll):
                    i = steps - 1 - (outer * unroll + q)
                    here = pl.ds(pl.multiple_of(i * BLOCKS, BLOCKS), BLOCKS)
                    u = uperm_ref[lane, here, :]
                    y = None if part == 0 else aloc_ref[lane, here, :]
                    for m in range(half):
                        g[m] = decays[m] * g[m] + u
                        term = weights[m] * g[m]
                        y = term if y is None else y + term
                    aloc_ref[lane, here, :] = y
                return tuple(g)

            begin = tuple(gin[pl.ds(part * half + m, BLOCKS, stride=modes), :] for m in range(half))
            lax.fori_loop(0, steps // unroll, body, begin)


def gather_body(segments, modes, *refs):
    count = len(segments)
    gb_refs, sums_refs = refs[:count], refs[count:2 * count]
    scale_ref, decay_ref, out_ref = refs[2 * count:]
    channels = decay_ref.shape[1]
    for lane in range(channels // LANES):
        lanes = pl.ds(lane * LANES, LANES)
        state = jnp.zeros((modes, LANES), F32)
        for seg in reversed(range(count)):
            power = jnp.exp(-decay_ref[:, lanes] * (segments[seg][1] // BLOCKS))
            for b in reversed(range(BLOCKS)):
                state = power * state + gb_refs[seg][lane, pl.ds(b * modes, modes), :]
        out_ref[pl.ds(0, modes), lanes] = state
    sums = sum(ref[...] for ref in sums_refs)
    out_ref[pl.ds(modes, modes), :] = sums[:modes]
    out_ref[pl.ds(2 * modes, modes), :] = sums[modes:] * scale_ref[...]


def three_parts(values):
    parts = []
    for _ in range(3):
        parts.append(values.astype(BF16))
        values = values - parts[-1].astype(F32)
    return parts


def pick(values, chosen, dims):
    return sum(
        lax.dot_general(part, chosen, dims, preferred_element_type=F32)
        for part in three_parts(values)
    )


def backward_pair_body(modes, tokens, owned, message_ref, partner_ref, decay_ref, both_ref):
    _, core = place()
    channels = decay_ref.shape[1]
    state, sums = pl.ds(0, modes), pl.ds(modes, 2 * modes)
    first = jnp.where(core == 0, message_ref[state, :], partner_ref[state, :])
    second = jnp.where(core == 0, partner_ref[state, :], message_ref[state, :])
    both_ref[state, :] = first + jnp.exp(-decay_ref[...] * tokens) * second
    channel = lax.broadcasted_iota(jnp.int32, (channels, LANES), 0)
    lane = lax.broadcasted_iota(jnp.int32, (channels, LANES), 1)
    wanted = (2 * (lane // owned) + core) * owned + lane % owned
    picked = pick(message_ref[sums, :] + partner_ref[sums, :], (channel == wanted).astype(BF16),
                  (((1,), (0,)), ((), ())))
    tiles = channels // LANES
    rows = 2 * modes // tiles
    for tile in range(tiles):
        both_ref[pl.ds(modes, rows), pl.ds(tile * LANES, LANES)] = picked[tile * rows:(tile + 1) * rows]


def finish_body(segments, modes, tokens, length, pairs, *refs):
    count = len(segments)
    aloc_refs = refs[:count]
    a_ref, r_ref, decay_ref, x2_ref, v_ref, partner_ref, both_ref = refs[count:count + 7]
    got_refs = refs[count + 7:count + 6 + pairs]
    gx2_ref, gv_ref, rgrad_ref, dgrad_ref, gin, nat, gx2_here, gv_here, r_here, d_here, sems = refs[-11:]
    channels = a_ref.shape[1]
    unroll = 4
    pair, core = place()
    states = []
    for lane in range(channels // LANES):
        lanes = pl.ds(lane * LANES, LANES)
        state = jnp.where(core == 0, partner_ref[pl.ds(0, modes), lanes], 0.0)
        for step, got_ref in enumerate(got_refs, 1):
            other = pair ^ step
            gap = jnp.maximum((2 * (other - pair - 1) + 1 - core) * tokens, 0).astype(F32)
            weight = jnp.where(other > pair, jnp.exp(-decay_ref[:, lanes] * gap), 0.0)
            state = state + weight * got_ref[pl.ds(0, modes), lanes]
        states.append(state)
    copies = []
    owned = rgrad_ref.shape[1]
    tiles = channels // LANES
    lower = pl.ds(modes, 2 * modes // tiles)
    sums = both_ref[lower, :]
    for got_ref in got_refs:
        sums = sums + got_ref[lower, :]
    row = lax.broadcasted_iota(jnp.int32, (owned, LANES), 0)
    column = lax.broadcasted_iota(jnp.int32, (owned, LANES), 1)
    chosen = (column == pair * owned + row).astype(BF16)

    def choose(values):
        return sum(
            lax.dot_general(part, chosen, CONTRACT_LAST, preferred_element_type=F32)
            for part in three_parts(values)
        )

    if tiles == 1:
        residue_sums, decay_sums = sums[:modes], sums[modes:]
    else:
        residue_sums, decay_sums = sums[:, :LANES], sums[:, LANES:]
    r_here[...] = choose(residue_sums) / length
    d_here[...] = choose(decay_sums) / length
    for j, (here, there) in enumerate(((r_here, rgrad_ref), (d_here, dgrad_ref))):
        copy = pltpu.make_async_copy(here, there, sems.at[count, j])
        copy.start()
        copies.append(copy)
    for seg in reversed(range(count)):
        start, rows = segments[seg]
        steps = rows // BLOCKS
        window = pl.ds(start, rows)
        for lane in range(channels // LANES):
            lanes = pl.ds(lane * LANES, LANES)
            decays = [spread(a_ref, m, lanes) for m in range(modes)]
            state = states[lane]
            power = jnp.exp(-decay_ref[:, lanes] * steps)
            for b in reversed(range(BLOCKS)):
                rowsb = pl.ds(b * modes, modes)
                gin[rowsb, :] = state
                state = power * state
            states[lane] = state
            edge = tuple(
                spread(r_ref, m, lanes) * decays[m] * gin[pl.ds(m, BLOCKS, stride=modes), :]
                for m in range(modes)
            )

            def body(outer, edge):
                edge = list(edge)
                for q in range(unroll):
                    i = steps - 1 - (outer * unroll + q)
                    here = pl.ds(pl.multiple_of(i * BLOCKS, BLOCKS), BLOCKS)
                    y = aloc_refs[seg][lane, here, :]
                    for m in range(modes):
                        y = y + edge[m]
                        edge[m] = edge[m] * decays[m]
                    nat[lane, pl.ds(start + i, BLOCKS, stride=steps), :] = y
                return tuple(edge)

            lax.fori_loop(0, steps // unroll, body, edge)
            adjoint = nat[lane, window, :]
            gx2_here[window, lanes] = (adjoint * v_ref[window, lanes].astype(F32)).astype(BF16)
            gv_here[window, lanes] = (adjoint * x2_ref[window, lanes].astype(F32)).astype(BF16)
        for j, (here, there) in enumerate(((gx2_here, gx2_ref), (gv_here, gv_ref))):
            copy = pltpu.make_async_copy(here.at[window, :], there.at[window, :], sems.at[seg, j])
            copy.start()
            copies.append(copy)
    for copy in copies:
        copy.wait()


def on_device(g_out, w_out, gate_x1, gate_x2, value_v, residue, decay):
    tokens, channels = gate_x1.shape
    context_size = lax.axis_size("ctx")
    ch_size = lax.axis_size("ch")
    length = tokens * context_size
    modes = residue.shape[1]
    lane_tiles = channels // LANES
    owned = channels // context_size

    bits = [1 << bit for bit in range(ch_size.bit_length() - 1)]
    half_rows = tokens // 2
    chunks = [(0, half_rows, bits), (half_rows, half_rows, bits[::-1])]
    segments = [(start, rows) for start, rows, _ in chunks]
    count = len(chunks)
    layouts = [halving_layout(order) for _, _, order in chunks]
    cut = ch_size // 2

    rows_of = [(start, rows) for start, rows, _ in chunks]
    projected = project(
        g_out, w_out, [(*where, layout[:cut]) for where, layout in zip(rows_of, layouts)], channels)
    sent = [lax.ppermute(piece, "ch", xor_pairs(ch_size, order[0]))
            for piece, (_, _, order) in zip(projected, chunks)]
    kept = project_kept(
        g_out, w_out, [(*where, layout[cut:]) for where, layout in zip(rows_of, layouts)], channels)

    decay_t = decay.T
    residue_t = residue.T
    a = jnp.exp(-decay_t)
    r = residue_t * length ** (-0.5)
    scale = -residue_t * decay_t

    state_shape = jax.ShapeDtypeStruct((lane_tiles, count, BLOCKS * modes, LANES), F32)
    perm_shape = jax.ShapeDtypeStruct((lane_tiles, tokens, LANES), F32)
    work = tokens * channels * modes
    xperm, hb, eb, total = pl.pallas_call(
        functools.partial(forward_body, segments, modes),
        out_shape=[perm_shape, state_shape, state_shape,
                   jax.ShapeDtypeStruct((2 * modes, channels), F32)],
        scratch_shapes=[pltpu.VMEM((lane_tiles, tokens, LANES), F32)],
        compiler_params=params(),
        cost_estimate=cost(3.7),
        name="forward",
    )(gate_x2, value_v, a, decay_t)

    pairs = context_size // 2
    partner = lax.ppermute(total, "ctx", xor_pairs(context_size, 1))
    both = pl.pallas_call(
        functools.partial(forward_pair_body, modes, tokens),
        out_shape=jax.ShapeDtypeStruct((2 * modes, channels), F32),
        compiler_params=params(),
        name="forward_pair",
    )(total, partner, decay_t)
    got = [lax.ppermute(both, "ctx", xor_pairs(context_size, 2 * step)) for step in range(1, pairs)]

    uperms, gbs, sums = [], [], []
    arrived = [[piece] for piece in sent]
    away = both
    for level in range(1, len(bits)):
        for which, (_, _, order) in enumerate(chunks):
            arrived[which][-1], _ = lax.optimization_barrier((arrived[which][-1], away))
            stop = cut >> level
            width = kept[which].shape[1]
            left = width - 2 * stop * channels
            away = kept[which][:, left:left + stop * channels].astype(F32)
            for piece in arrived[which]:
                left = piece.shape[1] - 2 * stop * channels
                away = away + piece[:, left:left + stop * channels].astype(F32)
            away = away.astype(BF16)
            hb, away = lax.optimization_barrier((hb, away))
            arrived[which].append(lax.ppermute(away, "ch", xor_pairs(ch_size, order[level])))
    store_shape = jax.ShapeDtypeStruct((lane_tiles, modes, tokens, LANES), F32)
    resp, store, hin, kin = pl.pallas_call(
        functools.partial(respond_body, segments, modes, tokens),
        out_shape=[perm_shape, store_shape, state_shape, state_shape],
        scratch_shapes=[pltpu.VMEM((tokens, LANES), F32)],
        compiler_params=params(),
        cost_estimate=cost(3.5),
        name="respond",
    )(hb, eb, xperm, a, r, decay_t, partner, *got)

    previous = []
    for seg, (start, rows) in enumerate(segments):
        block_shape = jax.ShapeDtypeStruct((lane_tiles, BLOCKS * modes, LANES), F32)
        pieces = arrived[seg]
        *buffers, uperm, gb, partial_sums = pl.pallas_call(
            functools.partial(adjoint_body, (seg, start, rows), modes, len(pieces), len(previous)),
            in_specs=in_vmem(1 + len(pieces)) + [pl.BlockSpec(memory_space=HBM)] * len(previous) + in_vmem(6),
            out_specs=[pl.BlockSpec(memory_space=HBM)] * 3 + in_vmem(3),
            out_shape=[jax.ShapeDtypeStruct((tokens, channels), BF16)] * 3
            + [
                       jax.ShapeDtypeStruct((lane_tiles, rows, LANES), F32),
                       block_shape,
                       jax.ShapeDtypeStruct((2 * modes, channels), F32)],
            scratch_shapes=[pltpu.VMEM((lane_tiles, rows, LANES), F32)]
            + [pltpu.VMEM((BLOCKS * modes, LANES), F32)] * 2
            + [pltpu.VMEM((rows, channels), BF16), pltpu.SemaphoreType.DMA(())],
            input_output_aliases={1 + len(pieces) + j: j for j in range(len(previous))},
            compiler_params=params(),
            cost_estimate=cost(2.7 * rows / 512),
            name="adjoint",
        )(kept[seg], *pieces, *previous, gate_x1, resp, store, hin, kin, a)
        previous = buffers
        uperms.append(uperm)
        gbs.append(gb)
        sums.append(partial_sums)

    message = pl.pallas_call(
        functools.partial(gather_body, segments, modes),
        out_shape=jax.ShapeDtypeStruct((3 * modes, channels), F32),
        compiler_params=params(),
        name="totals",
    )(*gbs, *sums, scale, decay_t)
    partner = lax.ppermute(message, "ctx", xor_pairs(context_size, 1))
    both = pl.pallas_call(
        functools.partial(backward_pair_body, modes, tokens, owned),
        out_shape=jax.ShapeDtypeStruct((modes + 2 * modes // lane_tiles, channels), F32),
        compiler_params=params(),
        name="backward_pair",
    )(message, partner, decay_t)
    got = [lax.ppermute(both, "ctx", xor_pairs(context_size, 2 * step)) for step in range(1, pairs)]
    *uperms, _ = lax.optimization_barrier((*uperms, both))
    alocs = [
        pl.pallas_call(
            functools.partial(local_body, segments, modes, seg),
            out_shape=jax.ShapeDtypeStruct((lane_tiles, rows, LANES), F32),
            scratch_shapes=[pltpu.VMEM((BLOCKS * modes, LANES), F32)],
            compiler_params=params(),
            cost_estimate=cost(1.8 * rows / 512),
            name="local_adjoint",
        )(uperms[seg], *gbs[seg:], a, r, decay_t)
        for seg, (_, rows) in enumerate(segments)
    ]

    grad_x2, grad_v, residue_grad, decay_grad = pl.pallas_call(
        functools.partial(finish_body, segments, modes, tokens, length, pairs),
        in_specs=in_vmem(count + 6 + pairs) + [pl.BlockSpec(memory_space=HBM)] * 2,
        out_specs=[pl.BlockSpec(memory_space=HBM)] * 4,
        out_shape=[jax.ShapeDtypeStruct((tokens, channels), BF16)] * 2
        + [jax.ShapeDtypeStruct((modes, owned), F32)] * 2,
        scratch_shapes=[pltpu.VMEM((BLOCKS * modes, LANES), F32),
                        pltpu.VMEM((lane_tiles, tokens, LANES), F32),
                        pltpu.VMEM((tokens, channels), BF16),
                        pltpu.VMEM((tokens, channels), BF16),
                        pltpu.VMEM((modes, owned), F32),
                        pltpu.VMEM((modes, owned), F32),
                        pltpu.SemaphoreType.DMA((count + 1, 2))],
        input_output_aliases={count + 6 + pairs: 0, count + 7 + pairs: 1},
        compiler_params=params(),
        cost_estimate=cost(3.4),
        name="finish",
    )(*alocs, a, r, decay_t, gate_x2, value_v, partner, both, *got, *previous[1:])
    return previous[0], grad_x2, grad_v, residue_grad.T, decay_grad.T


def solution(mesh):
    return jax.shard_map(
        on_device,
        mesh=mesh,
        in_specs=(
            P("ctx", "ch"),
            P(None, "ch"),
            P("ctx", "ch"),
            P("ctx", "ch"),
            P("ctx", "ch"),
            P("ch", None),
            P("ch", None),
        ),
        out_specs=(
            P("ctx", "ch"),
            P("ctx", "ch"),
            P("ctx", "ch"),
            P(("ch", "ctx"), None),
            P(("ch", "ctx"), None),
        ),
        check_vma=False,
    )
```

```python
import functools

import jax
import jax.numpy as jnp
from jax import lax
from jax.experimental import pallas as pl
from jax.experimental.pallas import tpu as pltpu
from jax.sharding import PartitionSpec as P

LANES = 128
PIECES = 2
FPARTS = 2
KEPT = jnp.bfloat16
BLOCKS = 8
F32 = jnp.float32
BF16 = jnp.bfloat16


def halving_layout(order):
    if not order:
        return [0]
    rest = halving_layout(order[1:])
    return [offset ^ order[0] for offset in rest] + rest


def xor_pairs(count, step):
    return [(index, index ^ step) for index in range(count)]


HBM = pltpu.MemorySpace.HBM
VMEM = pltpu.MemorySpace.VMEM
CONTRACT_LAST = (((1,), (1,)), ((), ()))


def params(mebibytes=24):
    return pltpu.CompilerParams(vmem_limit_bytes=mebibytes * 2**20)


def cost(microseconds):
    return pl.CostEstimate(flops=int(microseconds * 1.1e9), bytes_accessed=0, transcendentals=0)


def in_vmem(count):
    return [pl.BlockSpec(memory_space=VMEM)] * count


def block_rows(offset, width):
    block = lax.axis_index("ch") ^ offset
    return pl.ds(pl.multiple_of(block * width, width), width)


def arrange(count):
    return [1, 3, 2, 0] if count == 4 else list(range(count))


def block_runs(offsets, arranged):
    places = sorted((arranged.index(offset), spot) for spot, offset in enumerate(offsets))
    runs = []
    for where, spot in places:
        if runs and runs[-1][1] + len(runs[-1][0]) == where:
            runs[-1][0].append(spot)
        else:
            runs.append(([spot], where))
    return runs


def project_body(work, width, pieces, g_ref, w_ref, *refs):
    count = len(work)
    out_refs = refs[:count]
    out_here = refs[count:2 * count]
    g_here, w_here, total, g_sems, w_sems, out_sems = refs[2 * count:]
    depth = g_ref.shape[1] // pieces
    arranged = arrange(w_ref.shape[0] // width)
    pending = {}

    def g_copy(rows, piece):
        columns = pl.ds(piece * depth, depth)
        return pltpu.make_async_copy(
            g_ref.at[rows, columns], g_here.at[rows, columns], g_sems.at[rows.start // rows.size, piece])

    def w_copy(offset, piece):
        columns = pl.ds(piece * depth, depth)
        there = pl.ds(arranged.index(offset) * width, width)
        return pltpu.make_async_copy(
            w_ref.at[block_rows(offset, width), columns], w_here.at[there, columns],
            w_sems.at[offset, piece])

    for start, rows, offsets in work:
        for piece in range(pieces):
            for key, copy in [((start, piece), lambda: g_copy(pl.ds(start, rows), piece))] + [
                    ((-1 - offset, piece), functools.partial(w_copy, offset, piece)) for offset in offsets]:
                if key not in pending:
                    pending[key] = copy()
                    pending[key].start()
    leaving = []
    for which, (start, rows, offsets) in enumerate(work):
        out_ref = out_here[which]
        for piece in range(pieces):
            columns = pl.ds(piece * depth, depth)
            for key in [(start, piece)] + [(-1 - offset, piece) for offset in offsets]:
                copy = pending.pop(key, None)
                if copy is not None:
                    copy.wait()
            for spots, where in block_runs(offsets, arranged):
                product = lax.dot_general(
                    g_here[pl.ds(start, rows), columns],
                    w_here[pl.ds(where * width, len(spots) * width), columns],
                    CONTRACT_LAST, preferred_element_type=F32)
                for k, spot in enumerate(spots):
                    here = pl.ds(spot * width, width)
                    value = product[:, k * width:(k + 1) * width]
                    if piece > 0:
                        value = value + total[:, here]
                    if piece < pieces - 1:
                        total[:, here] = value
                    else:
                        out_ref[:, here] = value.astype(out_ref.dtype)
        leaving.append(pltpu.make_async_copy(out_ref, out_refs[which], out_sems.at[which]))
        leaving[-1].start()
    for copy in leaving:
        copy.wait()


def project(g_out, w_out, work, width):
    blocks = w_out.shape[0] // width
    pieces = PIECES
    shapes = [jax.ShapeDtypeStruct((rows, len(offsets) * width), BF16) for _, rows, offsets in work]
    groups = g_out.shape[0] // work[0][1]
    return pl.pallas_call(
        functools.partial(project_body, work, width, pieces),
        in_specs=[pl.BlockSpec(memory_space=HBM)] * 2,
        out_specs=[pl.BlockSpec(memory_space=HBM)] * len(work),
        out_shape=shapes,
        scratch_shapes=[pltpu.VMEM(shape.shape, BF16) for shape in shapes] + [
            pltpu.VMEM(g_out.shape, BF16),
            pltpu.VMEM(w_out.shape, BF16),
            pltpu.VMEM(shapes[0].shape, F32),
            pltpu.SemaphoreType.DMA((groups, pieces)),
            pltpu.SemaphoreType.DMA((blocks, pieces)),
            pltpu.SemaphoreType.DMA((len(work),)),
        ],
        compiler_params=params(60),
        cost_estimate=cost(5),
        name="project",
    )(g_out, w_out)


def project_kept_body(work, width, g_ref, w_ref, *out_refs):
    for (start, rows, offsets), out_ref in zip(work, out_refs):
        for spot, offset in enumerate(offsets):
            out_ref[:, pl.ds(spot * width, width)] = lax.dot_general(
                g_ref[pl.ds(start, rows), :], w_ref[block_rows(offset, width), :],
                CONTRACT_LAST, preferred_element_type=F32).astype(out_ref.dtype)


def project_kept(g_out, w_out, work, width):
    return pl.pallas_call(
        functools.partial(project_kept_body, work, width),
        in_specs=in_vmem(2),
        out_specs=in_vmem(len(work)),
        out_shape=[jax.ShapeDtypeStruct((rows, len(offsets) * width), KEPT)
                   for _, rows, offsets in work],
        compiler_params=params(),
        cost_estimate=cost(3),
        name="project_kept",
    )(g_out, w_out)


def tree_sum(terms):
    terms = list(terms)
    while len(terms) > 1:
        terms = [sum(terms[i:i + 2][1:], terms[i]) for i in range(0, len(terms), 2)]
    return terms[0]


def spread(ref, row, lanes):
    return jnp.broadcast_to(ref[pl.ds(row, 1), lanes], (BLOCKS, LANES))


def forward_body(segments, modes, x2_ref, v_ref, a_ref, decay_ref,
                 xperm_ref, hb_ref, eb_ref, total_ref, nat):
    channels = x2_ref.shape[1]
    unroll = 16
    group = modes // FPARTS
    for lane in range(channels // LANES):
        lanes = pl.ds(lane * LANES, LANES)
        mixed = (x2_ref[:, lanes].astype(F32) * v_ref[:, lanes].astype(F32)).astype(BF16)
        nat[lane] = mixed.astype(F32)
        for seg, (start, rows) in enumerate(segments):
            steps = rows // BLOCKS
            for part in range(FPARTS):
                decays = [spread(a_ref, part * group + m, lanes) for m in range(group)]

                def body(outer, carry):
                    h, e = list(carry[0]), list(carry[1])
                    for q in range(unroll):
                        i = outer * unroll + q
                        here = pl.ds(pl.multiple_of(start + i * BLOCKS, BLOCKS), BLOCKS)
                        if part == 0:
                            x = nat[lane, pl.ds(start + i, BLOCKS, stride=steps), :]
                            xperm_ref[lane, here, :] = x
                        else:
                            x = xperm_ref[lane, here, :]
                        for m in range(group):
                            e[m] = decays[m] * e[m] + h[m]
                            h[m] = decays[m] * h[m] + x
                    return tuple(h), tuple(e)

                zero = (jnp.zeros((BLOCKS, LANES), F32),) * group
                h, e = lax.fori_loop(0, steps // unroll, body, (zero, zero))
                for m in range(group):
                    row = pl.ds(part * group + m, BLOCKS, stride=modes)
                    hb_ref[lane, seg, row, :] = h[m]
                    eb_ref[lane, seg, row, :] = e[m]
        a = a_ref[:, lanes]
        state = jnp.zeros((modes, LANES), F32)
        moment = jnp.zeros((modes, LANES), F32)
        for seg, (start, rows) in enumerate(segments):
            steps = rows // BLOCKS
            power = jnp.exp(-decay_ref[:, lanes] * steps)
            for b in range(BLOCKS):
                rowsb = pl.ds(b * modes, modes)
                moment = power * (moment + steps * state) + a * eb_ref[lane, seg, rowsb, :]
                state = power * state + hb_ref[lane, seg, rowsb, :]
        total_ref[pl.ds(0, modes), lanes] = state
        total_ref[pl.ds(modes, modes), lanes] = moment


def place():
    index = lax.axis_index("ctx")
    return index // 2, index % 2


def forward_pair_body(modes, tokens, total_ref, partner_ref, decay_ref, both_ref):
    _, core = place()
    state, moment = pl.ds(0, modes), pl.ds(modes, modes)
    power = jnp.exp(-decay_ref[...] * tokens)
    later = core == 1
    first_h = jnp.where(later, partner_ref[state, :], total_ref[state, :])
    first_k = jnp.where(later, partner_ref[moment, :], total_ref[moment, :])
    second_h = jnp.where(later, total_ref[state, :], partner_ref[state, :])
    second_k = jnp.where(later, total_ref[moment, :], partner_ref[moment, :])
    both_ref[state, :] = second_h + power * first_h
    both_ref[moment, :] = second_k + power * (first_k + tokens * first_h)


def respond_body(segments, modes, tokens, hb_ref, eb_ref, xperm_ref, a_ref, r_ref, decay_ref, partner_ref, *refs):
    got_refs, (resp_ref, store_ref, hin_ref, kin_ref, yloc) = refs[:-5], refs[-5:]
    half = modes // 2
    pair, core = place()
    channels = a_ref.shape[1]
    unroll = 16
    for lane in range(channels // LANES):
        lanes = pl.ds(lane * LANES, LANES)
        a = a_ref[:, lanes]
        state = jnp.where(core == 1, partner_ref[pl.ds(0, modes), lanes], 0.0)
        moment = jnp.where(core == 1, partner_ref[pl.ds(modes, modes), lanes], 0.0)
        for step, got_ref in enumerate(got_refs, 1):
            other = pair ^ step
            gap = jnp.maximum((2 * (pair - other - 1) + core) * tokens, 0).astype(F32)
            weight = jnp.where(other < pair, jnp.exp(-decay_ref[:, lanes] * gap), 0.0)
            got = got_ref[pl.ds(0, modes), lanes]
            state = state + weight * got
            moment = moment + weight * (got_ref[pl.ds(modes, modes), lanes] + gap * got)
        for seg, (start, rows) in enumerate(segments):
            steps = rows // BLOCKS
            power = jnp.exp(-decay_ref[:, lanes] * steps)
            for b in range(BLOCKS):
                rowsb = pl.ds(b * modes, modes)
                hin_ref[lane, seg, rowsb, :] = state
                kin_ref[lane, seg, rowsb, :] = moment
                moment = power * (moment + steps * state) + a * eb_ref[lane, seg, rowsb, :]
                state = power * state + hb_ref[lane, seg, rowsb, :]
        for seg, (start, rows) in enumerate(segments):
            steps = rows // BLOCKS
            for part in range(2):
                decays = [spread(a_ref, part * half + m, lanes) for m in range(half)]
                weights = [spread(r_ref, part * half + m, lanes) for m in range(half)]

                def body(outer, h):
                    h = list(h)
                    for q in range(unroll):
                        i = outer * unroll + q
                        here = pl.ds(pl.multiple_of(start + i * BLOCKS, BLOCKS), BLOCKS)
                        x = xperm_ref[lane, here, :]
                        for m in range(half):
                            h[m] = decays[m] * h[m] + x
                            store_ref[lane, part * half + m, here, :] = h[m]
                        y = tree_sum(weights[m] * h[m] for m in range(half))
                        if part == 0:
                            yloc[here, :] = y
                        else:
                            y = y + yloc[here, :]
                            resp_ref[lane, pl.ds(start + i, BLOCKS, stride=steps), :] = y
                    return tuple(h)

                begin = tuple(
                    hin_ref[lane, seg, pl.ds(part * half + m, BLOCKS, stride=modes), :]
                    for m in range(half))
                lax.fori_loop(0, steps // unroll, body, begin)


def adjoint_body(segment, modes, received, has_previous, kept_ref, *refs):
    seg, start, rows = segment
    recv_refs = refs[:received]
    refs = refs[received + has_previous:]
    x1_ref, resp_ref, store_ref, hin_ref, kin_ref, a_ref, grad_ref = refs[:7]
    uperm, gb_ref, sums_ref, nat, rb, qb, grad_here, sem = refs[-8:]
    steps = rows // BLOCKS
    channels = x1_ref.shape[1]
    unroll = 16
    half = modes // 2
    window = pl.ds(start, rows)
    for lane in range(channels // LANES):
        lanes = pl.ds(lane * LANES, LANES)

        def own(ref):
            return ref[:, pl.ds(ref.shape[1] - channels + lane * LANES, LANES)]

        grad_in = own(kept_ref).astype(F32)
        for recv_ref in recv_refs:
            grad_in = grad_in + own(recv_ref).astype(F32)
        grad_here[:, lanes] = (grad_in * resp_ref[lane, window, :]).astype(BF16)
        nat[lane] = (grad_in * x1_ref[window, lanes].astype(F32)).astype(BF16).astype(F32)
    copy = pltpu.make_async_copy(grad_here, grad_ref.at[window, :], sem)
    copy.start()
    for lane in range(channels // LANES):
        lanes = pl.ds(lane * LANES, LANES)
        for part in range(2):
            decays = [spread(a_ref, part * half + m, lanes) for m in range(half)]

            def body(outer, carry):
                g, racc, qacc = (list(item) for item in carry)
                for q in range(unroll):
                    i = steps - 1 - (outer * unroll + q)
                    here = pl.ds(pl.multiple_of(i * BLOCKS, BLOCKS), BLOCKS)
                    if part == 0:
                        u = nat[lane, pl.ds(i, BLOCKS, stride=steps), :]
                        uperm[lane, here, :] = u
                    else:
                        u = uperm[lane, here, :]
                    there = pl.ds(pl.multiple_of(start + i * BLOCKS, BLOCKS), BLOCKS)
                    for m in range(half):
                        h = store_ref[lane, part * half + m, there, :]
                        g[m] = decays[m] * g[m] + u
                        racc[m] = racc[m] + u * h
                        qacc[m] = qacc[m] + g[m] * h
                return tuple(g), tuple(racc), tuple(qacc)

            zero = (jnp.zeros((BLOCKS, LANES), F32),) * half
            g, racc, qacc = lax.fori_loop(0, steps // unroll, body, (zero,) * 3)
            for m in range(half):
                row = pl.ds(part * half + m, BLOCKS, stride=modes)
                gb_ref[lane, row, :] = g[m]
                rb[row, :] = racc[m]
                qb[row, :] = qacc[m]
        a = a_ref[:, lanes]
        total = jnp.zeros((modes, LANES), F32)
        moment = jnp.zeros((modes, LANES), F32)
        for b in range(BLOCKS):
            rowsb = pl.ds(b * modes, modes)
            before = hin_ref[lane, seg, rowsb, :] + kin_ref[lane, seg, rowsb, :]
            total = total + rb[rowsb, :]
            moment = moment + qb[rowsb, :] - rb[rowsb, :] + a * gb_ref[lane, rowsb, :] * before
        sums_ref[pl.ds(0, modes), lanes] = total
        sums_ref[pl.ds(modes, modes), lanes] = moment
    copy.wait()


def local_body(segments, modes, seg, uperm_ref, *refs):
    count = len(segments)
    gb_refs = refs[:count - seg]
    a_ref, r_ref, decay_ref, aloc_ref, gin = refs[count - seg:]
    channels = a_ref.shape[1]
    unroll = 16
    half = modes // 2
    for lane in range(channels // LANES):
        lanes = pl.ds(lane * LANES, LANES)
        state = jnp.zeros((modes, LANES), F32)
        for other in reversed(range(seg, count)):
            steps = segments[other][1] // BLOCKS
            power = jnp.exp(-decay_ref[:, lanes] * steps)
            for b in reversed(range(BLOCKS)):
                rowsb = pl.ds(b * modes, modes)
                if other == seg:
                    gin[rowsb, :] = state
                state = power * state + gb_refs[other - seg][lane, rowsb, :]
        for part in range(2):
            decays = [spread(a_ref, part * half + m, lanes) for m in range(half)]
            weights = [spread(r_ref, part * half + m, lanes) for m in range(half)]

            def body(outer, g):
                g = list(g)
                for q in range(unroll):
                    i = steps - 1 - (outer * unroll + q)
                    here = pl.ds(pl.multiple_of(i * BLOCKS, BLOCKS), BLOCKS)
                    u = uperm_ref[lane, here, :]
                    for m in range(half):
                        g[m] = decays[m] * g[m] + u
                    y = tree_sum(weights[m] * g[m] for m in range(half))
                    if part == 1:
                        y = y + aloc_ref[lane, here, :]
                    aloc_ref[lane, here, :] = y
                return tuple(g)

            begin = tuple(gin[pl.ds(part * half + m, BLOCKS, stride=modes), :] for m in range(half))
            lax.fori_loop(0, steps // unroll, body, begin)


def gather_body(segments, modes, *refs):
    count = len(segments)
    gb_refs, sums_refs = refs[:count], refs[count:2 * count]
    scale_ref, decay_ref, out_ref = refs[2 * count:]
    channels = decay_ref.shape[1]
    for lane in range(channels // LANES):
        lanes = pl.ds(lane * LANES, LANES)
        state = jnp.zeros((modes, LANES), F32)
        for seg in reversed(range(count)):
            power = jnp.exp(-decay_ref[:, lanes] * (segments[seg][1] // BLOCKS))
            for b in reversed(range(BLOCKS)):
                state = power * state + gb_refs[seg][lane, pl.ds(b * modes, modes), :]
        out_ref[pl.ds(0, modes), lanes] = state
    sums = sum(ref[...] for ref in sums_refs)
    out_ref[pl.ds(modes, modes), :] = sums[:modes]
    out_ref[pl.ds(2 * modes, modes), :] = sums[modes:] * scale_ref[...]


def three_parts(values):
    parts = []
    for _ in range(3):
        parts.append(values.astype(BF16))
        values = values - parts[-1].astype(F32)
    return parts


def pick(values, chosen, dims):
    return sum(
        lax.dot_general(part, chosen, dims, preferred_element_type=F32)
        for part in three_parts(values)
    )


def backward_pair_body(modes, tokens, owned, message_ref, partner_ref, decay_ref, both_ref):
    _, core = place()
    channels = decay_ref.shape[1]
    state, sums = pl.ds(0, modes), pl.ds(modes, 2 * modes)
    first = jnp.where(core == 0, message_ref[state, :], partner_ref[state, :])
    second = jnp.where(core == 0, partner_ref[state, :], message_ref[state, :])
    both_ref[state, :] = first + jnp.exp(-decay_ref[...] * tokens) * second
    channel = lax.broadcasted_iota(jnp.int32, (channels, LANES), 0)
    lane = lax.broadcasted_iota(jnp.int32, (channels, LANES), 1)
    wanted = (2 * (lane // owned) + core) * owned + lane % owned
    picked = pick(message_ref[sums, :] + partner_ref[sums, :], (channel == wanted).astype(BF16),
                  (((1,), (0,)), ((), ())))
    tiles = channels // LANES
    rows = 2 * modes // tiles
    for tile in range(tiles):
        both_ref[pl.ds(modes, rows), pl.ds(tile * LANES, LANES)] = picked[tile * rows:(tile + 1) * rows]


def finish_body(segments, modes, tokens, length, pairs, *refs):
    count = len(segments)
    aloc_refs = refs[:count]
    a_ref, r_ref, decay_ref, x2_ref, v_ref, partner_ref, both_ref = refs[count:count + 7]
    got_refs = refs[count + 7:count + 6 + pairs]
    gx2_ref, gv_ref, rgrad_ref, dgrad_ref, gin, nat, gx2_here, gv_here, r_here, d_here, sems = refs[-11:]
    channels = a_ref.shape[1]
    unroll = 16
    pair, core = place()
    states = []
    for lane in range(channels // LANES):
        lanes = pl.ds(lane * LANES, LANES)
        state = jnp.where(core == 0, partner_ref[pl.ds(0, modes), lanes], 0.0)
        for step, got_ref in enumerate(got_refs, 1):
            other = pair ^ step
            gap = jnp.maximum((2 * (other - pair - 1) + 1 - core) * tokens, 0).astype(F32)
            weight = jnp.where(other > pair, jnp.exp(-decay_ref[:, lanes] * gap), 0.0)
            state = state + weight * got_ref[pl.ds(0, modes), lanes]
        states.append(state)
    copies = []
    owned = rgrad_ref.shape[1]
    tiles = channels // LANES
    lower = pl.ds(modes, 2 * modes // tiles)
    sums = both_ref[lower, :]
    for got_ref in got_refs:
        sums = sums + got_ref[lower, :]
    row = lax.broadcasted_iota(jnp.int32, (owned, LANES), 0)
    column = lax.broadcasted_iota(jnp.int32, (owned, LANES), 1)
    chosen = (column == pair * owned + row).astype(BF16)

    def choose(values):
        return sum(
            lax.dot_general(part, chosen, CONTRACT_LAST, preferred_element_type=F32)
            for part in three_parts(values)
        )

    if tiles == 1:
        residue_sums, decay_sums = sums[:modes], sums[modes:]
    else:
        residue_sums, decay_sums = sums[:, :LANES], sums[:, LANES:]
    r_here[...] = choose(residue_sums) / length
    d_here[...] = choose(decay_sums) / length
    for j, (here, there) in enumerate(((r_here, rgrad_ref), (d_here, dgrad_ref))):
        copy = pltpu.make_async_copy(here, there, sems.at[count, j])
        copy.start()
        copies.append(copy)
    for seg in reversed(range(count)):
        start, rows = segments[seg]
        steps = rows // BLOCKS
        window = pl.ds(start, rows)
        for lane in range(channels // LANES):
            lanes = pl.ds(lane * LANES, LANES)
            decays = [spread(a_ref, m, lanes) for m in range(modes)]
            state = states[lane]
            power = jnp.exp(-decay_ref[:, lanes] * steps)
            for b in reversed(range(BLOCKS)):
                rowsb = pl.ds(b * modes, modes)
                gin[rowsb, :] = state
                state = power * state
            states[lane] = state
            edge = tuple(
                spread(r_ref, m, lanes) * decays[m] * gin[pl.ds(m, BLOCKS, stride=modes), :]
                for m in range(modes)
            )

            def body(outer, edge):
                edge = list(edge)
                for q in range(unroll):
                    i = steps - 1 - (outer * unroll + q)
                    here = pl.ds(pl.multiple_of(i * BLOCKS, BLOCKS), BLOCKS)
                    y = tree_sum(edge) + aloc_refs[seg][lane, here, :]
                    for m in range(modes):
                        edge[m] = edge[m] * decays[m]
                    nat[lane, pl.ds(start + i, BLOCKS, stride=steps), :] = y
                return tuple(edge)

            lax.fori_loop(0, steps // unroll, body, edge)
            adjoint = nat[lane, window, :]
            gx2_here[window, lanes] = (adjoint * v_ref[window, lanes].astype(F32)).astype(BF16)
            gv_here[window, lanes] = (adjoint * x2_ref[window, lanes].astype(F32)).astype(BF16)
        for j, (here, there) in enumerate(((gx2_here, gx2_ref), (gv_here, gv_ref))):
            copy = pltpu.make_async_copy(here.at[window, :], there.at[window, :], sems.at[seg, j])
            copy.start()
            copies.append(copy)
    for copy in copies:
        copy.wait()


def on_device(g_out, w_out, gate_x1, gate_x2, value_v, residue, decay):
    tokens, channels = gate_x1.shape
    context_size = lax.axis_size("ctx")
    ch_size = lax.axis_size("ch")
    length = tokens * context_size
    modes = residue.shape[1]
    lane_tiles = channels // LANES
    owned = channels // context_size

    bits = [1 << bit for bit in range(ch_size.bit_length() - 1)]
    half_rows = tokens // 2
    chunks = [(0, half_rows, bits), (half_rows, half_rows, bits[::-1])]
    segments = [(start, rows) for start, rows, _ in chunks]
    count = len(chunks)
    layouts = [halving_layout(order) for _, _, order in chunks]
    cut = ch_size // 2

    rows_of = [(start, rows) for start, rows, _ in chunks]
    projected = project(
        g_out, w_out, [(*where, layout[:cut]) for where, layout in zip(rows_of, layouts)], channels)
    sent = [lax.ppermute(piece, "ch", xor_pairs(ch_size, order[0]))
            for piece, (_, _, order) in zip(projected, chunks)]
    kept = project_kept(
        g_out, w_out, [(*where, layout[cut:]) for where, layout in zip(rows_of, layouts)], channels)

    decay_t = decay.T
    residue_t = residue.T
    a = jnp.exp(-decay_t)
    r = residue_t * length ** (-0.5)
    scale = -residue_t * decay_t

    state_shape = jax.ShapeDtypeStruct((lane_tiles, count, BLOCKS * modes, LANES), F32)
    perm_shape = jax.ShapeDtypeStruct((lane_tiles, tokens, LANES), F32)
    work = tokens * channels * modes
    xperm, hb, eb, total = pl.pallas_call(
        functools.partial(forward_body, segments, modes),
        out_shape=[perm_shape, state_shape, state_shape,
                   jax.ShapeDtypeStruct((2 * modes, channels), F32)],
        scratch_shapes=[pltpu.VMEM((lane_tiles, tokens, LANES), F32)],
        compiler_params=params(),
        cost_estimate=cost(3.7),
        name="forward",
    )(gate_x2, value_v, a, decay_t)

    pairs = context_size // 2
    partner = lax.ppermute(total, "ctx", xor_pairs(context_size, 1))
    both = pl.pallas_call(
        functools.partial(forward_pair_body, modes, tokens),
        out_shape=jax.ShapeDtypeStruct((2 * modes, channels), F32),
        compiler_params=params(),
        name="forward_pair",
    )(total, partner, decay_t)
    got = [lax.ppermute(both, "ctx", xor_pairs(context_size, 2 * step)) for step in range(1, pairs)]

    uperms, gbs, sums = [], [], []
    arrived = [[piece] for piece in sent]
    away = both
    for level in range(1, len(bits)):
        for which, (_, _, order) in enumerate(chunks):
            arrived[which][-1], _ = lax.optimization_barrier((arrived[which][-1], away))
            stop = cut >> level
            width = kept[which].shape[1]
            left = width - 2 * stop * channels
            away = kept[which][:, left:left + stop * channels].astype(F32)
            for piece in arrived[which]:
                left = piece.shape[1] - 2 * stop * channels
                away = away + piece[:, left:left + stop * channels].astype(F32)
            away = away.astype(BF16)
            hb, away = lax.optimization_barrier((hb, away))
            arrived[which].append(lax.ppermute(away, "ch", xor_pairs(ch_size, order[level])))
    store_shape = jax.ShapeDtypeStruct((lane_tiles, modes, tokens, LANES), F32)
    resp, store, hin, kin = pl.pallas_call(
        functools.partial(respond_body, segments, modes, tokens),
        out_shape=[perm_shape, store_shape, state_shape, state_shape],
        scratch_shapes=[pltpu.VMEM((tokens, LANES), F32)],
        compiler_params=params(),
        cost_estimate=cost(3.5),
        name="respond",
    )(hb, eb, xperm, a, r, decay_t, partner, *got)

    previous = []
    for seg, (start, rows) in enumerate(segments):
        block_shape = jax.ShapeDtypeStruct((lane_tiles, BLOCKS * modes, LANES), F32)
        pieces = arrived[seg]
        *buffers, uperm, gb, partial_sums = pl.pallas_call(
            functools.partial(adjoint_body, (seg, start, rows), modes, len(pieces), len(previous)),
            in_specs=in_vmem(1 + len(pieces)) + [pl.BlockSpec(memory_space=HBM)] * len(previous) + in_vmem(6),
            out_specs=[pl.BlockSpec(memory_space=HBM)] * 3 + in_vmem(3),
            out_shape=[jax.ShapeDtypeStruct((tokens, channels), BF16)] * 3
            + [
                       jax.ShapeDtypeStruct((lane_tiles, rows, LANES), F32),
                       block_shape,
                       jax.ShapeDtypeStruct((2 * modes, channels), F32)],
            scratch_shapes=[pltpu.VMEM((lane_tiles, rows, LANES), F32)]
            + [pltpu.VMEM((BLOCKS * modes, LANES), F32)] * 2
            + [pltpu.VMEM((rows, channels), BF16), pltpu.SemaphoreType.DMA(())],
            input_output_aliases={1 + len(pieces) + j: j for j in range(len(previous))},
            compiler_params=params(),
            cost_estimate=cost(2.7 * rows / 512),
            name="adjoint",
        )(kept[seg], *pieces, *previous, gate_x1, resp, store, hin, kin, a)
        previous = buffers
        uperms.append(uperm)
        gbs.append(gb)
        sums.append(partial_sums)

    message = pl.pallas_call(
        functools.partial(gather_body, segments, modes),
        out_shape=jax.ShapeDtypeStruct((3 * modes, channels), F32),
        compiler_params=params(),
        name="totals",
    )(*gbs, *sums, scale, decay_t)
    partner = lax.ppermute(message, "ctx", xor_pairs(context_size, 1))
    both = pl.pallas_call(
        functools.partial(backward_pair_body, modes, tokens, owned),
        out_shape=jax.ShapeDtypeStruct((modes + 2 * modes // lane_tiles, channels), F32),
        compiler_params=params(),
        name="backward_pair",
    )(message, partner, decay_t)
    got = [lax.ppermute(both, "ctx", xor_pairs(context_size, 2 * step)) for step in range(1, pairs)]
    *uperms, _ = lax.optimization_barrier((*uperms, both))
    alocs = [
        pl.pallas_call(
            functools.partial(local_body, segments, modes, seg),
            out_shape=jax.ShapeDtypeStruct((lane_tiles, rows, LANES), F32),
            scratch_shapes=[pltpu.VMEM((BLOCKS * modes, LANES), F32)],
            compiler_params=params(),
            cost_estimate=cost(1.8 * rows / 512),
            name="local_adjoint",
        )(uperms[seg], *gbs[seg:], a, r, decay_t)
        for seg, (_, rows) in enumerate(segments)
    ]

    grad_x2, grad_v, residue_grad, decay_grad = pl.pallas_call(
        functools.partial(finish_body, segments, modes, tokens, length, pairs),
        in_specs=in_vmem(count + 6 + pairs) + [pl.BlockSpec(memory_space=HBM)] * 2,
        out_specs=[pl.BlockSpec(memory_space=HBM)] * 4,
        out_shape=[jax.ShapeDtypeStruct((tokens, channels), BF16)] * 2
        + [jax.ShapeDtypeStruct((modes, owned), F32)] * 2,
        scratch_shapes=[pltpu.VMEM((BLOCKS * modes, LANES), F32),
                        pltpu.VMEM((lane_tiles, tokens, LANES), F32),
                        pltpu.VMEM((tokens, channels), BF16),
                        pltpu.VMEM((tokens, channels), BF16),
                        pltpu.VMEM((modes, owned), F32),
                        pltpu.VMEM((modes, owned), F32),
                        pltpu.SemaphoreType.DMA((count + 1, 2))],
        input_output_aliases={count + 6 + pairs: 0, count + 7 + pairs: 1},
        compiler_params=params(),
        cost_estimate=cost(3.4),
        name="finish",
    )(*alocs, a, r, decay_t, gate_x2, value_v, partner, both, *got, *previous[1:])
    return previous[0], grad_x2, grad_v, residue_grad.T, decay_grad.T


def solution(mesh):
    return jax.shard_map(
        on_device,
        mesh=mesh,
        in_specs=(
            P("ctx", "ch"),
            P(None, "ch"),
            P("ctx", "ch"),
            P("ctx", "ch"),
            P("ctx", "ch"),
            P("ch", None),
            P("ch", None),
        ),
        out_specs=(
            P("ctx", "ch"),
            P("ctx", "ch"),
            P("ctx", "ch"),
            P(("ch", "ctx"), None),
            P(("ch", "ctx"), None),
        ),
        check_vma=False,
    )
```

```python
import functools

import jax
import jax.numpy as jnp
from jax import lax
from jax.experimental import pallas as pl
from jax.experimental.pallas import tpu as pltpu
from jax.sharding import PartitionSpec as P

LANES = 128
PIECES = 2
FPARTS = 2
KEPT = jnp.bfloat16
BLOCKS = 8
F32 = jnp.float32
BF16 = jnp.bfloat16


def halving_layout(order):
    if not order:
        return [0]
    rest = halving_layout(order[1:])
    return [offset ^ order[0] for offset in rest] + rest


def xor_pairs(count, step):
    return [(index, index ^ step) for index in range(count)]


HBM = pltpu.MemorySpace.HBM
VMEM = pltpu.MemorySpace.VMEM
CONTRACT_LAST = (((1,), (1,)), ((), ()))


def params(mebibytes=24):
    return pltpu.CompilerParams(vmem_limit_bytes=mebibytes * 2**20)


def cost(microseconds):
    return pl.CostEstimate(flops=int(microseconds * 1.1e9), bytes_accessed=0, transcendentals=0)


def in_vmem(count):
    return [pl.BlockSpec(memory_space=VMEM)] * count


def block_rows(offset, width):
    block = lax.axis_index("ch") ^ offset
    return pl.ds(pl.multiple_of(block * width, width), width)


def arrange(count):
    return [1, 3, 2, 0] if count == 4 else list(range(count))


def block_runs(offsets, arranged):
    places = sorted((arranged.index(offset), spot) for spot, offset in enumerate(offsets))
    runs = []
    for where, spot in places:
        if runs and runs[-1][1] + len(runs[-1][0]) == where:
            runs[-1][0].append(spot)
        else:
            runs.append(([spot], where))
    return runs


def project_body(work, width, pieces, g_ref, w_ref, *refs):
    count = len(work)
    out_refs = refs[:count]
    out_here = refs[count:2 * count]
    g_here, w_here, total, g_sems, w_sems, out_sems = refs[2 * count:]
    depth = g_ref.shape[1] // pieces
    arranged = arrange(w_ref.shape[0] // width)
    pending = {}

    def g_copy(rows, piece):
        columns = pl.ds(piece * depth, depth)
        return pltpu.make_async_copy(
            g_ref.at[rows, columns], g_here.at[rows, columns], g_sems.at[rows.start // rows.size, piece])

    def w_copy(offset, piece):
        columns = pl.ds(piece * depth, depth)
        there = pl.ds(arranged.index(offset) * width, width)
        return pltpu.make_async_copy(
            w_ref.at[block_rows(offset, width), columns], w_here.at[there, columns],
            w_sems.at[offset, piece])

    for start, rows, offsets in work:
        for piece in range(pieces):
            for key, copy in [((start, piece), lambda: g_copy(pl.ds(start, rows), piece))] + [
                    ((-1 - offset, piece), functools.partial(w_copy, offset, piece)) for offset in offsets]:
                if key not in pending:
                    pending[key] = copy()
                    pending[key].start()
    leaving = []
    for which, (start, rows, offsets) in enumerate(work):
        out_ref = out_here[which]
        for piece in range(pieces):
            columns = pl.ds(piece * depth, depth)
            for key in [(start, piece)] + [(-1 - offset, piece) for offset in offsets]:
                copy = pending.pop(key, None)
                if copy is not None:
                    copy.wait()
            for spots, where in block_runs(offsets, arranged):
                product = lax.dot_general(
                    g_here[pl.ds(start, rows), columns],
                    w_here[pl.ds(where * width, len(spots) * width), columns],
                    CONTRACT_LAST, preferred_element_type=F32)
                for k, spot in enumerate(spots):
                    here = pl.ds(spot * width, width)
                    value = product[:, k * width:(k + 1) * width]
                    if piece > 0:
                        value = value + total[:, here]
                    if piece < pieces - 1:
                        total[:, here] = value
                    else:
                        out_ref[:, here] = value.astype(out_ref.dtype)
        leaving.append(pltpu.make_async_copy(out_ref, out_refs[which], out_sems.at[which]))
        leaving[-1].start()
    for copy in leaving:
        copy.wait()


def project(g_out, w_out, work, width):
    blocks = w_out.shape[0] // width
    pieces = PIECES
    shapes = [jax.ShapeDtypeStruct((rows, len(offsets) * width), BF16) for _, rows, offsets in work]
    groups = g_out.shape[0] // work[0][1]
    return pl.pallas_call(
        functools.partial(project_body, work, width, pieces),
        in_specs=[pl.BlockSpec(memory_space=HBM)] * 2,
        out_specs=[pl.BlockSpec(memory_space=HBM)] * len(work),
        out_shape=shapes,
        scratch_shapes=[pltpu.VMEM(shape.shape, BF16) for shape in shapes] + [
            pltpu.VMEM(g_out.shape, BF16),
            pltpu.VMEM(w_out.shape, BF16),
            pltpu.VMEM(shapes[0].shape, F32),
            pltpu.SemaphoreType.DMA((groups, pieces)),
            pltpu.SemaphoreType.DMA((blocks, pieces)),
            pltpu.SemaphoreType.DMA((len(work),)),
        ],
        compiler_params=params(60),
        cost_estimate=cost(5),
        name="project",
    )(g_out, w_out)


def project_kept_body(work, width, g_ref, w_ref, *out_refs):
    for (start, rows, offsets), out_ref in zip(work, out_refs):
        for spot, offset in enumerate(offsets):
            out_ref[:, pl.ds(spot * width, width)] = lax.dot_general(
                g_ref[pl.ds(start, rows), :], w_ref[block_rows(offset, width), :],
                CONTRACT_LAST, preferred_element_type=F32).astype(out_ref.dtype)


def project_kept(g_out, w_out, work, width):
    return pl.pallas_call(
        functools.partial(project_kept_body, work, width),
        in_specs=in_vmem(2),
        out_specs=in_vmem(len(work)),
        out_shape=[jax.ShapeDtypeStruct((rows, len(offsets) * width), KEPT)
                   for _, rows, offsets in work],
        compiler_params=params(),
        cost_estimate=cost(3),
        name="project_kept",
    )(g_out, w_out)


def tree_sum(terms):
    terms = list(terms)
    while len(terms) > 1:
        terms = [sum(terms[i:i + 2][1:], terms[i]) for i in range(0, len(terms), 2)]
    return terms[0]


def spread(ref, row, lanes):
    return jnp.broadcast_to(ref[pl.ds(row, 1), lanes], (BLOCKS, LANES))


def forward_body(segments, modes, x2_ref, v_ref, a_ref, decay_ref,
                 xperm_ref, hb_ref, eb_ref, total_ref, nat):
    channels = x2_ref.shape[1]
    unroll = 16
    group = modes // FPARTS
    for lane in range(channels // LANES):
        lanes = pl.ds(lane * LANES, LANES)
        mixed = (x2_ref[:, lanes].astype(F32) * v_ref[:, lanes].astype(F32)).astype(BF16)
        nat[lane] = mixed.astype(F32)
        for seg, (start, rows) in enumerate(segments):
            steps = rows // BLOCKS
            for part in range(FPARTS):
                decays = [spread(a_ref, part * group + m, lanes) for m in range(group)]

                def body(outer, carry):
                    h, e = list(carry[0]), list(carry[1])
                    for q in range(unroll):
                        i = outer * unroll + q
                        here = pl.ds(pl.multiple_of(start + i * BLOCKS, BLOCKS), BLOCKS)
                        if part == 0:
                            x = nat[lane, pl.ds(start + i, BLOCKS, stride=steps), :]
                            xperm_ref[lane, here, :] = x
                        else:
                            x = xperm_ref[lane, here, :]
                        for m in range(group):
                            e[m] = decays[m] * e[m] + h[m]
                            h[m] = decays[m] * h[m] + x
                    return tuple(h), tuple(e)

                zero = (jnp.zeros((BLOCKS, LANES), F32),) * group
                h, e = lax.fori_loop(0, steps // unroll, body, (zero, zero))
                for m in range(group):
                    row = pl.ds(part * group + m, BLOCKS, stride=modes)
                    hb_ref[lane, seg, row, :] = h[m]
                    eb_ref[lane, seg, row, :] = e[m]
        a = a_ref[:, lanes]
        state = jnp.zeros((modes, LANES), F32)
        moment = jnp.zeros((modes, LANES), F32)
        for seg, (start, rows) in enumerate(segments):
            steps = rows // BLOCKS
            power = jnp.exp(-decay_ref[:, lanes] * steps)
            for b in range(BLOCKS):
                rowsb = pl.ds(b * modes, modes)
                moment = power * (moment + steps * state) + a * eb_ref[lane, seg, rowsb, :]
                state = power * state + hb_ref[lane, seg, rowsb, :]
        total_ref[pl.ds(0, modes), lanes] = state
        total_ref[pl.ds(modes, modes), lanes] = moment


def place():
    index = lax.axis_index("ctx")
    return index // 2, index % 2


def forward_pair_body(modes, tokens, total_ref, partner_ref, decay_ref, both_ref):
    _, core = place()
    state, moment = pl.ds(0, modes), pl.ds(modes, modes)
    power = jnp.exp(-decay_ref[...] * tokens)
    later = core == 1
    first_h = jnp.where(later, partner_ref[state, :], total_ref[state, :])
    first_k = jnp.where(later, partner_ref[moment, :], total_ref[moment, :])
    second_h = jnp.where(later, total_ref[state, :], partner_ref[state, :])
    second_k = jnp.where(later, total_ref[moment, :], partner_ref[moment, :])
    both_ref[state, :] = second_h + power * first_h
    both_ref[moment, :] = second_k + power * (first_k + tokens * first_h)


def respond_body(segments, modes, tokens, hb_ref, eb_ref, xperm_ref, a_ref, r_ref, decay_ref, partner_ref, *refs):
    got_refs, (resp_ref, store_ref, hin_ref, kin_ref, yloc) = refs[:-5], refs[-5:]
    half = modes // 2
    pair, core = place()
    channels = a_ref.shape[1]
    unroll = 16
    for lane in range(channels // LANES):
        lanes = pl.ds(lane * LANES, LANES)
        a = a_ref[:, lanes]
        state = jnp.where(core == 1, partner_ref[pl.ds(0, modes), lanes], 0.0)
        moment = jnp.where(core == 1, partner_ref[pl.ds(modes, modes), lanes], 0.0)
        for step, got_ref in enumerate(got_refs, 1):
            other = pair ^ step
            gap = jnp.maximum((2 * (pair - other - 1) + core) * tokens, 0).astype(F32)
            weight = jnp.where(other < pair, jnp.exp(-decay_ref[:, lanes] * gap), 0.0)
            got = got_ref[pl.ds(0, modes), lanes]
            state = state + weight * got
            moment = moment + weight * (got_ref[pl.ds(modes, modes), lanes] + gap * got)
        for seg, (start, rows) in enumerate(segments):
            steps = rows // BLOCKS
            power = jnp.exp(-decay_ref[:, lanes] * steps)
            for b in range(BLOCKS):
                rowsb = pl.ds(b * modes, modes)
                hin_ref[lane, seg, rowsb, :] = state
                kin_ref[lane, seg, rowsb, :] = moment
                moment = power * (moment + steps * state) + a * eb_ref[lane, seg, rowsb, :]
                state = power * state + hb_ref[lane, seg, rowsb, :]
        for seg, (start, rows) in enumerate(segments):
            steps = rows // BLOCKS
            for part in range(2):
                decays = [spread(a_ref, part * half + m, lanes) for m in range(half)]
                weights = [spread(r_ref, part * half + m, lanes) for m in range(half)]

                def body(outer, h):
                    h = list(h)
                    for q in range(unroll):
                        i = outer * unroll + q
                        here = pl.ds(pl.multiple_of(start + i * BLOCKS, BLOCKS), BLOCKS)
                        x = xperm_ref[lane, here, :]
                        for m in range(half):
                            h[m] = decays[m] * h[m] + x
                            store_ref[lane, part * half + m, here, :] = h[m]
                        y = tree_sum(weights[m] * h[m] for m in range(half))
                        if part == 0:
                            yloc[here, :] = y
                        else:
                            y = y + yloc[here, :]
                            resp_ref[lane, pl.ds(start + i, BLOCKS, stride=steps), :] = y
                    return tuple(h)

                begin = tuple(
                    hin_ref[lane, seg, pl.ds(part * half + m, BLOCKS, stride=modes), :]
                    for m in range(half))
                lax.fori_loop(0, steps // unroll, body, begin)


def adjoint_body(segment, modes, received, kept_ref, *refs):
    seg, start, rows = segment
    recv_refs = refs[:received]
    x1_ref, resp_ref, store_ref, hin_ref, kin_ref, a_ref = refs[received:received + 6]
    grad_ref, uperm, gb_ref, sums_ref, nat, rb, qb = refs[received + 6:]
    steps = rows // BLOCKS
    channels = x1_ref.shape[1]
    unroll = 16
    half = modes // 2
    window = pl.ds(start, rows)
    for lane in range(channels // LANES):
        lanes = pl.ds(lane * LANES, LANES)

        def own(ref):
            return ref[:, pl.ds(ref.shape[1] - channels + lane * LANES, LANES)]

        grad_in = own(kept_ref).astype(F32)
        for recv_ref in recv_refs:
            grad_in = grad_in + own(recv_ref).astype(F32)
        grad_ref[:, lanes] = (grad_in * resp_ref[lane, window, :]).astype(BF16)
        nat[lane] = (grad_in * x1_ref[window, lanes].astype(F32)).astype(BF16).astype(F32)
    for lane in range(channels // LANES):
        lanes = pl.ds(lane * LANES, LANES)
        for part in range(2):
            decays = [spread(a_ref, part * half + m, lanes) for m in range(half)]

            def body(outer, carry):
                g, racc, qacc = (list(item) for item in carry)
                for q in range(unroll):
                    i = steps - 1 - (outer * unroll + q)
                    here = pl.ds(pl.multiple_of(i * BLOCKS, BLOCKS), BLOCKS)
                    if part == 0:
                        u = nat[lane, pl.ds(i, BLOCKS, stride=steps), :]
                        uperm[lane, here, :] = u
                    else:
                        u = uperm[lane, here, :]
                    there = pl.ds(pl.multiple_of(start + i * BLOCKS, BLOCKS), BLOCKS)
                    for m in range(half):
                        h = store_ref[lane, part * half + m, there, :]
                        g[m] = decays[m] * g[m] + u
                        racc[m] = racc[m] + u * h
                        qacc[m] = qacc[m] + g[m] * h
                return tuple(g), tuple(racc), tuple(qacc)

            zero = (jnp.zeros((BLOCKS, LANES), F32),) * half
            g, racc, qacc = lax.fori_loop(0, steps // unroll, body, (zero,) * 3)
            for m in range(half):
                row = pl.ds(part * half + m, BLOCKS, stride=modes)
                gb_ref[lane, row, :] = g[m]
                rb[row, :] = racc[m]
                qb[row, :] = qacc[m]
        a = a_ref[:, lanes]
        total = jnp.zeros((modes, LANES), F32)
        moment = jnp.zeros((modes, LANES), F32)
        for b in range(BLOCKS):
            rowsb = pl.ds(b * modes, modes)
            before = hin_ref[lane, seg, rowsb, :] + kin_ref[lane, seg, rowsb, :]
            total = total + rb[rowsb, :]
            moment = moment + qb[rowsb, :] - rb[rowsb, :] + a * gb_ref[lane, rowsb, :] * before
        sums_ref[pl.ds(0, modes), lanes] = total
        sums_ref[pl.ds(modes, modes), lanes] = moment


def local_body(segments, modes, seg, uperm_ref, *refs):
    count = len(segments)
    gb_refs = refs[:count - seg]
    a_ref, r_ref, decay_ref, aloc_ref, gin = refs[count - seg:]
    channels = a_ref.shape[1]
    unroll = 16
    half = modes // 2
    for lane in range(channels // LANES):
        lanes = pl.ds(lane * LANES, LANES)
        state = jnp.zeros((modes, LANES), F32)
        for other in reversed(range(seg, count)):
            steps = segments[other][1] // BLOCKS
            power = jnp.exp(-decay_ref[:, lanes] * steps)
            for b in reversed(range(BLOCKS)):
                rowsb = pl.ds(b * modes, modes)
                if other == seg:
                    gin[rowsb, :] = state
                state = power * state + gb_refs[other - seg][lane, rowsb, :]
        for part in range(2):
            decays = [spread(a_ref, part * half + m, lanes) for m in range(half)]
            weights = [spread(r_ref, part * half + m, lanes) for m in range(half)]

            def body(outer, g):
                g = list(g)
                for q in range(unroll):
                    i = steps - 1 - (outer * unroll + q)
                    here = pl.ds(pl.multiple_of(i * BLOCKS, BLOCKS), BLOCKS)
                    u = uperm_ref[lane, here, :]
                    for m in range(half):
                        g[m] = decays[m] * g[m] + u
                    y = tree_sum(weights[m] * g[m] for m in range(half))
                    if part == 1:
                        y = y + aloc_ref[lane, here, :]
                    aloc_ref[lane, here, :] = y
                return tuple(g)

            begin = tuple(gin[pl.ds(part * half + m, BLOCKS, stride=modes), :] for m in range(half))
            lax.fori_loop(0, steps // unroll, body, begin)


def gather_body(segments, modes, *refs):
    count = len(segments)
    gb_refs, sums_refs = refs[:count], refs[count:2 * count]
    scale_ref, decay_ref, out_ref = refs[2 * count:]
    channels = decay_ref.shape[1]
    for lane in range(channels // LANES):
        lanes = pl.ds(lane * LANES, LANES)
        state = jnp.zeros((modes, LANES), F32)
        for seg in reversed(range(count)):
            power = jnp.exp(-decay_ref[:, lanes] * (segments[seg][1] // BLOCKS))
            for b in reversed(range(BLOCKS)):
                state = power * state + gb_refs[seg][lane, pl.ds(b * modes, modes), :]
        out_ref[pl.ds(0, modes), lanes] = state
    sums = sum(ref[...] for ref in sums_refs)
    out_ref[pl.ds(modes, modes), :] = sums[:modes]
    out_ref[pl.ds(2 * modes, modes), :] = sums[modes:] * scale_ref[...]


def three_parts(values):
    parts = []
    for _ in range(3):
        parts.append(values.astype(BF16))
        values = values - parts[-1].astype(F32)
    return parts


def pick(values, chosen, dims):
    return sum(
        lax.dot_general(part, chosen, dims, preferred_element_type=F32)
        for part in three_parts(values)
    )


def backward_pair_body(modes, tokens, owned, message_ref, partner_ref, decay_ref, both_ref):
    _, core = place()
    channels = decay_ref.shape[1]
    state, sums = pl.ds(0, modes), pl.ds(modes, 2 * modes)
    first = jnp.where(core == 0, message_ref[state, :], partner_ref[state, :])
    second = jnp.where(core == 0, partner_ref[state, :], message_ref[state, :])
    both_ref[state, :] = first + jnp.exp(-decay_ref[...] * tokens) * second
    channel = lax.broadcasted_iota(jnp.int32, (channels, LANES), 0)
    lane = lax.broadcasted_iota(jnp.int32, (channels, LANES), 1)
    wanted = (2 * (lane // owned) + core) * owned + lane % owned
    picked = pick(message_ref[sums, :] + partner_ref[sums, :], (channel == wanted).astype(BF16),
                  (((1,), (0,)), ((), ())))
    tiles = channels // LANES
    rows = 2 * modes // tiles
    for tile in range(tiles):
        both_ref[pl.ds(modes, rows), pl.ds(tile * LANES, LANES)] = picked[tile * rows:(tile + 1) * rows]


def finish_body(segments, modes, tokens, length, pairs, *refs):
    count = len(segments)
    aloc_refs, grad_refs = refs[:count], refs[count:2 * count]
    refs = refs[count:]
    a_ref, r_ref, decay_ref, x2_ref, v_ref, partner_ref, both_ref = refs[count:count + 7]
    got_refs = refs[count + 7:count + 6 + pairs]
    gx1_ref, gx2_ref, gv_ref, rgrad_ref, dgrad_ref, gin, nat, gx2_here, gv_here, r_here, d_here, sems = refs[-12:]
    channels = a_ref.shape[1]
    unroll = 16
    pair, core = place()
    states = []
    for lane in range(channels // LANES):
        lanes = pl.ds(lane * LANES, LANES)
        state = jnp.where(core == 0, partner_ref[pl.ds(0, modes), lanes], 0.0)
        for step, got_ref in enumerate(got_refs, 1):
            other = pair ^ step
            gap = jnp.maximum((2 * (other - pair - 1) + 1 - core) * tokens, 0).astype(F32)
            weight = jnp.where(other > pair, jnp.exp(-decay_ref[:, lanes] * gap), 0.0)
            state = state + weight * got_ref[pl.ds(0, modes), lanes]
        states.append(state)
    copies = []
    for seg, grad_ref in enumerate(grad_refs):
        copies.append(pltpu.make_async_copy(grad_ref, gx1_ref.at[pl.ds(*segments[seg]), :], sems.at[seg, 2]))
        copies[-1].start()
    owned = rgrad_ref.shape[1]
    tiles = channels // LANES
    lower = pl.ds(modes, 2 * modes // tiles)
    sums = both_ref[lower, :]
    for got_ref in got_refs:
        sums = sums + got_ref[lower, :]
    row = lax.broadcasted_iota(jnp.int32, (owned, LANES), 0)
    column = lax.broadcasted_iota(jnp.int32, (owned, LANES), 1)
    chosen = (column == pair * owned + row).astype(BF16)

    def choose(values):
        return sum(
            lax.dot_general(part, chosen, CONTRACT_LAST, preferred_element_type=F32)
            for part in three_parts(values)
        )

    if tiles == 1:
        residue_sums, decay_sums = sums[:modes], sums[modes:]
    else:
        residue_sums, decay_sums = sums[:, :LANES], sums[:, LANES:]
    r_here[...] = choose(residue_sums) / length
    d_here[...] = choose(decay_sums) / length
    for j, (here, there) in enumerate(((r_here, rgrad_ref), (d_here, dgrad_ref))):
        copy = pltpu.make_async_copy(here, there, sems.at[count, j])
        copy.start()
        copies.append(copy)
    for seg in reversed(range(count)):
        start, rows = segments[seg]
        steps = rows // BLOCKS
        window = pl.ds(start, rows)
        for lane in range(channels // LANES):
            lanes = pl.ds(lane * LANES, LANES)
            decays = [spread(a_ref, m, lanes) for m in range(modes)]
            state = states[lane]
            power = jnp.exp(-decay_ref[:, lanes] * steps)
            for b in reversed(range(BLOCKS)):
                rowsb = pl.ds(b * modes, modes)
                gin[rowsb, :] = state
                state = power * state
            states[lane] = state
            edge = tuple(
                spread(r_ref, m, lanes) * decays[m] * gin[pl.ds(m, BLOCKS, stride=modes), :]
                for m in range(modes)
            )

            def body(outer, edge):
                edge = list(edge)
                for q in range(unroll):
                    i = steps - 1 - (outer * unroll + q)
                    here = pl.ds(pl.multiple_of(i * BLOCKS, BLOCKS), BLOCKS)
                    y = tree_sum(edge) + aloc_refs[seg][lane, here, :]
                    for m in range(modes):
                        edge[m] = edge[m] * decays[m]
                    nat[lane, pl.ds(start + i, BLOCKS, stride=steps), :] = y
                return tuple(edge)

            lax.fori_loop(0, steps // unroll, body, edge)
            adjoint = nat[lane, window, :]
            gx2_here[window, lanes] = (adjoint * v_ref[window, lanes].astype(F32)).astype(BF16)
            gv_here[window, lanes] = (adjoint * x2_ref[window, lanes].astype(F32)).astype(BF16)
        for j, (here, there) in enumerate(((gx2_here, gx2_ref), (gv_here, gv_ref))):
            copy = pltpu.make_async_copy(here.at[window, :], there.at[window, :], sems.at[seg, j])
            copy.start()
            copies.append(copy)
    for copy in copies:
        copy.wait()


def on_device(g_out, w_out, gate_x1, gate_x2, value_v, residue, decay):
    tokens, channels = gate_x1.shape
    context_size = lax.axis_size("ctx")
    ch_size = lax.axis_size("ch")
    length = tokens * context_size
    modes = residue.shape[1]
    lane_tiles = channels // LANES
    owned = channels // context_size

    bits = [1 << bit for bit in range(ch_size.bit_length() - 1)]
    half_rows = tokens // 2
    chunks = [(0, half_rows, bits), (half_rows, half_rows, bits[::-1])]
    segments = [(start, rows) for start, rows, _ in chunks]
    count = len(chunks)
    layouts = [halving_layout(order) for _, _, order in chunks]
    cut = ch_size // 2

    rows_of = [(start, rows) for start, rows, _ in chunks]
    projected = project(
        g_out, w_out, [(*where, layout[:cut]) for where, layout in zip(rows_of, layouts)], channels)
    sent = [lax.ppermute(piece, "ch", xor_pairs(ch_size, order[0]))
            for piece, (_, _, order) in zip(projected, chunks)]
    kept = project_kept(
        g_out, w_out, [(*where, layout[cut:]) for where, layout in zip(rows_of, layouts)], channels)

    decay_t = decay.T
    residue_t = residue.T
    a = jnp.exp(-decay_t)
    r = residue_t * length ** (-0.5)
    scale = -residue_t * decay_t

    state_shape = jax.ShapeDtypeStruct((lane_tiles, count, BLOCKS * modes, LANES), F32)
    perm_shape = jax.ShapeDtypeStruct((lane_tiles, tokens, LANES), F32)
    work = tokens * channels * modes
    xperm, hb, eb, total = pl.pallas_call(
        functools.partial(forward_body, segments, modes),
        out_shape=[perm_shape, state_shape, state_shape,
                   jax.ShapeDtypeStruct((2 * modes, channels), F32)],
        scratch_shapes=[pltpu.VMEM((lane_tiles, tokens, LANES), F32)],
        compiler_params=params(),
        cost_estimate=cost(3.7),
        name="forward",
    )(gate_x2, value_v, a, decay_t)

    pairs = context_size // 2
    partner = lax.ppermute(total, "ctx", xor_pairs(context_size, 1))
    both = pl.pallas_call(
        functools.partial(forward_pair_body, modes, tokens),
        out_shape=jax.ShapeDtypeStruct((2 * modes, channels), F32),
        compiler_params=params(),
        name="forward_pair",
    )(total, partner, decay_t)
    got = [lax.ppermute(both, "ctx", xor_pairs(context_size, 2 * step)) for step in range(1, pairs)]

    uperms, gbs, sums = [], [], []
    arrived = [[piece] for piece in sent]
    away = both
    for level in range(1, len(bits)):
        for which in reversed(range(count)):
            order = chunks[which][2]
            arrived[which][-1], _ = lax.optimization_barrier((arrived[which][-1], away))
            stop = cut >> level
            width = kept[which].shape[1]
            left = width - 2 * stop * channels
            away = kept[which][:, left:left + stop * channels].astype(F32)
            for piece in arrived[which]:
                left = piece.shape[1] - 2 * stop * channels
                away = away + piece[:, left:left + stop * channels].astype(F32)
            away = away.astype(BF16)
            hb, away = lax.optimization_barrier((hb, away))
            arrived[which].append(lax.ppermute(away, "ch", xor_pairs(ch_size, order[level])))
    store_shape = jax.ShapeDtypeStruct((lane_tiles, modes, tokens, LANES), F32)
    resp, store, hin, kin = pl.pallas_call(
        functools.partial(respond_body, segments, modes, tokens),
        out_shape=[perm_shape, store_shape, state_shape, state_shape],
        scratch_shapes=[pltpu.VMEM((tokens, LANES), F32)],
        compiler_params=params(),
        cost_estimate=cost(3.5),
        name="respond",
    )(hb, eb, xperm, a, r, decay_t, partner, *got)

    grads = []
    for seg in reversed(range(count)):
        start, rows = segments[seg]
        block_shape = jax.ShapeDtypeStruct((lane_tiles, BLOCKS * modes, LANES), F32)
        pieces = arrived[seg]
        grad, uperm, gb, partial_sums = pl.pallas_call(
            functools.partial(adjoint_body, (seg, start, rows), modes, len(pieces)),
            in_specs=in_vmem(7 + len(pieces)),
            out_specs=in_vmem(4),
            out_shape=[
                       jax.ShapeDtypeStruct((rows, channels), BF16),
                       jax.ShapeDtypeStruct((lane_tiles, rows, LANES), F32),
                       block_shape,
                       jax.ShapeDtypeStruct((2 * modes, channels), F32)],
            scratch_shapes=[pltpu.VMEM((lane_tiles, rows, LANES), F32)]
            + [pltpu.VMEM((BLOCKS * modes, LANES), F32)] * 2,
            compiler_params=params(),
            cost_estimate=cost(2.7 * rows / 512),
            name="adjoint",
        )(kept[seg], *pieces, gate_x1, resp, store, hin, kin, a)
        grads.append(grad)
        uperms.append(uperm)
        gbs.append(gb)
        sums.append(partial_sums)

    uperms, gbs, sums, grads = uperms[::-1], gbs[::-1], sums[::-1], grads[::-1]
    message = pl.pallas_call(
        functools.partial(gather_body, segments, modes),
        out_shape=jax.ShapeDtypeStruct((3 * modes, channels), F32),
        compiler_params=params(),
        name="totals",
    )(*gbs, *sums, scale, decay_t)
    partner = lax.ppermute(message, "ctx", xor_pairs(context_size, 1))
    both = pl.pallas_call(
        functools.partial(backward_pair_body, modes, tokens, owned),
        out_shape=jax.ShapeDtypeStruct((modes + 2 * modes // lane_tiles, channels), F32),
        compiler_params=params(),
        name="backward_pair",
    )(message, partner, decay_t)
    got = [lax.ppermute(both, "ctx", xor_pairs(context_size, 2 * step)) for step in range(1, pairs)]
    *uperms, _ = lax.optimization_barrier((*uperms, both))
    alocs = [
        pl.pallas_call(
            functools.partial(local_body, segments, modes, seg),
            out_shape=jax.ShapeDtypeStruct((lane_tiles, rows, LANES), F32),
            scratch_shapes=[pltpu.VMEM((BLOCKS * modes, LANES), F32)],
            compiler_params=params(),
            cost_estimate=cost(1.8 * rows / 512),
            name="local_adjoint",
        )(uperms[seg], *gbs[seg:], a, r, decay_t)
        for seg, (_, rows) in enumerate(segments)
    ]

    grad_x1, grad_x2, grad_v, residue_grad, decay_grad = pl.pallas_call(
        functools.partial(finish_body, segments, modes, tokens, length, pairs),
        in_specs=in_vmem(2 * count + 6 + pairs),
        out_specs=[pl.BlockSpec(memory_space=HBM)] * 5,
        out_shape=[jax.ShapeDtypeStruct((tokens, channels), BF16)] * 3
        + [jax.ShapeDtypeStruct((modes, owned), F32)] * 2,
        scratch_shapes=[pltpu.VMEM((BLOCKS * modes, LANES), F32),
                        pltpu.VMEM((lane_tiles, tokens, LANES), F32),
                        pltpu.VMEM((tokens, channels), BF16),
                        pltpu.VMEM((tokens, channels), BF16),
                        pltpu.VMEM((modes, owned), F32),
                        pltpu.VMEM((modes, owned), F32),
                        pltpu.SemaphoreType.DMA((count + 1, 3))],
        compiler_params=params(),
        cost_estimate=cost(3.4),
        name="finish",
    )(*alocs, *grads, a, r, decay_t, gate_x2, value_v, partner, both, *got)
    return grad_x1, grad_x2, grad_v, residue_grad.T, decay_grad.T


def solution(mesh):
    return jax.shard_map(
        on_device,
        mesh=mesh,
        in_specs=(
            P("ctx", "ch"),
            P(None, "ch"),
            P("ctx", "ch"),
            P("ctx", "ch"),
            P("ctx", "ch"),
            P("ch", None),
            P("ch", None),
        ),
        out_specs=(
            P("ctx", "ch"),
            P("ctx", "ch"),
            P("ctx", "ch"),
            P(("ch", "ctx"), None),
            P(("ch", "ctx"), None),
        ),
        check_vma=False,
    )
```

```python
import functools

import jax
import jax.numpy as jnp
from jax import lax
from jax.experimental import pallas as pl
from jax.experimental.pallas import tpu as pltpu
from jax.sharding import PartitionSpec as P

LANES = 128
PIECES = 2
FPARTS = 2
KEPT = jnp.bfloat16
BLOCKS = 8
F32 = jnp.float32
BF16 = jnp.bfloat16


def halving_layout(order):
    if not order:
        return [0]
    rest = halving_layout(order[1:])
    return [offset ^ order[0] for offset in rest] + rest


def xor_pairs(count, step):
    return [(index, index ^ step) for index in range(count)]


HBM = pltpu.MemorySpace.HBM
VMEM = pltpu.MemorySpace.VMEM
CONTRACT_LAST = (((1,), (1,)), ((), ()))


def params(mebibytes=24):
    return pltpu.CompilerParams(vmem_limit_bytes=mebibytes * 2**20)


def cost(microseconds):
    return pl.CostEstimate(flops=int(microseconds * 1.1e9), bytes_accessed=0, transcendentals=0)


def in_vmem(count):
    return [pl.BlockSpec(memory_space=VMEM)] * count


def block_rows(offset, width):
    block = lax.axis_index("ch") ^ offset
    return pl.ds(pl.multiple_of(block * width, width), width)


def arrange(count):
    return [1, 3, 2, 0] if count == 4 else list(range(count))


def block_runs(offsets, arranged):
    places = sorted((arranged.index(offset), spot) for spot, offset in enumerate(offsets))
    runs = []
    for where, spot in places:
        if runs and runs[-1][1] + len(runs[-1][0]) == where:
            runs[-1][0].append(spot)
        else:
            runs.append(([spot], where))
    return runs


def project_body(work, width, pieces, g_ref, w_ref, *refs):
    count = len(work)
    out_refs = refs[:count]
    out_here = refs[count:2 * count]
    g_here, w_here, total, g_sems, w_sems, out_sems = refs[2 * count:]
    depth = g_ref.shape[1] // pieces
    arranged = arrange(w_ref.shape[0] // width)
    pending = {}

    def g_copy(rows, piece):
        columns = pl.ds(piece * depth, depth)
        return pltpu.make_async_copy(
            g_ref.at[rows, columns], g_here.at[rows, columns], g_sems.at[rows.start // rows.size, piece])

    def w_copy(offset, piece):
        columns = pl.ds(piece * depth, depth)
        there = pl.ds(arranged.index(offset) * width, width)
        return pltpu.make_async_copy(
            w_ref.at[block_rows(offset, width), columns], w_here.at[there, columns],
            w_sems.at[offset, piece])

    for start, rows, offsets in work:
        for piece in range(pieces):
            for key, copy in [((start, piece), lambda: g_copy(pl.ds(start, rows), piece))] + [
                    ((-1 - offset, piece), functools.partial(w_copy, offset, piece)) for offset in offsets]:
                if key not in pending:
                    pending[key] = copy()
                    pending[key].start()
    leaving = []
    for which, (start, rows, offsets) in enumerate(work):
        out_ref = out_here[which]
        for piece in range(pieces):
            columns = pl.ds(piece * depth, depth)
            for key in [(start, piece)] + [(-1 - offset, piece) for offset in offsets]:
                copy = pending.pop(key, None)
                if copy is not None:
                    copy.wait()
            parts = 2 if piece == pieces - 1 else 1
            for part in range(parts):
                height = rows // parts
                window = pl.ds(part * height, height)
                for spots, where in block_runs(offsets, arranged):
                    product = lax.dot_general(
                        g_here[pl.ds(start + part * height, height), columns],
                        w_here[pl.ds(where * width, len(spots) * width), columns],
                        CONTRACT_LAST, preferred_element_type=F32)
                    for k, spot in enumerate(spots):
                        here = pl.ds(spot * width, width)
                        value = product[:, k * width:(k + 1) * width]
                        if piece > 0:
                            value = value + total[window, here]
                        if piece < pieces - 1:
                            total[window, here] = value
                        else:
                            out_ref[window, here] = value.astype(out_ref.dtype)
                if piece == pieces - 1:
                    leaving.append(pltpu.make_async_copy(
                        out_ref.at[window, :], out_refs[which].at[window, :], out_sems.at[which, part]))
                    leaving[-1].start()
    for copy in leaving:
        copy.wait()


def project(g_out, w_out, work, width):
    blocks = w_out.shape[0] // width
    pieces = PIECES
    shapes = [jax.ShapeDtypeStruct((rows, len(offsets) * width), BF16) for _, rows, offsets in work]
    groups = g_out.shape[0] // work[0][1]
    return pl.pallas_call(
        functools.partial(project_body, work, width, pieces),
        in_specs=[pl.BlockSpec(memory_space=HBM)] * 2,
        out_specs=[pl.BlockSpec(memory_space=HBM)] * len(work),
        out_shape=shapes,
        scratch_shapes=[pltpu.VMEM(shape.shape, BF16) for shape in shapes] + [
            pltpu.VMEM(g_out.shape, BF16),
            pltpu.VMEM(w_out.shape, BF16),
            pltpu.VMEM(shapes[0].shape, F32),
            pltpu.SemaphoreType.DMA((groups, pieces)),
            pltpu.SemaphoreType.DMA((blocks, pieces)),
            pltpu.SemaphoreType.DMA((len(work), 2)),
        ],
        compiler_params=params(60),
        cost_estimate=cost(5),
        name="project",
    )(g_out, w_out)


def project_kept_body(work, width, g_ref, w_ref, *out_refs):
    for (start, rows, offsets), out_ref in zip(work, out_refs):
        for spot, offset in enumerate(offsets):
            out_ref[:, pl.ds(spot * width, width)] = lax.dot_general(
                g_ref[pl.ds(start, rows), :], w_ref[block_rows(offset, width), :],
                CONTRACT_LAST, preferred_element_type=F32).astype(out_ref.dtype)


def project_kept(g_out, w_out, work, width):
    return pl.pallas_call(
        functools.partial(project_kept_body, work, width),
        in_specs=in_vmem(2),
        out_specs=in_vmem(len(work)),
        out_shape=[jax.ShapeDtypeStruct((rows, len(offsets) * width), KEPT)
                   for _, rows, offsets in work],
        compiler_params=params(),
        cost_estimate=cost(3),
        name="project_kept",
    )(g_out, w_out)


def tree_sum(terms):
    terms = list(terms)
    while len(terms) > 1:
        terms = [sum(terms[i:i + 2][1:], terms[i]) for i in range(0, len(terms), 2)]
    return terms[0]


def spread(ref, row, lanes):
    return jnp.broadcast_to(ref[pl.ds(row, 1), lanes], (BLOCKS, LANES))


def forward_body(segments, modes, x2_ref, v_ref, a_ref, decay_ref,
                 xperm_ref, hb_ref, eb_ref, total_ref, nat):
    channels = x2_ref.shape[1]
    unroll = 32
    group = modes // FPARTS
    for lane in range(channels // LANES):
        lanes = pl.ds(lane * LANES, LANES)
        mixed = (x2_ref[:, lanes].astype(F32) * v_ref[:, lanes].astype(F32)).astype(BF16)
        nat[lane] = mixed.astype(F32)
        for seg, (start, rows) in enumerate(segments):
            steps = rows // BLOCKS
            for part in range(FPARTS):
                decays = [spread(a_ref, part * group + m, lanes) for m in range(group)]

                def body(outer, carry):
                    h, e = list(carry[0]), list(carry[1])
                    for q in range(unroll):
                        i = outer * unroll + q
                        here = pl.ds(pl.multiple_of(start + i * BLOCKS, BLOCKS), BLOCKS)
                        if part == 0:
                            x = nat[lane, pl.ds(start + i, BLOCKS, stride=steps), :]
                            xperm_ref[lane, here, :] = x
                        else:
                            x = xperm_ref[lane, here, :]
                        for m in range(group):
                            e[m] = decays[m] * e[m] + h[m]
                            h[m] = decays[m] * h[m] + x
                    return tuple(h), tuple(e)

                zero = (jnp.zeros((BLOCKS, LANES), F32),) * group
                h, e = lax.fori_loop(0, steps // unroll, body, (zero, zero))
                for m in range(group):
                    row = pl.ds(part * group + m, BLOCKS, stride=modes)
                    hb_ref[lane, seg, row, :] = h[m]
                    eb_ref[lane, seg, row, :] = e[m]
        a = a_ref[:, lanes]
        state = jnp.zeros((modes, LANES), F32)
        moment = jnp.zeros((modes, LANES), F32)
        for seg, (start, rows) in enumerate(segments):
            steps = rows // BLOCKS
            power = jnp.exp(-decay_ref[:, lanes] * steps)
            for b in range(BLOCKS):
                rowsb = pl.ds(b * modes, modes)
                moment = power * (moment + steps * state) + a * eb_ref[lane, seg, rowsb, :]
                state = power * state + hb_ref[lane, seg, rowsb, :]
        total_ref[pl.ds(0, modes), lanes] = state
        total_ref[pl.ds(modes, modes), lanes] = moment


def place():
    index = lax.axis_index("ctx")
    return index // 2, index % 2


def forward_pair_body(modes, tokens, total_ref, partner_ref, decay_ref, both_ref):
    _, core = place()
    state, moment = pl.ds(0, modes), pl.ds(modes, modes)
    power = jnp.exp(-decay_ref[...] * tokens)
    later = core == 1
    first_h = jnp.where(later, partner_ref[state, :], total_ref[state, :])
    first_k = jnp.where(later, partner_ref[moment, :], total_ref[moment, :])
    second_h = jnp.where(later, total_ref[state, :], partner_ref[state, :])
    second_k = jnp.where(later, total_ref[moment, :], partner_ref[moment, :])
    both_ref[state, :] = second_h + power * first_h
    both_ref[moment, :] = second_k + power * (first_k + tokens * first_h)


def respond_body(segments, modes, tokens, hb_ref, eb_ref, xperm_ref, a_ref, r_ref, decay_ref, partner_ref, *refs):
    got_refs, (resp_ref, store_ref, hin_ref, kin_ref, yloc) = refs[:-5], refs[-5:]
    half = modes // 2
    pair, core = place()
    channels = a_ref.shape[1]
    unroll = 32
    for lane in range(channels // LANES):
        lanes = pl.ds(lane * LANES, LANES)
        a = a_ref[:, lanes]
        state = jnp.where(core == 1, partner_ref[pl.ds(0, modes), lanes], 0.0)
        moment = jnp.where(core == 1, partner_ref[pl.ds(modes, modes), lanes], 0.0)
        for step, got_ref in enumerate(got_refs, 1):
            other = pair ^ step
            gap = jnp.maximum((2 * (pair - other - 1) + core) * tokens, 0).astype(F32)
            weight = jnp.where(other < pair, jnp.exp(-decay_ref[:, lanes] * gap), 0.0)
            got = got_ref[pl.ds(0, modes), lanes]
            state = state + weight * got
            moment = moment + weight * (got_ref[pl.ds(modes, modes), lanes] + gap * got)
        for seg, (start, rows) in enumerate(segments):
            steps = rows // BLOCKS
            power = jnp.exp(-decay_ref[:, lanes] * steps)
            for b in range(BLOCKS):
                rowsb = pl.ds(b * modes, modes)
                hin_ref[lane, seg, rowsb, :] = state
                kin_ref[lane, seg, rowsb, :] = moment
                moment = power * (moment + steps * state) + a * eb_ref[lane, seg, rowsb, :]
                state = power * state + hb_ref[lane, seg, rowsb, :]
        for seg, (start, rows) in enumerate(segments):
            steps = rows // BLOCKS
            for part in range(2):
                decays = [spread(a_ref, part * half + m, lanes) for m in range(half)]
                weights = [spread(r_ref, part * half + m, lanes) for m in range(half)]

                def body(outer, h):
                    h = list(h)
                    for q in range(unroll):
                        i = outer * unroll + q
                        here = pl.ds(pl.multiple_of(start + i * BLOCKS, BLOCKS), BLOCKS)
                        x = xperm_ref[lane, here, :]
                        for m in range(half):
                            h[m] = decays[m] * h[m] + x
                            store_ref[lane, part * half + m, here, :] = h[m]
                        y = tree_sum(weights[m] * h[m] for m in range(half))
                        if part == 0:
                            yloc[here, :] = y
                        else:
                            y = y + yloc[here, :]
                            resp_ref[lane, pl.ds(start + i, BLOCKS, stride=steps), :] = y
                    return tuple(h)

                begin = tuple(
                    hin_ref[lane, seg, pl.ds(part * half + m, BLOCKS, stride=modes), :]
                    for m in range(half))
                lax.fori_loop(0, steps // unroll, body, begin)


def adjoint_body(segment, modes, received, kept_ref, *refs):
    seg, start, rows = segment
    recv_refs = refs[:received]
    x1_ref, resp_ref, store_ref, hin_ref, kin_ref, a_ref = refs[received:received + 6]
    grad_ref, uperm, gb_ref, sums_ref, nat, rb, qb = refs[received + 6:]
    steps = rows // BLOCKS
    channels = x1_ref.shape[1]
    unroll = 32
    half = modes // 2
    window = pl.ds(start, rows)
    for lane in range(channels // LANES):
        lanes = pl.ds(lane * LANES, LANES)

        def own(ref):
            return ref[:, pl.ds(ref.shape[1] - channels + lane * LANES, LANES)]

        grad_in = own(kept_ref).astype(F32)
        for recv_ref in recv_refs:
            grad_in = grad_in + own(recv_ref).astype(F32)
        grad_ref[:, lanes] = (grad_in * resp_ref[lane, window, :]).astype(BF16)
        nat[lane] = (grad_in * x1_ref[window, lanes].astype(F32)).astype(BF16).astype(F32)
    for lane in range(channels // LANES):
        lanes = pl.ds(lane * LANES, LANES)
        for part in range(2):
            decays = [spread(a_ref, part * half + m, lanes) for m in range(half)]

            def body(outer, carry):
                g, racc, qacc = (list(item) for item in carry)
                for q in range(unroll):
                    i = steps - 1 - (outer * unroll + q)
                    here = pl.ds(pl.multiple_of(i * BLOCKS, BLOCKS), BLOCKS)
                    if part == 0:
                        u = nat[lane, pl.ds(i, BLOCKS, stride=steps), :]
                        uperm[lane, here, :] = u
                    else:
                        u = uperm[lane, here, :]
                    there = pl.ds(pl.multiple_of(start + i * BLOCKS, BLOCKS), BLOCKS)
                    for m in range(half):
                        h = store_ref[lane, part * half + m, there, :]
                        g[m] = decays[m] * g[m] + u
                        racc[m] = racc[m] + u * h
                        qacc[m] = qacc[m] + g[m] * h
                return tuple(g), tuple(racc), tuple(qacc)

            zero = (jnp.zeros((BLOCKS, LANES), F32),) * half
            g, racc, qacc = lax.fori_loop(0, steps // unroll, body, (zero,) * 3)
            for m in range(half):
                row = pl.ds(part * half + m, BLOCKS, stride=modes)
                gb_ref[lane, row, :] = g[m]
                rb[row, :] = racc[m]
                qb[row, :] = qacc[m]
        a = a_ref[:, lanes]
        total = jnp.zeros((modes, LANES), F32)
        moment = jnp.zeros((modes, LANES), F32)
        for b in range(BLOCKS):
            rowsb = pl.ds(b * modes, modes)
            before = hin_ref[lane, seg, rowsb, :] + kin_ref[lane, seg, rowsb, :]
            total = total + rb[rowsb, :]
            moment = moment + qb[rowsb, :] - rb[rowsb, :] + a * gb_ref[lane, rowsb, :] * before
        sums_ref[pl.ds(0, modes), lanes] = total
        sums_ref[pl.ds(modes, modes), lanes] = moment


def local_body(segments, modes, seg, uperm_ref, *refs):
    count = len(segments)
    gb_refs = refs[:count - seg]
    a_ref, r_ref, decay_ref, aloc_ref, gin = refs[count - seg:]
    channels = a_ref.shape[1]
    unroll = 32
    half = modes // 2
    for lane in range(channels // LANES):
        lanes = pl.ds(lane * LANES, LANES)
        state = jnp.zeros((modes, LANES), F32)
        for other in reversed(range(seg, count)):
            steps = segments[other][1] // BLOCKS
            power = jnp.exp(-decay_ref[:, lanes] * steps)
            for b in reversed(range(BLOCKS)):
                rowsb = pl.ds(b * modes, modes)
                if other == seg:
                    gin[rowsb, :] = state
                state = power * state + gb_refs[other - seg][lane, rowsb, :]
        for part in range(2):
            decays = [spread(a_ref, part * half + m, lanes) for m in range(half)]
            weights = [spread(r_ref, part * half + m, lanes) for m in range(half)]

            def body(outer, g):
                g = list(g)
                for q in range(unroll):
                    i = steps - 1 - (outer * unroll + q)
                    here = pl.ds(pl.multiple_of(i * BLOCKS, BLOCKS), BLOCKS)
                    u = uperm_ref[lane, here, :]
                    for m in range(half):
                        g[m] = decays[m] * g[m] + u
                    y = tree_sum(weights[m] * g[m] for m in range(half))
                    if part == 1:
                        y = y + aloc_ref[lane, here, :]
                    aloc_ref[lane, here, :] = y
                return tuple(g)

            begin = tuple(gin[pl.ds(part * half + m, BLOCKS, stride=modes), :] for m in range(half))
            lax.fori_loop(0, steps // unroll, body, begin)


def gather_body(segments, modes, *refs):
    count = len(segments)
    gb_refs, sums_refs = refs[:count], refs[count:2 * count]
    scale_ref, decay_ref, out_ref = refs[2 * count:]
    channels = decay_ref.shape[1]
    for lane in range(channels // LANES):
        lanes = pl.ds(lane * LANES, LANES)
        state = jnp.zeros((modes, LANES), F32)
        for seg in reversed(range(count)):
            power = jnp.exp(-decay_ref[:, lanes] * (segments[seg][1] // BLOCKS))
            for b in reversed(range(BLOCKS)):
                state = power * state + gb_refs[seg][lane, pl.ds(b * modes, modes), :]
        out_ref[pl.ds(0, modes), lanes] = state
    sums = sum(ref[...] for ref in sums_refs)
    out_ref[pl.ds(modes, modes), :] = sums[:modes]
    out_ref[pl.ds(2 * modes, modes), :] = sums[modes:] * scale_ref[...]


def three_parts(values):
    parts = []
    for _ in range(3):
        parts.append(values.astype(BF16))
        values = values - parts[-1].astype(F32)
    return parts


def pick(values, chosen, dims):
    return sum(
        lax.dot_general(part, chosen, dims, preferred_element_type=F32)
        for part in three_parts(values)
    )


def backward_pair_body(modes, tokens, owned, message_ref, partner_ref, decay_ref, both_ref):
    _, core = place()
    channels = decay_ref.shape[1]
    state, sums = pl.ds(0, modes), pl.ds(modes, 2 * modes)
    first = jnp.where(core == 0, message_ref[state, :], partner_ref[state, :])
    second = jnp.where(core == 0, partner_ref[state, :], message_ref[state, :])
    both_ref[state, :] = first + jnp.exp(-decay_ref[...] * tokens) * second
    channel = lax.broadcasted_iota(jnp.int32, (channels, LANES), 0)
    lane = lax.broadcasted_iota(jnp.int32, (channels, LANES), 1)
    wanted = (2 * (lane // owned) + core) * owned + lane % owned
    picked = pick(message_ref[sums, :] + partner_ref[sums, :], (channel == wanted).astype(BF16),
                  (((1,), (0,)), ((), ())))
    tiles = channels // LANES
    rows = 2 * modes // tiles
    for tile in range(tiles):
        both_ref[pl.ds(modes, rows), pl.ds(tile * LANES, LANES)] = picked[tile * rows:(tile + 1) * rows]


def finish_body(segments, modes, tokens, length, pairs, *refs):
    count = len(segments)
    aloc_refs, grad_refs = refs[:count], refs[count:2 * count]
    refs = refs[count:]
    a_ref, r_ref, decay_ref, x2_ref, v_ref, partner_ref, both_ref = refs[count:count + 7]
    got_refs = refs[count + 7:count + 6 + pairs]
    gx1_ref, gx2_ref, gv_ref, rgrad_ref, dgrad_ref, gin, nat, gx2_here, gv_here, r_here, d_here, sems = refs[-12:]
    channels = a_ref.shape[1]
    unroll = 16
    pair, core = place()
    states = []
    for lane in range(channels // LANES):
        lanes = pl.ds(lane * LANES, LANES)
        state = jnp.where(core == 0, partner_ref[pl.ds(0, modes), lanes], 0.0)
        for step, got_ref in enumerate(got_refs, 1):
            other = pair ^ step
            gap = jnp.maximum((2 * (other - pair - 1) + 1 - core) * tokens, 0).astype(F32)
            weight = jnp.where(other > pair, jnp.exp(-decay_ref[:, lanes] * gap), 0.0)
            state = state + weight * got_ref[pl.ds(0, modes), lanes]
        states.append(state)
    copies = []
    for seg, grad_ref in enumerate(grad_refs):
        copies.append(pltpu.make_async_copy(grad_ref, gx1_ref.at[pl.ds(*segments[seg]), :], sems.at[seg, 2]))
        copies[-1].start()
    owned = rgrad_ref.shape[1]
    tiles = channels // LANES
    lower = pl.ds(modes, 2 * modes // tiles)
    sums = both_ref[lower, :]
    for got_ref in got_refs:
        sums = sums + got_ref[lower, :]
    row = lax.broadcasted_iota(jnp.int32, (owned, LANES), 0)
    column = lax.broadcasted_iota(jnp.int32, (owned, LANES), 1)
    chosen = (column == pair * owned + row).astype(BF16)

    def choose(values):
        return sum(
            lax.dot_general(part, chosen, CONTRACT_LAST, preferred_element_type=F32)
            for part in three_parts(values)
        )

    if tiles == 1:
        residue_sums, decay_sums = sums[:modes], sums[modes:]
    else:
        residue_sums, decay_sums = sums[:, :LANES], sums[:, LANES:]
    r_here[...] = choose(residue_sums) / length
    d_here[...] = choose(decay_sums) / length
    for j, (here, there) in enumerate(((r_here, rgrad_ref), (d_here, dgrad_ref))):
        copy = pltpu.make_async_copy(here, there, sems.at[count, j])
        copy.start()
        copies.append(copy)
    for seg in reversed(range(count)):
        start, rows = segments[seg]
        steps = rows // BLOCKS
        window = pl.ds(start, rows)
        for lane in range(channels // LANES):
            lanes = pl.ds(lane * LANES, LANES)
            decays = [spread(a_ref, m, lanes) for m in range(modes)]
            state = states[lane]
            power = jnp.exp(-decay_ref[:, lanes] * steps)
            for b in reversed(range(BLOCKS)):
                rowsb = pl.ds(b * modes, modes)
                gin[rowsb, :] = state
                state = power * state
            states[lane] = state
            edge = tuple(
                spread(r_ref, m, lanes) * decays[m] * gin[pl.ds(m, BLOCKS, stride=modes), :]
                for m in range(modes)
            )

            def body(outer, edge):
                edge = list(edge)
                for q in range(unroll):
                    i = steps - 1 - (outer * unroll + q)
                    here = pl.ds(pl.multiple_of(i * BLOCKS, BLOCKS), BLOCKS)
                    y = tree_sum(edge) + aloc_refs[seg][lane, here, :]
                    for m in range(modes):
                        edge[m] = edge[m] * decays[m]
                    nat[lane, pl.ds(start + i, BLOCKS, stride=steps), :] = y
                return tuple(edge)

            lax.fori_loop(0, steps // unroll, body, edge)
            adjoint = nat[lane, window, :]
            gx2_here[window, lanes] = (adjoint * v_ref[window, lanes].astype(F32)).astype(BF16)
            gv_here[window, lanes] = (adjoint * x2_ref[window, lanes].astype(F32)).astype(BF16)
        for j, (here, there) in enumerate(((gx2_here, gx2_ref), (gv_here, gv_ref))):
            copy = pltpu.make_async_copy(here.at[window, :], there.at[window, :], sems.at[seg, j])
            copy.start()
            copies.append(copy)
    for copy in copies:
        copy.wait()


def on_device(g_out, w_out, gate_x1, gate_x2, value_v, residue, decay):
    tokens, channels = gate_x1.shape
    context_size = lax.axis_size("ctx")
    ch_size = lax.axis_size("ch")
    length = tokens * context_size
    modes = residue.shape[1]
    lane_tiles = channels // LANES
    owned = channels // context_size

    bits = [1 << bit for bit in range(ch_size.bit_length() - 1)]
    half_rows = tokens // 2
    chunks = [(0, half_rows, bits), (half_rows, half_rows, bits[::-1])]
    segments = [(start, rows) for start, rows, _ in chunks]
    count = len(chunks)
    layouts = [halving_layout(order) for _, _, order in chunks]
    cut = ch_size // 2

    rows_of = [(start, rows) for start, rows, _ in chunks]
    projected = project(
        g_out, w_out, [(*where, layout[:cut]) for where, layout in zip(rows_of, layouts)], channels)
    sent = [lax.ppermute(piece, "ch", xor_pairs(ch_size, order[0]))
            for piece, (_, _, order) in zip(projected, chunks)]
    kept = project_kept(
        g_out, w_out, [(*where, layout[cut:]) for where, layout in zip(rows_of, layouts)], channels)

    decay_t = decay.T
    residue_t = residue.T
    a = jnp.exp(-decay_t)
    r = residue_t * length ** (-0.5)
    scale = -residue_t * decay_t

    state_shape = jax.ShapeDtypeStruct((lane_tiles, count, BLOCKS * modes, LANES), F32)
    perm_shape = jax.ShapeDtypeStruct((lane_tiles, tokens, LANES), F32)
    work = tokens * channels * modes
    xperm, hb, eb, total = pl.pallas_call(
        functools.partial(forward_body, segments, modes),
        out_shape=[perm_shape, state_shape, state_shape,
                   jax.ShapeDtypeStruct((2 * modes, channels), F32)],
        scratch_shapes=[pltpu.VMEM((lane_tiles, tokens, LANES), F32)],
        compiler_params=params(),
        cost_estimate=cost(3.7),
        name="forward",
    )(gate_x2, value_v, a, decay_t)

    pairs = context_size // 2
    partner = lax.ppermute(total, "ctx", xor_pairs(context_size, 1))
    both = pl.pallas_call(
        functools.partial(forward_pair_body, modes, tokens),
        out_shape=jax.ShapeDtypeStruct((2 * modes, channels), F32),
        compiler_params=params(),
        name="forward_pair",
    )(total, partner, decay_t)
    got = [lax.ppermute(both, "ctx", xor_pairs(context_size, 2 * step)) for step in range(1, pairs)]

    uperms, gbs, sums = [], [], []
    arrived = [[piece] for piece in sent]
    away = both
    for level in range(1, len(bits)):
        for which in reversed(range(count)):
            order = chunks[which][2]
            arrived[which][-1], _ = lax.optimization_barrier((arrived[which][-1], away))
            stop = cut >> level
            width = kept[which].shape[1]
            left = width - 2 * stop * channels
            away = kept[which][:, left:left + stop * channels].astype(F32)
            for piece in arrived[which]:
                left = piece.shape[1] - 2 * stop * channels
                away = away + piece[:, left:left + stop * channels].astype(F32)
            away = away.astype(BF16)
            hb, away = lax.optimization_barrier((hb, away))
            arrived[which].append(lax.ppermute(away, "ch", xor_pairs(ch_size, order[level])))
    store_shape = jax.ShapeDtypeStruct((lane_tiles, modes, tokens, LANES), F32)
    resp, store, hin, kin = pl.pallas_call(
        functools.partial(respond_body, segments, modes, tokens),
        out_shape=[perm_shape, store_shape, state_shape, state_shape],
        scratch_shapes=[pltpu.VMEM((tokens, LANES), F32)],
        compiler_params=params(),
        cost_estimate=cost(3.5),
        name="respond",
    )(hb, eb, xperm, a, r, decay_t, partner, *got)

    grads = []
    for seg in reversed(range(count)):
        start, rows = segments[seg]
        block_shape = jax.ShapeDtypeStruct((lane_tiles, BLOCKS * modes, LANES), F32)
        pieces = arrived[seg]
        grad, uperm, gb, partial_sums = pl.pallas_call(
            functools.partial(adjoint_body, (seg, start, rows), modes, len(pieces)),
            in_specs=in_vmem(7 + len(pieces)),
            out_specs=in_vmem(4),
            out_shape=[
                       jax.ShapeDtypeStruct((rows, channels), BF16),
                       jax.ShapeDtypeStruct((lane_tiles, rows, LANES), F32),
                       block_shape,
                       jax.ShapeDtypeStruct((2 * modes, channels), F32)],
            scratch_shapes=[pltpu.VMEM((lane_tiles, rows, LANES), F32)]
            + [pltpu.VMEM((BLOCKS * modes, LANES), F32)] * 2,
            compiler_params=params(),
            cost_estimate=cost(2.7 * rows / 512),
            name="adjoint",
        )(kept[seg], *pieces, gate_x1, resp, store, hin, kin, a)
        grads.append(grad)
        uperms.append(uperm)
        gbs.append(gb)
        sums.append(partial_sums)

    uperms, gbs, sums, grads = uperms[::-1], gbs[::-1], sums[::-1], grads[::-1]
    message = pl.pallas_call(
        functools.partial(gather_body, segments, modes),
        out_shape=jax.ShapeDtypeStruct((3 * modes, channels), F32),
        compiler_params=params(),
        name="totals",
    )(*gbs, *sums, scale, decay_t)
    partner = lax.ppermute(message, "ctx", xor_pairs(context_size, 1))
    both = pl.pallas_call(
        functools.partial(backward_pair_body, modes, tokens, owned),
        out_shape=jax.ShapeDtypeStruct((modes + 2 * modes // lane_tiles, channels), F32),
        compiler_params=params(),
        name="backward_pair",
    )(message, partner, decay_t)
    got = [lax.ppermute(both, "ctx", xor_pairs(context_size, 2 * step)) for step in range(1, pairs)]
    *uperms, _ = lax.optimization_barrier((*uperms, both))
    alocs = [
        pl.pallas_call(
            functools.partial(local_body, segments, modes, seg),
            out_shape=jax.ShapeDtypeStruct((lane_tiles, rows, LANES), F32),
            scratch_shapes=[pltpu.VMEM((BLOCKS * modes, LANES), F32)],
            compiler_params=params(),
            cost_estimate=cost(1.8 * rows / 512),
            name="local_adjoint",
        )(uperms[seg], *gbs[seg:], a, r, decay_t)
        for seg, (_, rows) in enumerate(segments)
    ]

    grad_x1, grad_x2, grad_v, residue_grad, decay_grad = pl.pallas_call(
        functools.partial(finish_body, segments, modes, tokens, length, pairs),
        in_specs=in_vmem(2 * count + 6 + pairs),
        out_specs=[pl.BlockSpec(memory_space=HBM)] * 5,
        out_shape=[jax.ShapeDtypeStruct((tokens, channels), BF16)] * 3
        + [jax.ShapeDtypeStruct((modes, owned), F32)] * 2,
        scratch_shapes=[pltpu.VMEM((BLOCKS * modes, LANES), F32),
                        pltpu.VMEM((lane_tiles, tokens, LANES), F32),
                        pltpu.VMEM((tokens, channels), BF16),
                        pltpu.VMEM((tokens, channels), BF16),
                        pltpu.VMEM((modes, owned), F32),
                        pltpu.VMEM((modes, owned), F32),
                        pltpu.SemaphoreType.DMA((count + 1, 3))],
        compiler_params=params(),
        cost_estimate=cost(3.4),
        name="finish",
    )(*alocs, *grads, a, r, decay_t, gate_x2, value_v, partner, both, *got)
    return grad_x1, grad_x2, grad_v, residue_grad.T, decay_grad.T


def solution(mesh):
    return jax.shard_map(
        on_device,
        mesh=mesh,
        in_specs=(
            P("ctx", "ch"),
            P(None, "ch"),
            P("ctx", "ch"),
            P("ctx", "ch"),
            P("ctx", "ch"),
            P("ch", None),
            P("ch", None),
        ),
        out_specs=(
            P("ctx", "ch"),
            P("ctx", "ch"),
            P("ctx", "ch"),
            P(("ch", "ctx"), None),
            P(("ch", "ctx"), None),
        ),
        check_vma=False,
    )
```

```python
import functools

import jax
import jax.numpy as jnp
from jax import lax
from jax.experimental import pallas as pl
from jax.experimental.pallas import tpu as pltpu
from jax.sharding import PartitionSpec as P

LANES = 128
PIECES = 2
FPARTS = 2
KEPT = jnp.bfloat16
BLOCKS = 8
F32 = jnp.float32
BF16 = jnp.bfloat16


def halving_layout(order):
    if not order:
        return [0]
    rest = halving_layout(order[1:])
    return [offset ^ order[0] for offset in rest] + rest


def xor_pairs(count, step):
    return [(index, index ^ step) for index in range(count)]


HBM = pltpu.MemorySpace.HBM
VMEM = pltpu.MemorySpace.VMEM
CONTRACT_LAST = (((1,), (1,)), ((), ()))


def params(mebibytes=24):
    return pltpu.CompilerParams(vmem_limit_bytes=mebibytes * 2**20)


def cost(microseconds):
    return pl.CostEstimate(flops=int(microseconds * 1.1e9), bytes_accessed=0, transcendentals=0)


def in_vmem(count):
    return [pl.BlockSpec(memory_space=VMEM)] * count


def block_rows(offset, width):
    block = lax.axis_index("ch") ^ offset
    return pl.ds(pl.multiple_of(block * width, width), width)


def arrange(count):
    return [1, 3, 2, 0] if count == 4 else list(range(count))


def block_runs(offsets, arranged):
    places = sorted((arranged.index(offset), spot) for spot, offset in enumerate(offsets))
    runs = []
    for where, spot in places:
        if runs and runs[-1][1] + len(runs[-1][0]) == where:
            runs[-1][0].append(spot)
        else:
            runs.append(([spot], where))
    return runs


def project_body(work, width, pieces, g_ref, w_ref, *refs):
    count = len(work)
    out_refs = refs[:count]
    out_here = refs[count:2 * count]
    g_here, w_here, total, g_sems, w_sems, out_sems = refs[2 * count:]
    depth = g_ref.shape[1] // pieces
    arranged = arrange(w_ref.shape[0] // width)
    pending = {}

    def g_copy(rows, piece):
        columns = pl.ds(piece * depth, depth)
        return pltpu.make_async_copy(
            g_ref.at[rows, columns], g_here.at[rows, columns], g_sems.at[rows.start // rows.size, piece])

    def w_copy(offset, piece):
        columns = pl.ds(piece * depth, depth)
        there = pl.ds(arranged.index(offset) * width, width)
        return pltpu.make_async_copy(
            w_ref.at[block_rows(offset, width), columns], w_here.at[there, columns],
            w_sems.at[offset, piece])

    for start, rows, offsets in work:
        for piece in range(pieces):
            for key, copy in [((start, piece), lambda: g_copy(pl.ds(start, rows), piece))] + [
                    ((-1 - offset, piece), functools.partial(w_copy, offset, piece)) for offset in offsets]:
                if key not in pending:
                    pending[key] = copy()
                    pending[key].start()
    leaving = []
    for which, (start, rows, offsets) in enumerate(work):
        out_ref = out_here[which]
        for piece in range(pieces):
            columns = pl.ds(piece * depth, depth)
            for key in [(start, piece)] + [(-1 - offset, piece) for offset in offsets]:
                copy = pending.pop(key, None)
                if copy is not None:
                    copy.wait()
            parts = 2 if piece == pieces - 1 else 1
            for part in range(parts):
                height = rows // parts
                window = pl.ds(part * height, height)
                for spots, where in block_runs(offsets, arranged):
                    product = lax.dot_general(
                        g_here[pl.ds(start + part * height, height), columns],
                        w_here[pl.ds(where * width, len(spots) * width), columns],
                        CONTRACT_LAST, preferred_element_type=F32)
                    for k, spot in enumerate(spots):
                        here = pl.ds(spot * width, width)
                        value = product[:, k * width:(k + 1) * width]
                        if piece > 0:
                            value = value + total[window, here]
                        if piece < pieces - 1:
                            total[window, here] = value
                        else:
                            out_ref[window, here] = value.astype(out_ref.dtype)
                if piece == pieces - 1:
                    leaving.append(pltpu.make_async_copy(
                        out_ref.at[window, :], out_refs[which].at[window, :], out_sems.at[which, part]))
                    leaving[-1].start()
    for copy in leaving:
        copy.wait()


def project(g_out, w_out, work, width):
    blocks = w_out.shape[0] // width
    pieces = PIECES
    shapes = [jax.ShapeDtypeStruct((rows, len(offsets) * width), BF16) for _, rows, offsets in work]
    groups = g_out.shape[0] // work[0][1]
    return pl.pallas_call(
        functools.partial(project_body, work, width, pieces),
        in_specs=[pl.BlockSpec(memory_space=HBM)] * 2,
        out_specs=[pl.BlockSpec(memory_space=HBM)] * len(work),
        out_shape=shapes,
        scratch_shapes=[pltpu.VMEM(shape.shape, BF16) for shape in shapes] + [
            pltpu.VMEM(g_out.shape, BF16),
            pltpu.VMEM(w_out.shape, BF16),
            pltpu.VMEM(shapes[0].shape, F32),
            pltpu.SemaphoreType.DMA((groups, pieces)),
            pltpu.SemaphoreType.DMA((blocks, pieces)),
            pltpu.SemaphoreType.DMA((len(work), 2)),
        ],
        compiler_params=params(60),
        cost_estimate=cost(5),
        name="project",
    )(g_out, w_out)


def project_kept_body(work, width, g_ref, w_ref, *out_refs):
    for (start, rows, offsets), out_ref in zip(work, out_refs):
        for spot, offset in enumerate(offsets):
            out_ref[:, pl.ds(spot * width, width)] = lax.dot_general(
                g_ref[pl.ds(start, rows), :], w_ref[block_rows(offset, width), :],
                CONTRACT_LAST, preferred_element_type=F32).astype(out_ref.dtype)


def project_kept(g_out, w_out, work, width):
    return pl.pallas_call(
        functools.partial(project_kept_body, work, width),
        in_specs=in_vmem(2),
        out_specs=in_vmem(len(work)),
        out_shape=[jax.ShapeDtypeStruct((rows, len(offsets) * width), KEPT)
                   for _, rows, offsets in work],
        compiler_params=params(),
        cost_estimate=cost(3),
        name="project_kept",
    )(g_out, w_out)


def tree_sum(terms):
    terms = list(terms)
    while len(terms) > 1:
        terms = [sum(terms[i:i + 2][1:], terms[i]) for i in range(0, len(terms), 2)]
    return terms[0]


def spread(ref, row, lanes):
    return jnp.broadcast_to(ref[pl.ds(row, 1), lanes], (BLOCKS, LANES))


def forward_body(segments, modes, x2_ref, v_ref, a_ref, decay_ref,
                 xperm_ref, hb_ref, eb_ref, total_ref, nat):
    channels = x2_ref.shape[1]
    unroll = 32
    group = modes // FPARTS
    for lane in range(channels // LANES):
        lanes = pl.ds(lane * LANES, LANES)
        mixed = (x2_ref[:, lanes].astype(F32) * v_ref[:, lanes].astype(F32)).astype(BF16)
        nat[lane] = mixed.astype(F32)
        for seg, (start, rows) in enumerate(segments):
            steps = rows // BLOCKS
            for part in range(FPARTS):
                decays = [spread(a_ref, part * group + m, lanes) for m in range(group)]

                def body(outer, carry):
                    h, e = list(carry[0]), list(carry[1])
                    for q in range(unroll):
                        i = outer * unroll + q
                        here = pl.ds(pl.multiple_of(start + i * BLOCKS, BLOCKS), BLOCKS)
                        if part == 0:
                            x = nat[lane, pl.ds(start + i, BLOCKS, stride=steps), :]
                            xperm_ref[lane, here, :] = x
                        else:
                            x = xperm_ref[lane, here, :]
                        for m in range(group):
                            e[m] = decays[m] * e[m] + h[m]
                            h[m] = decays[m] * h[m] + x
                    return tuple(h), tuple(e)

                zero = (jnp.zeros((BLOCKS, LANES), F32),) * group
                h, e = lax.fori_loop(0, steps // unroll, body, (zero, zero))
                for m in range(group):
                    row = pl.ds(part * group + m, BLOCKS, stride=modes)
                    hb_ref[lane, seg, row, :] = h[m]
                    eb_ref[lane, seg, row, :] = e[m]
        a = a_ref[:, lanes]
        state = jnp.zeros((modes, LANES), F32)
        moment = jnp.zeros((modes, LANES), F32)
        for seg, (start, rows) in enumerate(segments):
            steps = rows // BLOCKS
            power = jnp.exp(-decay_ref[:, lanes] * steps)
            for b in range(BLOCKS):
                rowsb = pl.ds(b * modes, modes)
                moment = power * (moment + steps * state) + a * eb_ref[lane, seg, rowsb, :]
                state = power * state + hb_ref[lane, seg, rowsb, :]
        total_ref[pl.ds(0, modes), lanes] = state
        total_ref[pl.ds(modes, modes), lanes] = moment


def place():
    index = lax.axis_index("ctx")
    return index // 2, index % 2


def forward_pair_body(modes, tokens, total_ref, partner_ref, decay_ref, both_ref):
    _, core = place()
    state, moment = pl.ds(0, modes), pl.ds(modes, modes)
    power = jnp.exp(-decay_ref[...] * tokens)
    later = core == 1
    first_h = jnp.where(later, partner_ref[state, :], total_ref[state, :])
    first_k = jnp.where(later, partner_ref[moment, :], total_ref[moment, :])
    second_h = jnp.where(later, total_ref[state, :], partner_ref[state, :])
    second_k = jnp.where(later, total_ref[moment, :], partner_ref[moment, :])
    both_ref[state, :] = second_h + power * first_h
    both_ref[moment, :] = second_k + power * (first_k + tokens * first_h)


def respond_body(segments, modes, tokens, hb_ref, eb_ref, xperm_ref, a_ref, r_ref, decay_ref, partner_ref, *refs):
    got_refs, (resp_ref, store_ref, hin_ref, kin_ref, yloc) = refs[:-5], refs[-5:]
    half = modes // 2
    pair, core = place()
    channels = a_ref.shape[1]
    unroll = 64
    for lane in range(channels // LANES):
        lanes = pl.ds(lane * LANES, LANES)
        a = a_ref[:, lanes]
        state = jnp.where(core == 1, partner_ref[pl.ds(0, modes), lanes], 0.0)
        moment = jnp.where(core == 1, partner_ref[pl.ds(modes, modes), lanes], 0.0)
        for step, got_ref in enumerate(got_refs, 1):
            other = pair ^ step
            gap = jnp.maximum((2 * (pair - other - 1) + core) * tokens, 0).astype(F32)
            weight = jnp.where(other < pair, jnp.exp(-decay_ref[:, lanes] * gap), 0.0)
            got = got_ref[pl.ds(0, modes), lanes]
            state = state + weight * got
            moment = moment + weight * (got_ref[pl.ds(modes, modes), lanes] + gap * got)
        for seg, (start, rows) in enumerate(segments):
            steps = rows // BLOCKS
            power = jnp.exp(-decay_ref[:, lanes] * steps)
            for b in range(BLOCKS):
                rowsb = pl.ds(b * modes, modes)
                hin_ref[lane, seg, rowsb, :] = state
                kin_ref[lane, seg, rowsb, :] = moment
                moment = power * (moment + steps * state) + a * eb_ref[lane, seg, rowsb, :]
                state = power * state + hb_ref[lane, seg, rowsb, :]
        for seg, (start, rows) in enumerate(segments):
            steps = rows // BLOCKS
            for part in range(2):
                decays = [spread(a_ref, part * half + m, lanes) for m in range(half)]
                weights = [spread(r_ref, part * half + m, lanes) for m in range(half)]

                def body(outer, h):
                    h = list(h)
                    for q in range(unroll):
                        i = outer * unroll + q
                        here = pl.ds(pl.multiple_of(start + i * BLOCKS, BLOCKS), BLOCKS)
                        x = xperm_ref[lane, here, :]
                        for m in range(half):
                            h[m] = decays[m] * h[m] + x
                            store_ref[lane, part * half + m, here, :] = h[m]
                        y = tree_sum(weights[m] * h[m] for m in range(half))
                        if part == 0:
                            yloc[here, :] = y
                        else:
                            y = y + yloc[here, :]
                            resp_ref[lane, pl.ds(start + i, BLOCKS, stride=steps), :] = y
                    return tuple(h)

                begin = tuple(
                    hin_ref[lane, seg, pl.ds(part * half + m, BLOCKS, stride=modes), :]
                    for m in range(half))
                lax.fori_loop(0, steps // unroll, body, begin)


def adjoint_body(segment, modes, received, kept_ref, *refs):
    seg, start, rows = segment
    recv_refs = refs[:received]
    x1_ref, resp_ref, store_ref, hin_ref, kin_ref, a_ref = refs[received:received + 6]
    grad_ref, uperm, gb_ref, sums_ref, nat, rb, qb = refs[received + 6:]
    steps = rows // BLOCKS
    channels = x1_ref.shape[1]
    unroll = 64
    half = modes // 2
    window = pl.ds(start, rows)
    for lane in range(channels // LANES):
        lanes = pl.ds(lane * LANES, LANES)

        def own(ref):
            return ref[:, pl.ds(ref.shape[1] - channels + lane * LANES, LANES)]

        grad_in = own(kept_ref).astype(F32)
        for recv_ref in recv_refs:
            grad_in = grad_in + own(recv_ref).astype(F32)
        grad_ref[:, lanes] = (grad_in * resp_ref[lane, window, :]).astype(BF16)
        nat[lane] = (grad_in * x1_ref[window, lanes].astype(F32)).astype(BF16).astype(F32)
    for lane in range(channels // LANES):
        lanes = pl.ds(lane * LANES, LANES)
        for part in range(2):
            decays = [spread(a_ref, part * half + m, lanes) for m in range(half)]

            def body(outer, carry):
                g, racc, qacc = (list(item) for item in carry)
                for q in range(unroll):
                    i = steps - 1 - (outer * unroll + q)
                    here = pl.ds(pl.multiple_of(i * BLOCKS, BLOCKS), BLOCKS)
                    if part == 0:
                        u = nat[lane, pl.ds(i, BLOCKS, stride=steps), :]
                        uperm[lane, here, :] = u
                    else:
                        u = uperm[lane, here, :]
                    there = pl.ds(pl.multiple_of(start + i * BLOCKS, BLOCKS), BLOCKS)
                    for m in range(half):
                        h = store_ref[lane, part * half + m, there, :]
                        g[m] = decays[m] * g[m] + u
                        racc[m] = racc[m] + u * h
                        qacc[m] = qacc[m] + g[m] * h
                return tuple(g), tuple(racc), tuple(qacc)

            zero = (jnp.zeros((BLOCKS, LANES), F32),) * half
            g, racc, qacc = lax.fori_loop(0, steps // unroll, body, (zero,) * 3)
            for m in range(half):
                row = pl.ds(part * half + m, BLOCKS, stride=modes)
                gb_ref[lane, row, :] = g[m]
                rb[row, :] = racc[m]
                qb[row, :] = qacc[m]
        a = a_ref[:, lanes]
        total = jnp.zeros((modes, LANES), F32)
        moment = jnp.zeros((modes, LANES), F32)
        for b in range(BLOCKS):
            rowsb = pl.ds(b * modes, modes)
            before = hin_ref[lane, seg, rowsb, :] + kin_ref[lane, seg, rowsb, :]
            total = total + rb[rowsb, :]
            moment = moment + qb[rowsb, :] - rb[rowsb, :] + a * gb_ref[lane, rowsb, :] * before
        sums_ref[pl.ds(0, modes), lanes] = total
        sums_ref[pl.ds(modes, modes), lanes] = moment


def local_body(segments, modes, seg, uperm_ref, *refs):
    count = len(segments)
    gb_refs = refs[:count - seg]
    a_ref, r_ref, decay_ref, aloc_ref, gin = refs[count - seg:]
    channels = a_ref.shape[1]
    unroll = 32
    half = modes // 2
    for lane in range(channels // LANES):
        lanes = pl.ds(lane * LANES, LANES)
        state = jnp.zeros((modes, LANES), F32)
        for other in reversed(range(seg, count)):
            steps = segments[other][1] // BLOCKS
            power = jnp.exp(-decay_ref[:, lanes] * steps)
            for b in reversed(range(BLOCKS)):
                rowsb = pl.ds(b * modes, modes)
                if other == seg:
                    gin[rowsb, :] = state
                state = power * state + gb_refs[other - seg][lane, rowsb, :]
        for part in range(2):
            decays = [spread(a_ref, part * half + m, lanes) for m in range(half)]
            weights = [spread(r_ref, part * half + m, lanes) for m in range(half)]

            def body(outer, g):
                g = list(g)
                for q in range(unroll):
                    i = steps - 1 - (outer * unroll + q)
                    here = pl.ds(pl.multiple_of(i * BLOCKS, BLOCKS), BLOCKS)
                    u = uperm_ref[lane, here, :]
                    for m in range(half):
                        g[m] = decays[m] * g[m] + u
                    y = tree_sum(weights[m] * g[m] for m in range(half))
                    if part == 1:
                        y = y + aloc_ref[lane, here, :]
                    aloc_ref[lane, here, :] = y
                return tuple(g)

            begin = tuple(gin[pl.ds(part * half + m, BLOCKS, stride=modes), :] for m in range(half))
            lax.fori_loop(0, steps // unroll, body, begin)


def gather_body(segments, modes, *refs):
    count = len(segments)
    gb_refs, sums_refs = refs[:count], refs[count:2 * count]
    scale_ref, decay_ref, out_ref = refs[2 * count:]
    channels = decay_ref.shape[1]
    for lane in range(channels // LANES):
        lanes = pl.ds(lane * LANES, LANES)
        state = jnp.zeros((modes, LANES), F32)
        for seg in reversed(range(count)):
            power = jnp.exp(-decay_ref[:, lanes] * (segments[seg][1] // BLOCKS))
            for b in reversed(range(BLOCKS)):
                state = power * state + gb_refs[seg][lane, pl.ds(b * modes, modes), :]
        out_ref[pl.ds(0, modes), lanes] = state
    sums = sum(ref[...] for ref in sums_refs)
    out_ref[pl.ds(modes, modes), :] = sums[:modes]
    out_ref[pl.ds(2 * modes, modes), :] = sums[modes:] * scale_ref[...]


def three_parts(values):
    parts = []
    for _ in range(3):
        parts.append(values.astype(BF16))
        values = values - parts[-1].astype(F32)
    return parts


def pick(values, chosen, dims):
    return sum(
        lax.dot_general(part, chosen, dims, preferred_element_type=F32)
        for part in three_parts(values)
    )


def backward_pair_body(modes, tokens, owned, message_ref, partner_ref, decay_ref, both_ref):
    _, core = place()
    channels = decay_ref.shape[1]
    state, sums = pl.ds(0, modes), pl.ds(modes, 2 * modes)
    first = jnp.where(core == 0, message_ref[state, :], partner_ref[state, :])
    second = jnp.where(core == 0, partner_ref[state, :], message_ref[state, :])
    both_ref[state, :] = first + jnp.exp(-decay_ref[...] * tokens) * second
    channel = lax.broadcasted_iota(jnp.int32, (channels, LANES), 0)
    lane = lax.broadcasted_iota(jnp.int32, (channels, LANES), 1)
    wanted = (2 * (lane // owned) + core) * owned + lane % owned
    picked = pick(message_ref[sums, :] + partner_ref[sums, :], (channel == wanted).astype(BF16),
                  (((1,), (0,)), ((), ())))
    tiles = channels // LANES
    rows = 2 * modes // tiles
    for tile in range(tiles):
        both_ref[pl.ds(modes, rows), pl.ds(tile * LANES, LANES)] = picked[tile * rows:(tile + 1) * rows]


def finish_body(segments, modes, tokens, length, pairs, *refs):
    count = len(segments)
    aloc_refs, grad_refs = refs[:count], refs[count:2 * count]
    refs = refs[count:]
    a_ref, r_ref, decay_ref, x2_ref, v_ref, partner_ref, both_ref = refs[count:count + 7]
    got_refs = refs[count + 7:count + 6 + pairs]
    gx1_ref, gx2_ref, gv_ref, rgrad_ref, dgrad_ref, gin, nat, gx2_here, gv_here, r_here, d_here, sems = refs[-12:]
    channels = a_ref.shape[1]
    unroll = 16
    pair, core = place()
    states = []
    for lane in range(channels // LANES):
        lanes = pl.ds(lane * LANES, LANES)
        state = jnp.where(core == 0, partner_ref[pl.ds(0, modes), lanes], 0.0)
        for step, got_ref in enumerate(got_refs, 1):
            other = pair ^ step
            gap = jnp.maximum((2 * (other - pair - 1) + 1 - core) * tokens, 0).astype(F32)
            weight = jnp.where(other > pair, jnp.exp(-decay_ref[:, lanes] * gap), 0.0)
            state = state + weight * got_ref[pl.ds(0, modes), lanes]
        states.append(state)
    copies = []
    for seg, grad_ref in enumerate(grad_refs):
        copies.append(pltpu.make_async_copy(grad_ref, gx1_ref.at[pl.ds(*segments[seg]), :], sems.at[seg, 2]))
        copies[-1].start()
    owned = rgrad_ref.shape[1]
    tiles = channels // LANES
    lower = pl.ds(modes, 2 * modes // tiles)
    sums = both_ref[lower, :]
    for got_ref in got_refs:
        sums = sums + got_ref[lower, :]
    row = lax.broadcasted_iota(jnp.int32, (owned, LANES), 0)
    column = lax.broadcasted_iota(jnp.int32, (owned, LANES), 1)
    chosen = (column == pair * owned + row).astype(BF16)

    def choose(values):
        return sum(
            lax.dot_general(part, chosen, CONTRACT_LAST, preferred_element_type=F32)
            for part in three_parts(values)
        )

    if tiles == 1:
        residue_sums, decay_sums = sums[:modes], sums[modes:]
    else:
        residue_sums, decay_sums = sums[:, :LANES], sums[:, LANES:]
    r_here[...] = choose(residue_sums) / length
    d_here[...] = choose(decay_sums) / length
    for j, (here, there) in enumerate(((r_here, rgrad_ref), (d_here, dgrad_ref))):
        copy = pltpu.make_async_copy(here, there, sems.at[count, j])
        copy.start()
        copies.append(copy)
    for seg in reversed(range(count)):
        start, rows = segments[seg]
        steps = rows // BLOCKS
        window = pl.ds(start, rows)
        for lane in range(channels // LANES):
            lanes = pl.ds(lane * LANES, LANES)
            decays = [spread(a_ref, m, lanes) for m in range(modes)]
            state = states[lane]
            power = jnp.exp(-decay_ref[:, lanes] * steps)
            for b in reversed(range(BLOCKS)):
                rowsb = pl.ds(b * modes, modes)
                gin[rowsb, :] = state
                state = power * state
            states[lane] = state
            edge = tuple(
                spread(r_ref, m, lanes) * decays[m] * gin[pl.ds(m, BLOCKS, stride=modes), :]
                for m in range(modes)
            )

            def body(outer, edge):
                edge = list(edge)
                for q in range(unroll):
                    i = steps - 1 - (outer * unroll + q)
                    here = pl.ds(pl.multiple_of(i * BLOCKS, BLOCKS), BLOCKS)
                    y = tree_sum(edge) + aloc_refs[seg][lane, here, :]
                    for m in range(modes):
                        edge[m] = edge[m] * decays[m]
                    nat[lane, pl.ds(start + i, BLOCKS, stride=steps), :] = y
                return tuple(edge)

            lax.fori_loop(0, steps // unroll, body, edge)
            adjoint = nat[lane, window, :]
            gx2_here[window, lanes] = (adjoint * v_ref[window, lanes].astype(F32)).astype(BF16)
            gv_here[window, lanes] = (adjoint * x2_ref[window, lanes].astype(F32)).astype(BF16)
        for j, (here, there) in enumerate(((gx2_here, gx2_ref), (gv_here, gv_ref))):
            copy = pltpu.make_async_copy(here.at[window, :], there.at[window, :], sems.at[seg, j])
            copy.start()
            copies.append(copy)
    for copy in copies:
        copy.wait()


def on_device(g_out, w_out, gate_x1, gate_x2, value_v, residue, decay):
    tokens, channels = gate_x1.shape
    context_size = lax.axis_size("ctx")
    ch_size = lax.axis_size("ch")
    length = tokens * context_size
    modes = residue.shape[1]
    lane_tiles = channels // LANES
    owned = channels // context_size

    bits = [1 << bit for bit in range(ch_size.bit_length() - 1)]
    half_rows = tokens // 2
    chunks = [(0, half_rows, bits), (half_rows, half_rows, bits[::-1])]
    segments = [(start, rows) for start, rows, _ in chunks]
    count = len(chunks)
    layouts = [halving_layout(order) for _, _, order in chunks]
    cut = ch_size // 2

    rows_of = [(start, rows) for start, rows, _ in chunks]
    projected = project(
        g_out, w_out, [(*where, layout[:cut]) for where, layout in zip(rows_of, layouts)], channels)
    sent = [lax.ppermute(piece, "ch", xor_pairs(ch_size, order[0]))
            for piece, (_, _, order) in zip(projected, chunks)]
    kept = project_kept(
        g_out, w_out, [(*where, layout[cut:]) for where, layout in zip(rows_of, layouts)], channels)

    decay_t = decay.T
    residue_t = residue.T
    a = jnp.exp(-decay_t)
    r = residue_t * length ** (-0.5)
    scale = -residue_t * decay_t

    state_shape = jax.ShapeDtypeStruct((lane_tiles, count, BLOCKS * modes, LANES), F32)
    perm_shape = jax.ShapeDtypeStruct((lane_tiles, tokens, LANES), F32)
    work = tokens * channels * modes
    xperm, hb, eb, total = pl.pallas_call(
        functools.partial(forward_body, segments, modes),
        out_shape=[perm_shape, state_shape, state_shape,
                   jax.ShapeDtypeStruct((2 * modes, channels), F32)],
        scratch_shapes=[pltpu.VMEM((lane_tiles, tokens, LANES), F32)],
        compiler_params=params(),
        cost_estimate=cost(3.7),
        name="forward",
    )(gate_x2, value_v, a, decay_t)

    pairs = context_size // 2
    partner = lax.ppermute(total, "ctx", xor_pairs(context_size, 1))
    both = pl.pallas_call(
        functools.partial(forward_pair_body, modes, tokens),
        out_shape=jax.ShapeDtypeStruct((2 * modes, channels), F32),
        compiler_params=params(),
        name="forward_pair",
    )(total, partner, decay_t)
    got = [lax.ppermute(both, "ctx", xor_pairs(context_size, 2 * step)) for step in range(1, pairs)]

    uperms, gbs, sums = [], [], []
    arrived = [[piece] for piece in sent]
    away = both
    for level in range(1, len(bits)):
        for which in reversed(range(count)):
            order = chunks[which][2]
            arrived[which][-1], _ = lax.optimization_barrier((arrived[which][-1], away))
            stop = cut >> level
            width = kept[which].shape[1]
            left = width - 2 * stop * channels
            away = kept[which][:, left:left + stop * channels].astype(F32)
            for piece in arrived[which]:
                left = piece.shape[1] - 2 * stop * channels
                away = away + piece[:, left:left + stop * channels].astype(F32)
            away = away.astype(BF16)
            hb, away = lax.optimization_barrier((hb, away))
            arrived[which].append(lax.ppermute(away, "ch", xor_pairs(ch_size, order[level])))
    store_shape = jax.ShapeDtypeStruct((lane_tiles, modes, tokens, LANES), F32)
    resp, store, hin, kin = pl.pallas_call(
        functools.partial(respond_body, segments, modes, tokens),
        out_shape=[perm_shape, store_shape, state_shape, state_shape],
        scratch_shapes=[pltpu.VMEM((tokens, LANES), F32)],
        compiler_params=params(),
        cost_estimate=cost(3.5),
        name="respond",
    )(hb, eb, xperm, a, r, decay_t, partner, *got)

    grads = []
    for seg in reversed(range(count)):
        start, rows = segments[seg]
        block_shape = jax.ShapeDtypeStruct((lane_tiles, BLOCKS * modes, LANES), F32)
        pieces = arrived[seg]
        grad, uperm, gb, partial_sums = pl.pallas_call(
            functools.partial(adjoint_body, (seg, start, rows), modes, len(pieces)),
            in_specs=in_vmem(7 + len(pieces)),
            out_specs=in_vmem(4),
            out_shape=[
                       jax.ShapeDtypeStruct((rows, channels), BF16),
                       jax.ShapeDtypeStruct((lane_tiles, rows, LANES), F32),
                       block_shape,
                       jax.ShapeDtypeStruct((2 * modes, channels), F32)],
            scratch_shapes=[pltpu.VMEM((lane_tiles, rows, LANES), F32)]
            + [pltpu.VMEM((BLOCKS * modes, LANES), F32)] * 2,
            compiler_params=params(),
            cost_estimate=cost(2.7 * rows / 512),
            name="adjoint",
        )(kept[seg], *pieces, gate_x1, resp, store, hin, kin, a)
        grads.append(grad)
        uperms.append(uperm)
        gbs.append(gb)
        sums.append(partial_sums)

    uperms, gbs, sums, grads = uperms[::-1], gbs[::-1], sums[::-1], grads[::-1]
    message = pl.pallas_call(
        functools.partial(gather_body, segments, modes),
        out_shape=jax.ShapeDtypeStruct((3 * modes, channels), F32),
        compiler_params=params(),
        name="totals",
    )(*gbs, *sums, scale, decay_t)
    partner = lax.ppermute(message, "ctx", xor_pairs(context_size, 1))
    both = pl.pallas_call(
        functools.partial(backward_pair_body, modes, tokens, owned),
        out_shape=jax.ShapeDtypeStruct((modes + 2 * modes // lane_tiles, channels), F32),
        compiler_params=params(),
        name="backward_pair",
    )(message, partner, decay_t)
    got = [lax.ppermute(both, "ctx", xor_pairs(context_size, 2 * step)) for step in range(1, pairs)]
    *uperms, _ = lax.optimization_barrier((*uperms, both))
    alocs = [
        pl.pallas_call(
            functools.partial(local_body, segments, modes, seg),
            out_shape=jax.ShapeDtypeStruct((lane_tiles, rows, LANES), F32),
            scratch_shapes=[pltpu.VMEM((BLOCKS * modes, LANES), F32)],
            compiler_params=params(),
            cost_estimate=cost(1.8 * rows / 512),
            name="local_adjoint",
        )(uperms[seg], *gbs[seg:], a, r, decay_t)
        for seg, (_, rows) in enumerate(segments)
    ]

    grad_x1, grad_x2, grad_v, residue_grad, decay_grad = pl.pallas_call(
        functools.partial(finish_body, segments, modes, tokens, length, pairs),
        in_specs=in_vmem(2 * count + 6 + pairs),
        out_specs=[pl.BlockSpec(memory_space=HBM)] * 5,
        out_shape=[jax.ShapeDtypeStruct((tokens, channels), BF16)] * 3
        + [jax.ShapeDtypeStruct((modes, owned), F32)] * 2,
        scratch_shapes=[pltpu.VMEM((BLOCKS * modes, LANES), F32),
                        pltpu.VMEM((lane_tiles, tokens, LANES), F32),
                        pltpu.VMEM((tokens, channels), BF16),
                        pltpu.VMEM((tokens, channels), BF16),
                        pltpu.VMEM((modes, owned), F32),
                        pltpu.VMEM((modes, owned), F32),
                        pltpu.SemaphoreType.DMA((count + 1, 3))],
        compiler_params=params(),
        cost_estimate=cost(3.4),
        name="finish",
    )(*alocs, *grads, a, r, decay_t, gate_x2, value_v, partner, both, *got)
    return grad_x1, grad_x2, grad_v, residue_grad.T, decay_grad.T


def solution(mesh):
    return jax.shard_map(
        on_device,
        mesh=mesh,
        in_specs=(
            P("ctx", "ch"),
            P(None, "ch"),
            P("ctx", "ch"),
            P("ctx", "ch"),
            P("ctx", "ch"),
            P("ch", None),
            P("ch", None),
        ),
        out_specs=(
            P("ctx", "ch"),
            P("ctx", "ch"),
            P("ctx", "ch"),
            P(("ch", "ctx"), None),
            P(("ch", "ctx"), None),
        ),
        check_vma=False,
    )
```
